32 devices in a mesh: dp: 4 (over y, x), fsdp: 8 (over z, core).
Axes of the slice: x: 2, y: 2, z: 4, core: 2. Of those that a mesh axis runs over, the one named last changes fastest.
Arguments:
- enc_in: bfloat16 [64, 512, 512], P(('dp', 'fsdp')), may hold values from -6 to 6
- dec_in: bfloat16 [64, 512, 512], P(('dp', 'fsdp')), may hold values from -6 to 6
- bucket: int32 [64], P(('dp', 'fsdp')), may hold values from 0 to 2, as said below
- enc_lengths: int32 [64, 4], P(('dp', 'fsdp')), may hold values from 0 to 512, as said below
- dec_lengths: int32 [64, 4], P(('dp', 'fsdp')), may hold values from 0 to 512, as said below
- pred_ids: int32 [64, 512], P(('dp', 'fsdp')), may hold values from 0 to 522
- running_counts: int32 [523], replicated, may hold values from 0 to 15
- enc_attn_in: bfloat16 [786432], P(('dp', 'fsdp')), may hold values from -0.25 to 0.25
- enc_attn_out: bfloat16 [262144], P(('dp', 'fsdp')), may hold values from -1 to 1
- enc_ff_in: bfloat16 [1048576], P(('dp', 'fsdp')), may hold values from -0.25 to 0.25
- enc_ff_out: bfloat16 [1048576], P(('dp', 'fsdp')), may hold values from -0.125 to 0.125
- enc_norms: bfloat16 [2048], P(('dp', 'fsdp')), may hold values from -1.2 to 1.8
- dec_self_in: bfloat16 [786432], P(('dp', 'fsdp')), may hold values from -0.25 to 0.25
- dec_self_out: bfloat16 [262144], P(('dp', 'fsdp')), may hold values from -1 to 1
- dec_cross_q: bfloat16 [262144], P(('dp', 'fsdp')), may hold values from -0.25 to 0.25
- dec_cross_kv: bfloat16 [524288], P(('dp', 'fsdp')), may hold values from -0.25 to 0.25
- dec_cross_out: bfloat16 [262144], P(('dp', 'fsdp')), may hold values from -1 to 1
- dec_ff_in: bfloat16 [1048576], P(('dp', 'fsdp')), may hold values from -0.25 to 0.25
- dec_ff_out: bfloat16 [1048576], P(('dp', 'fsdp')), may hold values from -0.125 to 0.125
- dec_norms: bfloat16 [3072], P(('dp', 'fsdp')), may hold values from -1.2 to 1.8
- enc_cotangent: bfloat16 [64, 512, 512], P(('dp', 'fsdp')), may hold values from -6 to 6
- dec_cotangent: bfloat16 [64, 512, 512], P(('dp', 'fsdp')), may hold values from -6 to 6
Outputs:
- enc_out: bfloat16 [64, 512, 512], P(('dp', 'fsdp'))
- dec_out: bfloat16 [64, 512, 512], P(('dp', 'fsdp'))
- enc_in_grad: bfloat16 [64, 512, 512], P(('dp', 'fsdp'))
- dec_in_grad: bfloat16 [64, 512, 512], P(('dp', 'fsdp'))
- enc_attn_in_grad: float32 [786432], P(('dp', 'fsdp'))
- enc_attn_out_grad: float32 [262144], P(('dp', 'fsdp'))
- enc_ff_in_grad: float32 [1048576], P(('dp', 'fsdp'))
- enc_ff_out_grad: float32 [1048576], P(('dp', 'fsdp'))
- enc_norms_grad: float32 [2048], P(('dp', 'fsdp'))
- dec_self_in_grad: float32 [786432], P(('dp', 'fsdp'))
- dec_self_out_grad: float32 [262144], P(('dp', 'fsdp'))
- dec_cross_q_grad: float32 [262144], P(('dp', 'fsdp'))
- dec_cross_kv_grad: float32 [524288], P(('dp', 'fsdp'))
- dec_cross_out_grad: float32 [262144], P(('dp', 'fsdp'))
- dec_ff_in_grad: float32 [1048576], P(('dp', 'fsdp'))
- dec_ff_out_grad: float32 [1048576], P(('dp', 'fsdp'))
- dec_norms_grad: float32 [3072], P(('dp', 'fsdp'))
- counts: int32 [523], replicated
The draws below stay inside these ranges and needn't reach their ends.
Inputs may be any that keep to these rules, and one draw needn't show every extreme that they name: `bucket`: a slot of kind b holds 4 / 2**b sequences, each of up to 512 / 4 * 2**b positions; source and target of a pair share the slot and its sequence number; some slot is of kind 2. `enc_lengths`: for a slot of kind b, entries 0 to 4 / 2**b - 1 are its sequences' lengths, from a quarter of 512 / 4 * 2**b to all of it; the other entries are 0; some slot of kind 2 holds a sequence of all 512 positions. `dec_lengths`: as enc_lengths, for the targets.
All inputs are finite; a program needn't handle non-finite values.
Results may differ from the reference program's by a relative error of at most 0.025.
Values may be sent and summed in bfloat16 or wider, within the bound.
No kernel may reach another device: no remote copies, remote signals or barrier semaphores. Data moves between devices by JAX's collectives and lax.ppermute only.
A program may use at most 192 MiB of HBM per device.

```python
import math
from functools import partial
import jax
import jax.numpy as jnp
import numpy as np
from jax import lax

D = 512
HEAD = 64
FF = 2048
VOCAB = 523
SLOT = 512
SLOTS = 64


def chosen_slot(key):
    return jax.random.randint(jax.random.fold_in(key, 5), (), 0, SLOTS).astype(jnp.int32)


def slot_kinds(key):
    kinds = jax.random.randint(key, (SLOTS,), 0, 3).astype(jnp.int32)
    picked = jnp.arange(SLOTS, dtype=jnp.int32) == chosen_slot(key)
    return jnp.where(picked, jnp.int32(2), kinds).astype(jnp.int32)


def slot_lengths(key, constant):
    slot_kind = slot_kinds(key)
    slot_number = jnp.arange(SLOTS, dtype=jnp.int32)
    picked = slot_number == chosen_slot(key)
    key = jax.random.fold_in(key, constant)
    bucket_size = jnp.left_shift(jnp.int32(SLOT // 4), slot_kind)
    shortest = bucket_size // 4
    upper = shortest + (bucket_size - shortest) * slot_number // max(SLOTS - 1, 1)
    random_bits = jax.random.randint(key, (SLOTS, 4), 0, 1 << 20)
    lengths = upper[:, None] - random_bits % (bucket_size // 8 + 1)[:, None]
    lengths = jnp.maximum(lengths, shortest[:, None])
    sequence_count = jnp.right_shift(jnp.int32(4), slot_kind)
    is_live = jnp.arange(4, dtype=jnp.int32)[None, :] < sequence_count[:, None]
    lengths = jnp.where(is_live, lengths, 0)
    first_entry = picked[:, None] & (jnp.arange(4, dtype=jnp.int32)[None, :] == 0)
    return jnp.where(first_entry, jnp.int32(SLOT), lengths).astype(jnp.int32)


def norm_rows(key, branches):
    noise = jnp.clip(jax.random.normal(key, (branches, 2, D), jnp.float32), -4.0, 4.0)
    factors = jnp.array([0.2, 0.3], jnp.float32)
    centers = jnp.array([1.0, 0.0], jnp.float32)
    return (centers[None, :, None] + factors[None, :, None] * noise).reshape(-1)


def draw_bucket(key, part):
    slot_kind = slot_kinds(key)
    return slot_kind


def draw_enc_lengths(key, part):
    return slot_lengths(key, 11)


def draw_dec_lengths(key, part):
    return slot_lengths(key, 12)


def draw_enc_norms(key, part):
    key = jax.random.fold_in(key, 21)
    return norm_rows(key, 2).astype(jnp.bfloat16)


def draw_dec_norms(key, part):
    key = jax.random.fold_in(key, 22)
    return norm_rows(key, 3).astype(jnp.bfloat16)


def place_ends(drawn, key, low, high):
    index_at = [jax.random.randint(jax.random.fold_in(key, axis), (), 0, length) for axis, length in enumerate(drawn.shape)]
    main_axis = drawn.shape.index(max(drawn.shape))
    next_to = index_at[:main_axis] + [(index_at[main_axis] + 1) % drawn.shape[main_axis]] + index_at[main_axis + 1:]
    return drawn.at[tuple(index_at)].set(low).at[tuple(next_to)].set(high)


def shard_levels(key, dims, shards, low, high):
    loudness, own = 1.0, jax.random.fold_in(key, 6)
    for position, parts in shards:
        steps = jnp.exp(jax.random.uniform(jax.random.fold_in(own, position), (parts,), jnp.float32, low / len(shards), high / len(shards)))
        loudness = loudness * jnp.repeat(steps, dims[position] // parts).reshape([-1 if axis == position else 1 for axis in range(len(dims))])
    return loudness


def rank_table(count, slope):
    weights = [(1 << 20) // math.isqrt(standing ** slope) + 1 for standing in range(1, count + 1)]
    width = 1 + sum(weights) // (1 << 30)
    return np.cumsum(np.array([max(1, weight // width) for weight in weights]))


def ranked(own_key, extent, amount, skew):
    table = rank_table(amount, skew)
    pick = jax.random.randint(jax.random.fold_in(own_key, 1), extent, 0, int(table[amount - 1]))
    grade = jnp.searchsorted(jnp.asarray(table, jnp.int32), pick, side="right")
    return jax.random.permutation(jax.random.fold_in(own_key, 2), amount)[grade].astype(jnp.int32)


def bell_draw(rng, shape, deviation, limit, cuts=(), kind=jnp.bfloat16):
    entries = deviation * jax.random.normal(rng, shape, jnp.float32)
    if cuts:
        entries = entries * shard_levels(rng, shape, cuts, -0.22, 0.18)
    return jnp.clip(entries, -limit, limit).astype(kind)


def setup_inputs(seed: int = 0) -> dict:
    streams_of = jax.random.split(jax.random.key(seed), 23)
    enc_in = bell_draw(streams_of[0], (SLOTS, SLOT, D), 1.0, 6.0, ((0, 32),))
    dec_in = bell_draw(streams_of[1], (SLOTS, SLOT, D), 1.0, 6.0, ((0, 32),))
    bucket = draw_bucket(jax.random.fold_in(streams_of[22], 71), 0)
    enc_lengths = draw_enc_lengths(jax.random.fold_in(streams_of[22], 71), 0)
    dec_lengths = draw_dec_lengths(jax.random.fold_in(streams_of[22], 71), 0)
    pred_ids = place_ends(ranked(streams_of[5], (SLOTS, SLOT), VOCAB, 2), jax.random.fold_in(streams_of[5], 3), 0, VOCAB - 1).astype(jnp.int32)
    running_counts = place_ends(jax.random.randint(streams_of[6], (VOCAB,), 0, 16), jax.random.fold_in(streams_of[6], 1), 0, 15).astype(jnp.int32)
    enc_attn_in = bell_draw(streams_of[7], (D * 3 * D,), D ** -0.5, 0.25, ((0, 32),))
    enc_attn_out = bell_draw(streams_of[8], (D * D,), (D // 16) ** -0.5, 1.0, ((0, 32),))
    enc_ff_in = bell_draw(streams_of[9], (D * FF,), D ** -0.5, 0.25, ((0, 32),))
    enc_ff_out = bell_draw(streams_of[10], (FF * D,), FF ** -0.5, 0.125, ((0, 32),))
    enc_norms = draw_enc_norms(jax.random.fold_in(streams_of[22], 71), 0)
    dec_self_in = bell_draw(streams_of[12], (D * 3 * D,), D ** -0.5, 0.25, ((0, 32),))
    dec_self_out = bell_draw(streams_of[13], (D * D,), (D // 16) ** -0.5, 1.0, ((0, 32),))
    dec_cross_q = bell_draw(streams_of[14], (D * D,), D ** -0.5, 0.25, ((0, 32),))
    dec_cross_kv = bell_draw(streams_of[15], (D * 2 * D,), D ** -0.5, 0.25, ((0, 32),))
    dec_cross_out = bell_draw(streams_of[16], (D * D,), (D // 16) ** -0.5, 1.0, ((0, 32),))
    dec_ff_in = bell_draw(streams_of[17], (D * FF,), D ** -0.5, 0.25, ((0, 32),))
    dec_ff_out = bell_draw(streams_of[18], (FF * D,), FF ** -0.5, 0.125, ((0, 32),))
    dec_norms = draw_dec_norms(jax.random.fold_in(streams_of[22], 71), 0)
    enc_cotangent = bell_draw(streams_of[20], (SLOTS, SLOT, D), 1.0, 6.0, ((0, 32),))
    dec_cotangent = bell_draw(streams_of[21], (SLOTS, SLOT, D), 1.0, 6.0, ((0, 32),))
    return {"enc_in": enc_in, "dec_in": dec_in, "bucket": bucket, "enc_lengths": enc_lengths, "dec_lengths": dec_lengths, "pred_ids": pred_ids, "running_counts": running_counts, "enc_attn_in": enc_attn_in, "enc_attn_out": enc_attn_out, "enc_ff_in": enc_ff_in, "enc_ff_out": enc_ff_out, "enc_norms": enc_norms, "dec_self_in": dec_self_in, "dec_self_out": dec_self_out, "dec_cross_q": dec_cross_q, "dec_cross_kv": dec_cross_kv, "dec_cross_out": dec_cross_out, "dec_ff_in": dec_ff_in, "dec_ff_out": dec_ff_out, "dec_norms": dec_norms, "enc_cotangent": enc_cotangent, "dec_cotangent": dec_cotangent}


@jax.custom_vjp
def low(v):
    return lax.optimization_barrier(v.astype(jnp.bfloat16)).astype(jnp.float32)

@jax.custom_vjp
def low_back(v):
    return v

def low_keep(v):
    return (low(v), None)

def low_pass(kept, grad):
    return (grad,)

def back_keep(v):
    return (v, None)

def back_low(kept, grad):
    return (low(grad),)
low.defvjp(low_keep, low_pass)
low_back.defvjp(back_keep, back_low)
epsilon = 1e-05
precise = lax.Precision.HIGHEST

def product(left, right):
    return jnp.dot(left, right, precision=precise)

def layer_norm(values, norm_gain, norm_shift):
    row_mean = lax.optimization_barrier(jnp.mean(values, -1, keepdims=True))
    centered = values - row_mean
    variance = lax.optimization_barrier(jnp.mean(centered * centered, -1, keepdims=True))
    return centered * lax.rsqrt(variance + epsilon) * norm_gain + norm_shift

def slot_layout(bucket_kind, lengths):
    positions = jnp.arange(SLOT, dtype=jnp.int32)
    bucket_size = jnp.left_shift(jnp.int32(SLOT // 4), bucket_kind)
    segment = positions // bucket_size
    picker = segment[:, None] == jnp.arange(4, dtype=jnp.int32)[None, :]
    own_length = lax.optimization_barrier(jnp.sum(jnp.where(picker, lengths[None, :], 0), 1, dtype=jnp.int32))
    is_live = positions % bucket_size < own_length
    return (segment, is_live)

def pair_mask(bucket_kind, query_lengths, key_lengths, causal):
    query_segment, query_live = slot_layout(bucket_kind, query_lengths)
    key_segment, key_live = slot_layout(bucket_kind, key_lengths)
    allowed = (query_segment[:, None] == key_segment[None, :]) & key_live[None, :]
    if causal:
        positions = jnp.arange(SLOT, dtype=jnp.int32)
        allowed = allowed & (positions[None, :] <= positions[:, None])
    return allowed

def attend(queries, keys_in, values_in, allowed):
    head_count = D // HEAD
    query_heads = queries.reshape(SLOT, head_count, HEAD)
    key_heads = keys_in.reshape(SLOT, head_count, HEAD)
    value_heads = values_in.reshape(SLOT, head_count, HEAD)
    scores = low_back(HEAD ** (-0.5) * jnp.einsum('qhd,khd->hqk', query_heads, key_heads, precision=precise))
    scores = jnp.where(allowed[None], scores, -1000000000.0)
    largest = lax.optimization_barrier(jnp.max(scores, -1, keepdims=True))
    powers = jnp.exp(scores - largest)
    weights = low(powers / lax.optimization_barrier(jnp.sum(powers, -1, keepdims=True)))
    context = jnp.einsum('hqk,khd->qhd', weights, value_heads, precision=precise)
    return context.reshape(SLOT, D)

def self_branch(residual, w_in, w_out, norm_gain, norm_shift, bucket_kind, lengths, causal):
    normed = low(layer_norm(residual, norm_gain, norm_shift))
    projected = low(low_back(product(normed, w_in)))
    allowed = pair_mask(bucket_kind, lengths, lengths, causal)
    context = low(low_back(attend(projected[:, :D], projected[:, D:2 * D], projected[:, 2 * D:], allowed)))
    return residual + low_back(product(context, w_out))

def cross_branch(residual, memory, w_query, w_pair, w_out, norm_gain, norm_shift, bucket_kind, dec_len, enc_len):
    normed = low(layer_norm(residual, norm_gain, norm_shift))
    queries = low(low_back(product(normed, w_query)))
    pairs = low(low_back(product(memory, w_pair)))
    allowed = pair_mask(bucket_kind, dec_len, enc_len, False)
    context = low(low_back(attend(queries, pairs[:, :D], pairs[:, D:], allowed)))
    return residual + low_back(product(context, w_out))

def ffn_branch(residual, ff_in, ff_out, norm_gain, norm_shift):
    normed = low(layer_norm(residual, norm_gain, norm_shift))
    hidden_pre = low_back(product(normed, ff_in))
    active = low(jax.nn.gelu(hidden_pre, approximate=False))
    return residual + low_back(product(active, ff_out))

def slot_forward(parameters, pieces):
    enc_rows, dec_rows, bucket_kind, enc_len, dec_len = pieces
    enc_norm = parameters[4]
    dec_norm = parameters[12]
    encoded = self_branch(enc_rows, parameters[0], parameters[1], enc_norm[0], enc_norm[1], bucket_kind, enc_len, False)
    encoded = ffn_branch(encoded, parameters[2], parameters[3], enc_norm[2], enc_norm[3])
    memory = low(encoded)
    decoded = self_branch(dec_rows, parameters[5], parameters[6], dec_norm[0], dec_norm[1], bucket_kind, dec_len, True)
    decoded = cross_branch(decoded, memory, parameters[7], parameters[8], parameters[9], dec_norm[2], dec_norm[3], bucket_kind, dec_len, enc_len)
    decoded = ffn_branch(decoded, parameters[10], parameters[11], dec_norm[4], dec_norm[5])
    return (memory, decoded)

def reference(enc_in, dec_in, bucket, enc_lengths, dec_lengths, pred_ids, running_counts, enc_attn_in, enc_attn_out, enc_ff_in, enc_ff_out, enc_norms, dec_self_in, dec_self_out, dec_cross_q, dec_cross_kv, dec_cross_out, dec_ff_in, dec_ff_out, dec_norms, enc_cotangent, dec_cotangent):
    flat_weights = (enc_attn_in, enc_attn_out, enc_ff_in, enc_ff_out, enc_norms, dec_self_in, dec_self_out, dec_cross_q, dec_cross_kv, dec_cross_out, dec_ff_in, dec_ff_out, dec_norms)
    weight_shapes = ((D, 3 * D), (D, D), (D, FF), (FF, D), (4, D), (D, 3 * D), (D, D), (D, D), (D, 2 * D), (D, D), (D, FF), (FF, D), (6, D))
    parameters = tuple((weight_flat.astype(jnp.float32).reshape(weight_shape) for weight_flat, weight_shape in zip(flat_weights, weight_shapes)))

    def whole(enc_rows, dec_rows, weight_set):
        slot_step = jax.checkpoint(partial(slot_forward, weight_set))
        return lax.map(slot_step, (enc_rows, dec_rows, bucket, enc_lengths, dec_lengths))
    outputs, pullback = jax.vjp(whole, enc_in.astype(jnp.float32), dec_in.astype(jnp.float32), parameters)
    memory, decoded = outputs
    grad_enc, grad_dec, grad_weights = pullback((enc_cotangent.astype(jnp.float32), dec_cotangent.astype(jnp.float32)))
    flat_grads = tuple((weight_grad.reshape(-1) for weight_grad in grad_weights))

    def count_slot(pieces):
        slot_ids, bucket_kind, lengths = pieces
        segment, is_live = slot_layout(bucket_kind, lengths)
        hits = (slot_ids[:, None] == jnp.arange(VOCAB, dtype=jnp.int32)[None, :]) & is_live[:, None]
        return lax.optimization_barrier(jnp.sum(hits.astype(jnp.int32), 0, dtype=jnp.int32))
    slot_counts = lax.map(count_slot, (pred_ids, bucket, dec_lengths))
    counts = running_counts + lax.optimization_barrier(jnp.sum(slot_counts, 0, dtype=jnp.int32))
    return (memory.astype(jnp.bfloat16), decoded.astype(jnp.bfloat16), grad_enc.astype(jnp.bfloat16), grad_dec.astype(jnp.bfloat16), flat_grads[0], flat_grads[1], flat_grads[2], flat_grads[3], flat_grads[4], flat_grads[5], flat_grads[6], flat_grads[7], flat_grads[8], flat_grads[9], flat_grads[10], flat_grads[11], flat_grads[12], counts)
```

```python
import functools
import math
import jax
import jax.numpy as jnp
from jax import lax
from jax.experimental import pallas as pl
from jax.experimental.pallas import tpu as pltpu
from jax.sharding import PartitionSpec as P

D = 512
HEAD = 64
FF = 2048
VOCAB = 523
SLOT = 512
SHARDS = 32
BLOCKS = FF // D
EPS = 1e-05
PAIR = 2 * HEAD
PAIRS = D // PAIR
GROUP = 16
MASKED = -(2.0**30)
BF = jnp.bfloat16
F32 = jnp.float32
VMEM_LIMIT = 56 << 20

SELF_ROWS, SELF_IN, SELF_OUT = 64, 0, 48
FFN_ROWS, FFN_IN, FFN_OUT = 128, 0, 64
CROSS_ROWS, CROSS_Q, CROSS_KV, CROSS_OUT = 64, 0, 16, 48


def nn(left, right):
    return lax.dot_general(left, right, (((1,), (0,)), ((), ())), preferred_element_type=F32)


def nt(left, right):
    return lax.dot_general(left, right, (((1,), (1,)), ((), ())), preferred_element_type=F32)


def wide(ref, start, block):
    first = start + 16 * block
    return ref[:, :, first : first + 16, :].reshape(D, D)


def tall(ref, start, block):
    return ref[4 * block : 4 * block + 4, :, start : start + 64, :].reshape(D, D)


def put_wide(core, keep_ref, send_ref, start, block, value):
    rows = slice(start + 16 * block, start + 16 * block + 16)
    shards = value.reshape(SHARDS // 2, 2, 16, D)
    keep_ref[:, rows, :] = jnp.where(core == 0, shards[:, 0], shards[:, 1]).astype(BF)
    send_ref[:, rows, :] = jnp.where(core == 0, shards[:, 1], shards[:, 0]).astype(BF)


def put_tall(core, keep_ref, send_ref, start, block, value):
    rows = slice(start, start + 64)
    lead = slice(4 * block, 4 * block + 4)
    shards = value.reshape(4, 2, 64, D)
    keep_ref[lead, rows, :] = jnp.where(core == 0, shards[:, 0], shards[:, 1]).astype(BF)
    send_ref[lead, rows, :] = jnp.where(core == 0, shards[:, 1], shards[:, 0]).astype(BF)


class Weights:
    def __init__(self, own, other, places, half):
        self.arrays = (own[0], other[0], own[1], other[1])
        self.places = places
        self.half = half


def weight_copies(pieces, places, half, core, ref, sems, low, high):
    copies = []
    for number, place in enumerate(places):
        first, last = max(low, number * half), min(high, (number + 1) * half)
        if first < last:
            source = slice(place + first - number * half, place + last - number * half)
            for other in range(2):
                copies.append(
                    pltpu.make_async_copy(
                        pieces[2 * number + other].at[:, source, :],
                        ref.at[:, core if other == 0 else 1 - core, first - low : last - low, :],
                        sems.at[2 * number + other],
                    )
                )
    return copies


def on_first_slot(action, copies):
    @pl.when(pl.program_id(0) == 0)
    def _():
        for copy in copies:
            getattr(copy, action)()


def norm_grad_rows(ref, gains_and_shifts):
    rows = jnp.concatenate(gains_and_shifts + [jnp.zeros((8 - len(gains_and_shifts), D), F32)], 0)
    add_up(ref, rows)


def last_slot():
    return pl.program_id(0) == pl.num_programs(0) - 1


def lanes_of(pair):
    return slice(pair * PAIR, (pair + 1) * PAIR)


def normalize(values):
    centered = values - jnp.mean(values, -1, keepdims=True)
    scale = lax.rsqrt(jnp.mean(centered * centered, -1, keepdims=True) + EPS)
    return centered * scale, scale


def norm_backward(grad_normed, unit, scale, gain):
    grad_unit = grad_normed * gain
    first = jnp.mean(grad_unit, -1, keepdims=True)
    second = jnp.mean(grad_unit * unit, -1, keepdims=True)
    grad_gain = jnp.sum(grad_normed * unit, 0, keepdims=True)
    grad_shift = jnp.sum(grad_normed, 0, keepdims=True)
    return scale * (grad_unit - first - unit * second), grad_gain, grad_shift


def gelu_both(hidden):
    size = jnp.abs(hidden)
    ratio = 1.0 / (1.0 + (0.3275911 / math.sqrt(2.0)) * size)
    bell = jnp.exp(-0.5 * hidden * hidden)
    series = 0.5 * 1.061405429
    for factor in (-1.453152027, 1.421413741, -0.284496736, 0.254829592):
        series = series * ratio + 0.5 * factor
    tail = series * ratio * bell
    share = jnp.where(hidden >= 0, 1.0 - tail, tail)
    return hidden * share, share + hidden * bell * (1.0 / math.sqrt(2.0 * math.pi))


def lane_index():
    return lax.broadcasted_iota(jnp.int32, (1, 128), 1)


def query_extra(kind):
    place = lax.broadcasted_iota(jnp.int32, (SLOT, 128), 0)
    lane = lax.broadcasted_iota(jnp.int32, (SLOT, 128), 1)
    return (lax.shift_right_logical(place, kind + 7) == lane).astype(F32).astype(BF)


def key_extra(kind, lengths):
    place = lax.broadcasted_iota(jnp.int32, (SLOT, 128), 0)
    lane = lax.broadcasted_iota(jnp.int32, (SLOT, 128), 1)
    size = lax.shift_left(jnp.int32(128), kind)
    within = place & (size - 1)
    limit = jnp.where(
        lane == 0, lengths[0], jnp.where(lane == 1, lengths[1], jnp.where(lane == 2, lengths[2], lengths[3]))
    )
    allowed = (lax.shift_right_logical(place, kind + 7) == lane) & (within < limit)
    return jnp.where(allowed | (lane >= 4), 0.0, MASKED).astype(BF)


def halves():
    lane = lane_index()
    return ((lane < HEAD).astype(F32).astype(BF), (lane >= HEAD).astype(F32).astype(BF))


def future(rows, columns, first):
    row = lax.broadcasted_iota(jnp.int32, (rows, columns), 0)
    column = lax.broadcasted_iota(jnp.int32, (rows, columns), 1) + first
    return row <= column


def attend(query_of, key_of, value_of, store, kind, lengths, causal):
    step = 256 if causal else SLOT
    query_lanes = query_extra(kind)
    key_lanes = key_extra(kind, lengths)
    ones = jnp.ones((HEAD, SLOT), BF)
    logsums = []
    for pair in range(PAIRS):
        queries = query_of(pair) * BF(HEAD**-0.5)
        keys = jnp.concatenate([key_of(pair), key_lanes], 1)
        values = value_of(pair).T
        parts = []
        for half, mask in enumerate(halves()):
            own = jnp.concatenate([queries * mask, query_lanes], 1)
            head_values = jnp.concatenate([values[:HEAD], ones] if half == 0 else [ones, values[HEAD:]], 0)
            columns, sums = [], []
            for first in range(0, SLOT, step):
                seen = first + step if causal else SLOT
                scores = nt(keys[:seen], own[first : first + step])
                if causal:
                    scores = jnp.where(future(seen, step, first), scores, MASKED)
                largest = jnp.max(scores, 0, keepdims=True)
                powers = jnp.exp(scores - largest).astype(BF)
                context = nn(head_values[:, :seen], powers)
                total = context[HEAD : HEAD + 1] if half == 0 else context[0:1]
                columns.append((context[:HEAD] if half == 0 else context[HEAD:]) / total)
                sums.append(largest + jnp.log(total))
            parts.append(jnp.concatenate(columns, 1))
            logsums.append(jnp.concatenate(sums, 1))
        store(pair, jnp.concatenate(parts, 0).T)
    spread = jnp.concatenate([jnp.broadcast_to(row, (GROUP, SLOT)) for row in logsums], 0).T
    return split(spread, 4)


def split(values, first):
    lane = lane_index() % GROUP
    high = values.astype(BF).astype(F32)
    rest = values - high
    middle = rest.astype(BF).astype(F32)
    low = rest - middle
    terms = jnp.where(
        lane == first, high, jnp.where(lane == first + 1, middle, jnp.where(lane == first + 2, low, 0.0))
    )
    return (-terms).astype(BF)


def attend_back(query_of, key_of, value_of, grad_of, contexts, grads, store, logsums, kind, lengths, causal):
    step = 256 if causal else SLOT
    query_lanes = query_extra(kind) + logsums
    key_lanes = key_extra(kind, lengths)
    products = grads.astype(F32) * contexts
    high = products.astype(BF)
    low = (products - high.astype(F32)).astype(BF)
    source = lax.broadcasted_iota(jnp.int32, (D, 128), 0) // HEAD
    target = lax.broadcasted_iota(jnp.int32, (D, 128), 1) // GROUP
    picker = (source == target).astype(F32).astype(BF)
    inner_lanes = split(nn(high, picker) + nn(low, picker), 0)
    lane = lane_index()
    within, group = lane % GROUP, lane // GROUP
    for pair in range(PAIRS):
        queries = query_of(pair) * BF(HEAD**-0.5)
        keys, values, grad_context = key_of(pair), value_of(pair), grad_of(pair)
        keys_t, queries_t, grad_t = keys.T, queries.T, grad_context.T
        grad_queries, grad_keys, grad_values = [], [], []
        for half, mask in enumerate(halves()):
            head = 2 * pair + half
            sum_lanes = ((group == head) & (within >= 4) & (within < 7)).astype(F32).astype(BF)
            one_lanes = ((group == head) & (within < 3)).astype(F32).astype(BF)
            left = jnp.concatenate([keys, key_lanes + sum_lanes], 1)
            right = jnp.concatenate([queries * mask, query_lanes], 1)
            value_left = jnp.concatenate([values, jnp.broadcast_to(one_lanes, (SLOT, 128))], 1)
            grad_right = jnp.concatenate([grad_context * mask, inner_lanes], 1)
            rows = slice(half * HEAD, half * HEAD + HEAD)
            head_keys, head_queries, head_grads = keys_t[rows], queries_t[rows], grad_t[rows]
            for_queries, for_keys, for_values = [], None, None
            for first in range(0, SLOT, step):
                seen = first + step if causal else SLOT
                here = slice(first, first + step)
                scores = nt(left[:seen], right[here])
                if causal:
                    scores = jnp.where(future(seen, step, first), scores, MASKED)
                weights = jnp.exp(scores)
                grad_weights = nt(value_left[:seen], grad_right[here])
                grad_scores = (weights * grad_weights).astype(BF)
                for_queries.append(nn(head_keys[:, :seen], grad_scores))
                key_part = nt(head_queries[:, here], grad_scores)
                value_part = nt(head_grads[:, here], weights.astype(BF))
                if seen < SLOT:
                    none = jnp.zeros((HEAD, SLOT - seen), F32)
                    key_part = jnp.concatenate([key_part, none], 1)
                    value_part = jnp.concatenate([value_part, none], 1)
                for_keys = key_part if for_keys is None else for_keys + key_part
                for_values = value_part if for_values is None else for_values + value_part
            grad_queries.append(jnp.concatenate(for_queries, 1))
            grad_keys.append(for_keys)
            grad_values.append(for_values)
        store(
            pair,
            (jnp.concatenate(grad_queries, 0) * HEAD**-0.5).T.astype(BF),
            jnp.concatenate(grad_keys, 0).T.astype(BF),
            jnp.concatenate(grad_values, 0).T.astype(BF),
        )


def lengths_at(ref, slot):
    return [ref[slot, entry] for entry in range(4)]


def at(ref, start):
    return lambda pair: ref[0, :, start + pair * PAIR : start + (pair + 1) * PAIR]


def add_up(ref, value):
    slot = pl.program_id(0)

    @pl.when(slot == 0)
    def _():
        ref[...] = value

    @pl.when(slot > 0)
    def _():
        ref[...] += value


def project_kernel(me_ref, x_ref, w0, w1, w2, w3, norm_ref, qkv_ref, weights_ref, sems, *, places, half):
    copies = weight_copies((w0, w1, w2, w3), places, half, me_ref[4], weights_ref, sems, SELF_IN, SELF_OUT)
    on_first_slot("start", copies)
    unit, _ = normalize(x_ref[0].astype(F32))
    normed = (unit * norm_ref[0:1] + norm_ref[1:2]).astype(BF)
    on_first_slot("wait", copies)
    for block in range(3):
        qkv_ref[0, :, block * D : (block + 1) * D] = nn(normed, wide(weights_ref, 0, block)).astype(BF)


def keep_context(context_ref, rest_ref):
    def store(pair, context):
        high = context.astype(BF)
        context_ref[0, :, lanes_of(pair)] = high
        rest_ref[0, :, lanes_of(pair)] = (context - high.astype(F32)).astype(BF)

    return store


def self_attend_kernel(
    kind_ref,
    lengths_ref,
    me_ref,
    x_ref,
    qkv_ref,
    w0,
    w1,
    w2,
    w3,
    out_ref,
    context_ref,
    rest_ref,
    sums_ref,
    weights_ref,
    sems,
    *,
    places,
    half,
    causal,
):
    slot = pl.program_id(0)
    copies = weight_copies((w0, w1, w2, w3), places, half, me_ref[4], weights_ref, sems, SELF_OUT, SELF_ROWS)
    on_first_slot("start", copies)
    sums_ref[0] = attend(
        at(qkv_ref, 0),
        at(qkv_ref, D),
        at(qkv_ref, 2 * D),
        keep_context(context_ref, rest_ref),
        kind_ref[slot],
        lengths_at(lengths_ref, slot),
        causal,
    )
    on_first_slot("wait", copies)
    out_ref[0] = x_ref[0].astype(F32) + nn(context_ref[0], wide(weights_ref, 0, 0))


def cross_forward_kernel(
    kind_ref,
    lengths_ref,
    me_ref,
    r_ref,
    memory_ref,
    w0,
    w1,
    w2,
    w3,
    norm_ref,
    out_ref,
    q_ref,
    kv_ref,
    context_ref,
    rest_ref,
    sums_ref,
    weights_ref,
    sems,
    *,
    places,
    half,
):
    slot = pl.program_id(0)
    copies = weight_copies((w0, w1, w2, w3), places, half, me_ref[4], weights_ref, sems, 0, CROSS_ROWS)
    on_first_slot("start", copies)
    values = r_ref[0]
    unit, _ = normalize(values)
    normed = (unit * norm_ref[2:3] + norm_ref[3:4]).astype(BF)
    memory = memory_ref[0]
    on_first_slot("wait", copies)
    q_ref[0] = nn(normed, wide(weights_ref, CROSS_Q, 0)).astype(BF)
    for block in range(2):
        kv_ref[0, :, block * D : (block + 1) * D] = nn(memory, wide(weights_ref, CROSS_KV, block)).astype(BF)
    sums_ref[0] = attend(
        at(q_ref, 0),
        at(kv_ref, 0),
        at(kv_ref, D),
        keep_context(context_ref, rest_ref),
        kind_ref[slot],
        lengths_at(lengths_ref, slot),
        False,
    )
    out_ref[0] = values + nn(context_ref[0], wide(weights_ref, CROSS_OUT, 0))


def ffn_forward_kernel(
    me_ref, r_ref, w0, w1, w2, w3, norm_ref, out_ref, active_ref, slope_ref, weights_ref, sems, *, places, half
):
    copies = weight_copies((w0, w1, w2, w3), places, half, me_ref[4], weights_ref, sems, 0, FFN_ROWS)
    on_first_slot("start", copies)
    values = r_ref[0]
    unit, _ = normalize(values)
    normed = (unit * norm_ref[2:3] + norm_ref[3:4]).astype(BF)
    total = values
    on_first_slot("wait", copies)
    for block in range(BLOCKS):
        active, slope = gelu_both(nn(normed, wide(weights_ref, FFN_IN, block)))
        active = active.astype(BF)
        active_ref[0, :, block * D : (block + 1) * D] = active
        slope_ref[0, :, block * D : (block + 1) * D] = slope.astype(BF)
        total = total + nn(active, tall(weights_ref, FFN_OUT, block))
    out_ref[0] = total.astype(BF)


def ffn_back(grad_out, unit, scale, normed, gain, active_of, slope_of, w_ref, sums_ref):
    low = grad_out.astype(BF)
    normed_t = normed.T
    grad_normed = None
    for block in range(BLOCKS):
        grad_active = nt(low, tall(w_ref, FFN_OUT, block))
        grad_hidden = (grad_active * slope_of(block)).astype(BF)
        add_up(sums_ref.at[1, block], nn(active_of(block).T, low))
        add_up(sums_ref.at[0, block], nn(normed_t, grad_hidden))
        part = nt(grad_hidden, wide(w_ref, FFN_IN, block))
        grad_normed = part if grad_normed is None else grad_normed + part
    grad, grad_gain, grad_shift = norm_backward(grad_normed, unit, scale, gain)
    return grad_out + grad, grad_gain, grad_shift


def ffn_put(core, sums_ref, keep_ref, send_ref):
    @pl.when(last_slot())
    def _():
        for block in range(BLOCKS):
            put_wide(core, keep_ref, send_ref, FFN_IN, block, sums_ref[0, block])
            put_tall(core, keep_ref, send_ref, FFN_OUT, block, sums_ref[1, block])


def ffn_both_kernel(
    me_ref,
    r_ref,
    cotangent_ref,
    w0,
    w1,
    w2,
    w3,
    norm_ref,
    out_ref,
    grad_ref,
    keep_ref,
    send_ref,
    norm_grad_ref,
    weights_ref,
    sems,
    active_ref,
    slope_ref,
    sums_ref,
    *,
    places,
    half,
):
    copies = weight_copies((w0, w1, w2, w3), places, half, me_ref[4], weights_ref, sems, 0, FFN_ROWS)
    on_first_slot("start", copies)
    values = r_ref[0]
    unit, scale = normalize(values)
    gain = norm_ref[4:5]
    normed = (unit * gain + norm_ref[5:6]).astype(BF)
    total = values
    on_first_slot("wait", copies)
    for block in range(BLOCKS):
        active, slope = gelu_both(nn(normed, wide(weights_ref, FFN_IN, block)))
        active = active.astype(BF)
        active_ref[block] = active
        slope_ref[block] = slope
        total = total + nn(active, tall(weights_ref, FFN_OUT, block))
    out_ref[0] = total.astype(BF)
    grad, grad_gain, grad_shift = ffn_back(
        cotangent_ref[0].astype(F32),
        unit,
        scale,
        normed,
        gain,
        lambda block: active_ref[block],
        lambda block: slope_ref[block],
        weights_ref,
        sums_ref,
    )
    grad_ref[0] = grad
    norm_grad_rows(norm_grad_ref, [grad_gain, grad_shift])
    ffn_put(me_ref[4], sums_ref, keep_ref, send_ref)


def ffn_backward_kernel(
    me_ref,
    grad_out_ref,
    r_ref,
    active_ref,
    slope_ref,
    w0,
    w1,
    w2,
    w3,
    norm_ref,
    grad_ref,
    keep_ref,
    send_ref,
    norm_grad_ref,
    weights_ref,
    sems,
    sums_ref,
    *,
    places,
    half,
):
    copies = weight_copies((w0, w1, w2, w3), places, half, me_ref[4], weights_ref, sems, 0, FFN_ROWS)
    on_first_slot("start", copies)
    unit, scale = normalize(r_ref[0])
    gain = norm_ref[2:3]
    normed = (unit * gain + norm_ref[3:4]).astype(BF)
    on_first_slot("wait", copies)
    grad, grad_gain, grad_shift = ffn_back(
        grad_out_ref[0],
        unit,
        scale,
        normed,
        gain,
        lambda block: active_ref[0, :, block * D : (block + 1) * D],
        lambda block: slope_ref[0, :, block * D : (block + 1) * D].astype(F32),
        weights_ref,
        sums_ref,
    )
    grad_ref[0] = grad
    norm_grad_rows(norm_grad_ref, [grad_gain, grad_shift])
    ffn_put(me_ref[4], sums_ref, keep_ref, send_ref)


def attend_back_kernel(
    kind_ref,
    lengths_ref,
    me_ref,
    grad_out_ref,
    q_ref,
    kv_ref,
    context_ref,
    rest_ref,
    sums_in_ref,
    w0,
    w1,
    w2,
    w3,
    proj_ref,
    weights_ref,
    sems,
    low_ref,
    *,
    places,
    half,
    causal,
    start,
    key_at,
):
    slot = pl.program_id(0)
    copies = weight_copies((w0, w1, w2, w3), places, half, me_ref[4], weights_ref, sems, start, start + 16)
    on_first_slot("start", copies)
    on_first_slot("wait", copies)
    low_ref[0] = nt(grad_out_ref[0].astype(BF), wide(weights_ref, 0, 0)).astype(BF)

    def store(pair, grad_query, grad_key, grad_value):
        for number, value in enumerate((grad_query, grad_key, grad_value)):
            proj_ref[0, :, number * D + pair * PAIR : number * D + (pair + 1) * PAIR] = value

    attend_back(
        at(q_ref, 0),
        at(kv_ref, key_at),
        at(kv_ref, key_at + D),
        at(low_ref, 0),
        context_ref[0].astype(F32) + rest_ref[0].astype(F32),
        low_ref[0],
        store,
        sums_in_ref[0],
        kind_ref[slot],
        lengths_at(lengths_ref, slot),
        causal,
    )


def cross_weight_kernel(
    me_ref,
    grad_out_ref,
    r_ref,
    memory_ref,
    context_ref,
    proj_ref,
    cotangent_ref,
    w0,
    w1,
    w2,
    w3,
    norm_ref,
    grad_ref,
    memory_grad_ref,
    keep_ref,
    send_ref,
    norm_grad_ref,
    weights_ref,
    sems,
    sums_ref,
    *,
    places,
    half,
):
    copies = weight_copies((w0, w1, w2, w3), places, half, me_ref[4], weights_ref, sems, 0, CROSS_OUT)
    on_first_slot("start", copies)
    grad_out = grad_out_ref[0]
    unit, scale = normalize(r_ref[0])
    gain = norm_ref[2:3]
    normed_t = (unit * gain + norm_ref[3:4]).astype(BF).T
    memory_t = memory_ref[0].T
    for_query, for_key, for_value = (proj_ref[0, :, part * D : (part + 1) * D] for part in range(3))
    add_up(sums_ref.at[3], nn(context_ref[0].T, grad_out.astype(BF)))
    add_up(sums_ref.at[0], nn(normed_t, for_query))
    add_up(sums_ref.at[1], nn(memory_t, for_key))
    add_up(sums_ref.at[2], nn(memory_t, for_value))
    on_first_slot("wait", copies)
    memory_grad_ref[0] = (
        cotangent_ref[0].astype(F32)
        + nt(for_key, wide(weights_ref, CROSS_KV, 0))
        + nt(for_value, wide(weights_ref, CROSS_KV, 1))
    )
    grad_normed = nt(for_query, wide(weights_ref, CROSS_Q, 0))
    grad, grad_gain, grad_shift = norm_backward(grad_normed, unit, scale, gain)
    grad_ref[0] = grad_out + grad
    norm_grad_rows(norm_grad_ref, [grad_gain, grad_shift])

    @pl.when(last_slot())
    def _():
        core = me_ref[4]
        put_wide(core, keep_ref, send_ref, CROSS_Q, 0, sums_ref[0])
        put_wide(core, keep_ref, send_ref, CROSS_KV, 0, sums_ref[1])
        put_wide(core, keep_ref, send_ref, CROSS_KV, 1, sums_ref[2])
        put_wide(core, keep_ref, send_ref, CROSS_OUT, 0, sums_ref[3])


def self_weight_kernel(
    me_ref, grad_out_ref, x_ref, context_ref, proj_ref, norm_ref, keep_ref, send_ref, sums_ref
):
    unit, _ = normalize(x_ref[0].astype(F32))
    normed_t = (unit * norm_ref[0:1] + norm_ref[1:2]).astype(BF).T
    for block in range(3):
        add_up(sums_ref.at[block], nn(normed_t, proj_ref[0, :, block * D : (block + 1) * D]))
    add_up(sums_ref.at[3], nn(context_ref[0].T, grad_out_ref[0].astype(BF)))

    @pl.when(last_slot())
    def _():
        core = me_ref[4]
        for block in range(3):
            put_wide(core, keep_ref, send_ref, SELF_IN, block, sums_ref[block])
        put_wide(core, keep_ref, send_ref, SELF_OUT, 0, sums_ref[3])


def self_rows_kernel(
    me_ref,
    grad_out_ref,
    x_ref,
    proj_ref,
    w0,
    w1,
    w2,
    w3,
    norm_ref,
    grad_ref,
    norm_grad_ref,
    weights_ref,
    sems,
    *,
    places,
    half,
):
    copies = weight_copies((w0, w1, w2, w3), places, half, me_ref[4], weights_ref, sems, SELF_IN, SELF_OUT)
    on_first_slot("start", copies)
    unit, scale = normalize(x_ref[0].astype(F32))
    on_first_slot("wait", copies)
    grad_normed = None
    for block in range(3):
        part = nt(proj_ref[0, :, block * D : (block + 1) * D], wide(weights_ref, 0, block))
        grad_normed = part if grad_normed is None else grad_normed + part
    grad, grad_gain, grad_shift = norm_backward(grad_normed, unit, scale, norm_ref[0:1])
    grad_ref[0] = (grad_out_ref[0] + grad).astype(BF)
    norm_grad_rows(norm_grad_ref, [grad_gain, grad_shift])


def per_slot(*shape):
    return pl.BlockSpec((1,) + shape, lambda slot: (slot,) + (0,) * len(shape))


def whole_block(*shape):
    return pl.BlockSpec(shape, lambda slot: (0,) * len(shape))


def scalars():
    return pl.BlockSpec(memory_space=pltpu.SMEM)


def call(kernel, name, slots, ins, outs, scratch, *args, flops=0):
    return pl.pallas_call(
        kernel,
        name=name,
        grid=(slots,),
        in_specs=ins,
        out_specs=[spec for spec, _, _ in outs],
        out_shape=[jax.ShapeDtypeStruct(shape, dtype) for _, shape, dtype in outs],
        scratch_shapes=scratch,
        cost_estimate=pl.CostEstimate(flops=flops, bytes_accessed=8 << 20, transcendentals=0),
        compiler_params=pltpu.CompilerParams(vmem_limit_bytes=VMEM_LIMIT, dimension_semantics=("arbitrary",)),
    )(*args)


def slot_array(slots, width, dtype):
    return (per_slot(SLOT, width), (slots, SLOT, width), dtype)


def grad_group(rows):
    return [(whole_block(SHARDS // 2, rows, D), (SHARDS // 2, rows, D), BF)] * 2


NORM_GRADS = (whole_block(8, D), (8, D), F32)
IN_HBM = [pl.BlockSpec(memory_space=pl.ANY)] * 4


def weight_scratch(rows):
    return [pltpu.VMEM((SHARDS // 2, 2, rows, D), BF), pltpu.SemaphoreType.DMA((4,))]


def bound(kernel, weights, **options):
    return functools.partial(kernel, places=weights.places, half=weights.half, **options)


def project(me, rows, weights, norms, name):
    slots = rows.shape[0]
    return call(
        bound(project_kernel, weights),
        name,
        slots,
        [scalars(), per_slot(SLOT, D)] + IN_HBM + [whole_block(*norms.shape)],
        [slot_array(slots, 3 * D, BF)],
        weight_scratch(SELF_OUT - SELF_IN),
        me,
        rows,
        *weights.arrays,
        norms,
        flops=slots * 2 * SLOT * D * D * 3,
    )[0]


def self_attend(kinds, lengths, me, rows, qkv, weights, causal, name):
    slots = rows.shape[0]
    return call(
        bound(self_attend_kernel, weights, causal=causal),
        name,
        slots,
        [scalars(), scalars(), scalars(), per_slot(SLOT, D), per_slot(SLOT, 3 * D)] + IN_HBM,
        [slot_array(slots, D, F32), slot_array(slots, D, BF), slot_array(slots, D, BF), slot_array(slots, 128, BF)],
        weight_scratch(SELF_ROWS - SELF_OUT),
        kinds,
        lengths,
        me,
        rows,
        qkv,
        *weights.arrays,
        flops=slots * 2 * SLOT * D * D * 12,
    )


def cross_forward(kinds, lengths, me, rows, memory, weights, norms):
    slots = rows.shape[0]
    return call(
        bound(cross_forward_kernel, weights),
        "cross_forward",
        slots,
        [scalars(), scalars(), scalars(), per_slot(SLOT, D), per_slot(SLOT, D)]
        + IN_HBM
        + [whole_block(*norms.shape)],
        [
            slot_array(slots, D, F32),
            slot_array(slots, D, BF),
            slot_array(slots, 2 * D, BF),
            slot_array(slots, D, BF),
            slot_array(slots, D, BF),
            slot_array(slots, 128, BF),
        ],
        weight_scratch(CROSS_ROWS),
        kinds,
        lengths,
        me,
        rows,
        memory,
        *weights.arrays,
        norms,
        flops=slots * 2 * SLOT * D * D * 16,
    )


def ffn_forward(me, rows, weights, norms):
    slots = rows.shape[0]
    return call(
        bound(ffn_forward_kernel, weights),
        "ffn_forward",
        slots,
        [scalars(), per_slot(SLOT, D)] + IN_HBM + [whole_block(*norms.shape)],
        [slot_array(slots, D, BF), slot_array(slots, FF, BF), slot_array(slots, FF, BF)],
        weight_scratch(FFN_ROWS),
        me,
        rows,
        *weights.arrays,
        norms,
        flops=slots * 2 * SLOT * D * FF * 4,
    )


def ffn_both(me, rows, cotangent, weights, norms):
    slots = rows.shape[0]
    return call(
        bound(ffn_both_kernel, weights),
        "ffn_both",
        slots,
        [scalars(), per_slot(SLOT, D), per_slot(SLOT, D)] + IN_HBM + [whole_block(*norms.shape)],
        [slot_array(slots, D, BF), slot_array(slots, D, F32)] + grad_group(FFN_ROWS) + [NORM_GRADS],
        weight_scratch(FFN_ROWS)
        + [
            pltpu.VMEM((BLOCKS, SLOT, D), BF),
            pltpu.VMEM((BLOCKS, SLOT, D), F32),
            pltpu.VMEM((2, BLOCKS, D, D), F32),
        ],
        me,
        rows,
        cotangent,
        *weights.arrays,
        norms,
        flops=slots * 2 * SLOT * D * FF * 8,
    )


def ffn_backward(me, grad_out, rows, active, slope, weights, norms):
    slots = rows.shape[0]
    return call(
        bound(ffn_backward_kernel, weights),
        "ffn_backward",
        slots,
        [scalars(), per_slot(SLOT, D), per_slot(SLOT, D), per_slot(SLOT, FF), per_slot(SLOT, FF)]
        + IN_HBM
        + [whole_block(*norms.shape)],
        [slot_array(slots, D, F32)] + grad_group(FFN_ROWS) + [NORM_GRADS],
        weight_scratch(FFN_ROWS) + [pltpu.VMEM((2, BLOCKS, D, D), F32)],
        me,
        grad_out,
        rows,
        active,
        slope,
        *weights.arrays,
        norms,
        flops=slots * 2 * SLOT * D * FF * 6,
    )


def attend_backward(kinds, lengths, me, grad_out, q, kv, kept, weights, causal, start, key_at, name):
    slots = grad_out.shape[0]
    return call(
        bound(attend_back_kernel, weights, causal=causal, start=start, key_at=key_at),
        name,
        slots,
        [scalars(), scalars(), scalars(), per_slot(SLOT, D)]
        + [per_slot(SLOT, part.shape[-1]) for part in (q, kv)]
        + [per_slot(SLOT, D), per_slot(SLOT, D), per_slot(SLOT, 128)]
        + IN_HBM,
        [slot_array(slots, 3 * D, BF)],
        weight_scratch(16) + [pltpu.VMEM((1, SLOT, D), BF)],
        kinds,
        lengths,
        me,
        grad_out,
        q,
        kv,
        *kept,
        *weights.arrays,
        flops=slots * 2 * SLOT * D * D * 20,
    )[0]


def cross_weights(me, grad_out, rows, memory, context, proj, cotangent, weights, norms):
    slots = rows.shape[0]
    return call(
        bound(cross_weight_kernel, weights),
        "cross_weights",
        slots,
        [scalars()]
        + [per_slot(SLOT, D)] * 4
        + [per_slot(SLOT, 3 * D), per_slot(SLOT, D)]
        + IN_HBM
        + [whole_block(*norms.shape)],
        [slot_array(slots, D, F32), slot_array(slots, D, F32)] + grad_group(CROSS_ROWS) + [NORM_GRADS],
        weight_scratch(CROSS_OUT) + [pltpu.VMEM((4, D, D), F32)],
        me,
        grad_out,
        rows,
        memory,
        context,
        proj,
        cotangent,
        *weights.arrays,
        norms,
        flops=slots * 2 * SLOT * D * D * 8,
    )


def self_weights(me, grad_out, rows, context, proj, norms, name):
    slots = rows.shape[0]
    return call(
        self_weight_kernel,
        name,
        slots,
        [scalars()] + [per_slot(SLOT, D)] * 3 + [per_slot(SLOT, 3 * D), whole_block(*norms.shape)],
        grad_group(SELF_ROWS),
        [pltpu.VMEM((4, D, D), F32)],
        me,
        grad_out,
        rows,
        context,
        proj,
        norms,
        flops=slots * 2 * SLOT * D * D * 5,
    )


def self_rows(me, grad_out, rows, proj, weights, norms, name):
    slots = rows.shape[0]
    return call(
        bound(self_rows_kernel, weights),
        name,
        slots,
        [scalars(), per_slot(SLOT, D), per_slot(SLOT, D), per_slot(SLOT, 3 * D)] + IN_HBM + [whole_block(*norms.shape)],
        [slot_array(slots, D, BF), NORM_GRADS],
        weight_scratch(SELF_OUT - SELF_IN),
        me,
        grad_out,
        rows,
        proj,
        *weights.arrays,
        norms,
        flops=slots * 2 * SLOT * D * D * 5,
    )


def axis_sizes(mesh):
    dp, fsdp = mesh.shape["dp"], mesh.shape["fsdp"]
    core = 2 if fsdp % 2 == 0 else 1
    side = math.isqrt(dp)
    first, second = (side, side) if side * side == dp else (dp, 1)
    return (first, second, fsdp // core, core)


AXES = ("dp", "fsdp")
CUBE = (2, 2, 4, 2)
A_BIT, B_BIT, HIGH_BIT, LOW_BIT, CORE_BIT = 16, 8, 4, 2, 1


def swapped(values, bit):
    return lax.ppermute(values, AXES, [(device, device ^ bit) for device in range(SHARDS)])


def moved(values, sizes, axis, shift):
    stride = math.prod(sizes[axis + 1 :])
    pairs = []
    for device in range(math.prod(sizes)):
        place = device // stride % sizes[axis]
        pairs.append((device, device + ((place + shift) % sizes[axis] - place) * stride))
    return lax.ppermute(values, AXES, pairs)


def sum_everywhere(values, sizes):
    if sizes == CUBE:
        for bit in (CORE_BIT, B_BIT, A_BIT, LOW_BIT, HIGH_BIT):
            values = values + swapped(values, bit)
        return values
    for axis in (3, 1, 0, 2):
        total = values
        for shift in range(1, sizes[axis]):
            total = total + moved(values, sizes, axis, shift)
        values = total
    return values


def packed(flat, rows, columns, devices):
    part = flat.reshape(rows // devices, columns // D, D)
    return jnp.swapaxes(part, 0, 1).reshape(-1, D)


def unpacked(part, rows, columns, devices):
    return jnp.swapaxes(part.reshape(columns // D, rows // devices, D), 0, 1).reshape(-1)


SELF_SHAPES = ((D, 3 * D), (D, D))
FFN_SHAPES = ((D, FF), (FF, D))
CROSS_SHAPES = ((D, D), (D, 2 * D), (D, D))


def rows_of(shapes, devices=SHARDS):
    return sum(rows * columns for rows, columns in shapes) // D // devices


def joined(own, other, place, axis):
    return jnp.where(place == 0, jnp.stack([own, other], axis), jnp.stack([other, own], axis))


def gather_cube(groups, extra, me):
    parts = [jnp.concatenate([packed(flat, *shape, SHARDS) for flat, shape in group], 0) for group in groups]
    halves_of = [part.shape[0] // 2 for part in parts]
    one = [part[:half] for part, half in zip(parts, halves_of)]
    two = [part[half:] for part, half in zip(parts, halves_of)] + ([] if extra is None else [extra])
    count = sum(halves_of)
    values = jnp.concatenate(one + two, 0)
    values = joined(values, swapped(values, LOW_BIT), me[3], 0)
    other = swapped(values, HIGH_BIT)
    one = joined(values[:, :count], other[:, :count], me[2], 0)
    two = joined(values[:, count:], other[:, count:], me[2], 0)
    one_other, two_other = swapped(one, B_BIT), swapped(two, A_BIT)
    one, two = joined(one, one_other, me[1], 0), joined(two, two_other, me[0], 0)
    one_other, two_other = swapped(one, A_BIT), swapped(two, B_BIT)
    one, two = joined(one, one_other, me[0], 0), joined(two, two_other, me[1], 1)
    one_other, two_other = swapped(one, CORE_BIT), swapped(two, CORE_BIT)
    own = [half.reshape(SHARDS // 2, -1, D) for half in (one, two)]
    other = [half.reshape(SHARDS // 2, -1, D) for half in (one_other, two_other)]
    results, place = [], 0
    for half in halves_of:
        results.append(Weights(own, other, (place, place), half))
        place += half
    if extra is None:
        return results, None
    lines = joined(own[1][:, place], other[1][:, place], me[4], 1)
    return results, lines.reshape(SHARDS, D)


def gather_plain(groups, extra, devices):
    results = []
    for group in groups:
        parts = []
        for flat, shape in group:
            full = lax.all_gather(flat, AXES, axis=0, tiled=True).reshape(SHARDS, shape[0] // SHARDS, shape[1] // D, D)
            parts.append(jnp.swapaxes(full, 1, 2).reshape(SHARDS, -1, D))
        whole = jnp.concatenate(parts, 1)
        half = whole.shape[1] // 2
        own = [whole[0::2, :half], whole[0::2, half:]]
        other = [whole[1::2, :half], whole[1::2, half:]]
        results.append(Weights(own, other, (0, 0), half))
    return results, None if extra is None else lax.all_gather(extra[0], AXES, axis=0)


def both_halves(refs, rows):
    return slice(0, rows // 2), slice(rows // 2, rows)


def first_sum_kernel(me_ref, *refs):
    members = (len(refs) - 4) // 2
    send_one, keep_one, send_two, keep_two = refs[-4:]
    a, b = me_ref[0], me_ref[1]
    place = 0
    for member in range(members):
        keep, got = refs[member], refs[members + member]
        half = keep.shape[3] // 2
        low, high, here = slice(0, half), slice(half, 2 * half), slice(place, place + half)
        for other in range(2):
            for ref, pick in ((send_one, 1 - b), (keep_one, b)):
                ref[other, 0, here] = keep[other, pick, 0, low] + got[other, pick, 0, low]
            for ref, pick in ((send_two, 1 - a), (keep_two, a)):
                ref[other, 0, here] = keep[pick, other, 0, high] + got[pick, other, 0, high]
        place += half


def second_sum_kernel(me_ref, keep_one, got_one, keep_two, got_two, send_a, kept_a, send_b, kept_b):
    a, b = me_ref[0], me_ref[1]
    for ref, pick in ((send_a, 1 - a), (kept_a, a)):
        ref[0] = keep_one[pick, 0] + got_one[pick, 0]
    for ref, pick in ((send_b, 1 - b), (kept_b, b)):
        ref[0] = keep_two[pick, 0] + got_two[pick, 0]


def third_sum_kernel(me_ref, keep_one, got_one, keep_two, got_two, send, keep):
    z = me_ref[2]
    half = keep_one.shape[2]
    for ref, pick in ((send, 1 - z), (keep, z)):
        ref[0, :half] = keep_one[pick, 0] + got_one[pick, 0]
        ref[0, half:] = keep_two[pick, 0] + got_two[pick, 0]


def fourth_sum_kernel(me_ref, keep, got, send, kept):
    z = me_ref[3]
    for ref, pick in ((send, 1 - z), (kept, z)):
        ref[...] = keep[pick] + got[pick]


def sum_call(kernel, name, steps, me, args, ins, outs):
    return pl.pallas_call(
        kernel,
        name=name,
        grid=(steps,),
        in_specs=[scalars()] + ins,
        out_specs=[spec for spec, _ in outs],
        out_shape=[jax.ShapeDtypeStruct(shape, BF) for _, shape in outs],
        cost_estimate=pl.CostEstimate(flops=0, bytes_accessed=2 * sum(arg.size for arg in args) * 3 // 2, transcendentals=0),
        compiler_params=pltpu.CompilerParams(vmem_limit_bytes=VMEM_LIMIT, dimension_semantics=("arbitrary",)),
    )(me, *args)


def scatter_cube(groups, me, name):
    got = [swapped(send, CORE_BIT) for _, send, _ in groups]
    views = [part.reshape(2, 2, 4, -1, D) for part in [keep for keep, _, _ in groups] + got]
    half = sum(rows_of(shapes) for _, _, shapes in groups) // 2
    quad = (pl.BlockSpec((2, 1, half, D), lambda z: (0, z, 0, 0)), (2, 4, half, D))
    send_one, keep_one, send_two, keep_two = sum_call(
        first_sum_kernel,
        name + "_sum_1",
        4,
        me,
        views,
        [pl.BlockSpec((2, 2, 1, view.shape[3], D), lambda z: (0, 0, z, 0, 0)) for view in views],
        [quad] * 4,
    )
    got_one, got_two = swapped(send_one, B_BIT), swapped(send_two, A_BIT)
    line = (pl.BlockSpec((1, half, D), lambda z: (z, 0, 0)), (4, half, D))
    send_one, keep_one, send_two, keep_two = sum_call(
        second_sum_kernel,
        name + "_sum_2",
        4,
        me,
        [keep_one, got_one, keep_two, got_two],
        [quad[0]] * 4,
        [line] * 4,
    )
    got_one, got_two = swapped(send_one, A_BIT), swapped(send_two, B_BIT)
    views = [part.reshape(2, 2, half, D) for part in (keep_one, got_one, keep_two, got_two)]
    send, keep = sum_call(
        third_sum_kernel,
        name + "_sum_3",
        2,
        me,
        views,
        [pl.BlockSpec((2, 1, half, D), lambda z: (0, z, 0, 0))] * 4,
        [(pl.BlockSpec((1, 2 * half, D), lambda z: (z, 0, 0)), (2, 2 * half, D))] * 2,
    )
    got = swapped(send, HIGH_BIT)
    send, keep = sum_call(
        fourth_sum_kernel,
        name + "_sum_4",
        1,
        me,
        [keep, got],
        [whole_block(2, 2 * half, D)] * 2,
        [(whole_block(2 * half, D), (2 * half, D))] * 2,
    )
    own = keep.astype(F32) + swapped(send, LOW_BIT).astype(F32)
    results, place = [], 0
    for _, _, shapes in groups:
        part = rows_of(shapes) // 2
        rows = jnp.concatenate([own[place : place + part], own[half + place : half + place + part]], 0)
        place += part
        first = 0
        for shape in shapes:
            count = rows_of((shape,))
            results.append(unpacked(rows[first : first + count], *shape, SHARDS))
            first += count
    return results


def scatter_plain(groups, devices):
    results = []
    for keep, send, shapes in groups:
        grads = jnp.stack([keep, send], 1).reshape(SHARDS, -1, D)
        first = 0
        for rows, columns in shapes:
            count = rows_of(((rows, columns),))
            part = grads[:, first : first + count].reshape(SHARDS, columns // D, rows // SHARDS, D)
            flat = jnp.swapaxes(part, 1, 2).reshape(devices, -1)
            results.append(lax.psum_scatter(flat, AXES, scatter_dimension=0, tiled=True).reshape(-1).astype(F32))
            first += count
    return results


def count_live(kinds, lengths, ids):
    positions = jnp.arange(SLOT, dtype=jnp.int32)[None, :]
    size = jnp.left_shift(jnp.int32(SLOT // 4), kinds)[:, None]
    sequence = positions // size
    limit = jnp.zeros_like(sequence)
    for entry in range(4):
        limit = jnp.where(sequence == entry, lengths[:, entry : entry + 1], limit)
    live = positions % size < limit
    hits = (ids.reshape(-1)[:, None] == jnp.arange(VOCAB, dtype=jnp.int32)[None, :]) & live.reshape(-1)[:, None]
    return jnp.sum(hits.astype(F32), 0)


def local(
    sizes,
    enc_in,
    dec_in,
    bucket,
    enc_lengths,
    dec_lengths,
    pred_ids,
    running_counts,
    enc_attn_in,
    enc_attn_out,
    enc_ff_in,
    enc_ff_out,
    enc_norms,
    dec_self_in,
    dec_self_out,
    dec_cross_q,
    dec_cross_kv,
    dec_cross_out,
    dec_ff_in,
    dec_ff_out,
    dec_norms,
    enc_cotangent,
    dec_cotangent,
):
    devices = math.prod(sizes)
    cube = sizes == CUBE
    index = lax.axis_index("dp") * lax.axis_size("fsdp") + lax.axis_index("fsdp")
    if cube:
        me = jnp.stack([index >> 4 & 1, index >> 3 & 1, index >> 2 & 1, index >> 1 & 1, index & 1]).astype(jnp.int32)
    else:
        me = jnp.zeros((5,), jnp.int32)

    def gather(groups, extra=None):
        return gather_cube(groups, extra, me) if cube else gather_plain(groups, extra, devices)

    def scatter(name, *groups):
        return scatter_cube(groups, me, name) if cube else scatter_plain(groups, devices)

    enc_count, dec_count = enc_norms.shape[0], dec_norms.shape[0]
    both = jnp.concatenate([enc_norms, dec_norms])
    norm_part = jnp.pad(both[None, :], ((0, 7), (0, D - both.shape[0])))
    enc_self_group = list(zip((enc_attn_in, enc_attn_out), SELF_SHAPES))
    dec_self_group = list(zip((dec_self_in, dec_self_out), SELF_SHAPES))
    enc_ff_group = list(zip((enc_ff_in, enc_ff_out), FFN_SHAPES))
    cross_group = list(zip((dec_cross_q, dec_cross_kv, dec_cross_out), CROSS_SHAPES))
    dec_ff_group = list(zip((dec_ff_in, dec_ff_out), FFN_SHAPES))
    (enc_self_w, dec_self_w), norm_lines = gather([enc_self_group, dec_self_group], norm_part)
    (enc_ff_w,), _ = gather([enc_ff_group])
    (cross_w, dec_ff_w), _ = gather([cross_group, dec_ff_group])
    enc_norm = norm_lines[:, :enc_count].reshape(4, D).astype(F32)
    dec_norm = norm_lines[:, enc_count : enc_count + dec_count].reshape(6, D).astype(F32)

    enc_qkv = project(me, enc_in, enc_self_w, enc_norm, "enc_project")
    dec_qkv = project(me, dec_in, dec_self_w, dec_norm, "dec_project")
    attended, *enc_kept = self_attend(bucket, enc_lengths, me, enc_in, enc_qkv, enc_self_w, False, "enc_attend")
    first_out, *dec_kept = self_attend(bucket, dec_lengths, me, dec_in, dec_qkv, dec_self_w, True, "dec_attend")
    memory, active, slope = ffn_forward(me, attended, enc_ff_w, enc_norm)
    second_out, cross_q, cross_kv, *cross_kept = cross_forward(
        bucket, enc_lengths, me, first_out, memory, cross_w, dec_norm
    )
    decoded, grad_second, dec_ff_keep, dec_ff_send, ffn_norm_g = ffn_both(
        me, second_out, dec_cotangent, dec_ff_w, dec_norm
    )
    cross_proj = attend_backward(
        bucket,
        enc_lengths,
        me,
        grad_second,
        cross_q,
        cross_kv,
        cross_kept,
        cross_w,
        False,
        CROSS_OUT,
        0,
        "cross_attend_back",
    )
    grad_first, grad_memory, cross_keep, cross_send, cross_norm_g = cross_weights(
        me, grad_second, first_out, memory, cross_kept[0], cross_proj, enc_cotangent, cross_w, dec_norm
    )
    (dec_ff_in_g, dec_ff_out_g, cross_q_g, cross_kv_g, cross_out_g) = scatter(
        "dec", (dec_ff_keep, dec_ff_send, FFN_SHAPES), (cross_keep, cross_send, CROSS_SHAPES)
    )
    grad_attended, enc_ff_keep, enc_ff_send, enc_ffn_norm_g = ffn_backward(
        me, grad_memory, attended, active, slope, enc_ff_w, enc_norm
    )
    dec_proj = attend_backward(
        bucket, dec_lengths, me, grad_first, dec_qkv, dec_qkv, dec_kept, dec_self_w, True, SELF_OUT, D, "dec_attend_back"
    )
    dec_self_keep, dec_self_send = self_weights(
        me, grad_first, dec_in, dec_kept[0], dec_proj, dec_norm, "dec_self_weights"
    )
    (enc_ff_in_g, enc_ff_out_g, dec_self_in_g, dec_self_out_g) = scatter(
        "mid", (enc_ff_keep, enc_ff_send, FFN_SHAPES), (dec_self_keep, dec_self_send, SELF_SHAPES)
    )
    enc_proj = attend_backward(
        bucket,
        enc_lengths,
        me,
        grad_attended,
        enc_qkv,
        enc_qkv,
        enc_kept,
        enc_self_w,
        False,
        SELF_OUT,
        D,
        "enc_attend_back",
    )
    enc_self_keep, enc_self_send = self_weights(
        me, grad_attended, enc_in, enc_kept[0], enc_proj, enc_norm, "enc_self_weights"
    )
    (enc_attn_in_g, enc_attn_out_g) = scatter("enc", (enc_self_keep, enc_self_send, SELF_SHAPES))
    grad_enc_in, enc_self_norm_g = self_rows(me, grad_attended, enc_in, enc_proj, enc_self_w, enc_norm, "enc_self_rows")
    grad_dec_in, dec_self_norm_g = self_rows(me, grad_first, dec_in, dec_proj, dec_self_w, dec_norm, "dec_self_rows")

    counted = jnp.pad(count_live(bucket, dec_lengths, pred_ids), (0, 2 * D - VOCAB)).reshape(2, D)
    small = jnp.concatenate(
        [part[:2] for part in (enc_self_norm_g, enc_ffn_norm_g, dec_self_norm_g, cross_norm_g, ffn_norm_g, counted)]
        + [jnp.zeros((4, D), F32)],
        0,
    )
    small = sum_everywhere(small, sizes)
    enc_norm_own = lax.dynamic_slice(small[:4].reshape(-1), (index * enc_count,), (enc_count,))
    dec_norm_own = lax.dynamic_slice(small[4:10].reshape(-1), (index * dec_count,), (dec_count,))
    counts = running_counts + small[10:12].reshape(-1)[:VOCAB].astype(jnp.int32)
    return (
        memory,
        decoded,
        grad_enc_in,
        grad_dec_in,
        enc_attn_in_g,
        enc_attn_out_g,
        enc_ff_in_g,
        enc_ff_out_g,
        enc_norm_own,
        dec_self_in_g,
        dec_self_out_g,
        cross_q_g,
        cross_kv_g,
        cross_out_g,
        dec_ff_in_g,
        dec_ff_out_g,
        dec_norm_own,
        counts,
    )


def solution(mesh):
    rows = P(AXES, None, None)
    pair = P(AXES, None)
    flat = P(AXES)
    return jax.shard_map(
        functools.partial(local, axis_sizes(mesh)),
        mesh=mesh,
        in_specs=(rows, rows, flat, pair, pair, pair, P()) + (flat,) * 13 + (rows, rows),
        out_specs=(rows,) * 4 + (flat,) * 13 + (P(),),
        check_vma=False,
    )
```

```python
import functools
import math
import jax
import jax.numpy as jnp
from jax import lax
from jax.experimental import pallas as pl
from jax.experimental.pallas import tpu as pltpu
from jax.sharding import PartitionSpec as P

D = 512
HEAD = 64
FF = 2048
VOCAB = 523
SLOT = 512
SHARDS = 32
BLOCKS = FF // D
EPS = 1e-05
PAIR = 2 * HEAD
PAIRS = D // PAIR
GROUP = 16
MASKED = -(2.0**30)
COST = 3.0
UPPER_MB = 56
BF = jnp.bfloat16
F32 = jnp.float32

SELF_ROWS, SELF_IN, SELF_OUT = 64, 0, 48
FFN_ROWS, FFN_IN, FFN_OUT = 128, 0, 64
CROSS_ROWS, CROSS_Q, CROSS_KV, CROSS_OUT = 64, 0, 16, 48


def nn(left, right):
    return lax.dot_general(left, right, (((1,), (0,)), ((), ())), preferred_element_type=F32)


def nt(left, right):
    return lax.dot_general(left, right, (((1,), (1,)), ((), ())), preferred_element_type=F32)


def wide(ref, start, block):
    first = start + 16 * block
    return ref[:, :, first : first + 16, :].reshape(D, D)


def tall(ref, start, block):
    return ref[4 * block : 4 * block + 4, :, start : start + 64, :].reshape(D, D)


def put_shards(core, refs, lead, rows, shards):
    if len(refs) == 1:
        refs[0][lead, :, rows, :] = shards.astype(BF)
    else:
        refs[0][lead, rows, :] = jnp.where(core == 0, shards[:, 0], shards[:, 1]).astype(BF)
        refs[1][lead, rows, :] = jnp.where(core == 0, shards[:, 1], shards[:, 0]).astype(BF)


def put_wide(core, refs, start, block, value):
    rows = slice(start + 16 * block, start + 16 * block + 16)
    put_shards(core, refs, slice(0, SHARDS // 2), rows, value.reshape(SHARDS // 2, 2, 16, D))


def put_tall(core, refs, start, block, value):
    put_shards(core, refs, slice(4 * block, 4 * block + 4), slice(start, start + 64), value.reshape(4, 2, 64, D))


class Weights:
    def __init__(self, arrays, place, half):
        self.arrays = arrays
        self.place = place
        self.half = half


def weight_copies(pieces, place, half, core, ref, sems, low, high):
    if len(pieces) == 1:
        return [pltpu.make_async_copy(pieces[0].at[:, :, place + low : place + high, :], ref, sems.at[0])]
    copies = []
    for number in range(2):
        first, last = max(low, number * half), min(high, (number + 1) * half)
        if first < last:
            source = slice(place + first - number * half, place + last - number * half)
            for other in range(2):
                copies.append(
                    pltpu.make_async_copy(
                        pieces[2 * number + other].at[:, source, :],
                        ref.at[:, core if other == 0 else 1 - core, first - low : last - low, :],
                        sems.at[2 * number + other],
                    )
                )
    return copies


def on_first_slot(action, copies):
    @pl.when(pl.program_id(0) == 0)
    def _():
        for copy in copies:
            getattr(copy, action)()


def norm_grad_rows(ref, gains_and_shifts):
    rows = jnp.concatenate(gains_and_shifts + [jnp.zeros((8 - len(gains_and_shifts), D), F32)], 0)
    add_up(ref, rows)


def last_slot():
    return pl.program_id(0) == pl.num_programs(0) - 1


def lanes_of(pair):
    return slice(pair * PAIR, (pair + 1) * PAIR)


def normalize(values):
    centered = values - jnp.mean(values, -1, keepdims=True)
    scale = lax.rsqrt(jnp.mean(centered * centered, -1, keepdims=True) + EPS)
    return centered * scale, scale


def norm_backward(grad_normed, unit, scale, gain):
    grad_unit = grad_normed * gain
    first = jnp.mean(grad_unit, -1, keepdims=True)
    second = jnp.mean(grad_unit * unit, -1, keepdims=True)
    grad_gain = jnp.sum(grad_normed * unit, 0, keepdims=True)
    grad_shift = jnp.sum(grad_normed, 0, keepdims=True)
    return scale * (grad_unit - first - unit * second), grad_gain, grad_shift


def gelu_both(hidden):
    size = jnp.abs(hidden)
    ratio = 1.0 / (1.0 + (0.3275911 / math.sqrt(2.0)) * size)
    bell = jnp.exp(-0.5 * hidden * hidden)
    series = 0.5 * 1.061405429
    for factor in (-1.453152027, 1.421413741, -0.284496736, 0.254829592):
        series = series * ratio + 0.5 * factor
    tail = series * ratio * bell
    share = jnp.where(hidden >= 0, 1.0 - tail, tail)
    return hidden * share, share + hidden * bell * (1.0 / math.sqrt(2.0 * math.pi))


def lane_index():
    return lax.broadcasted_iota(jnp.int32, (1, 128), 1)


def query_extra(kind):
    place = lax.broadcasted_iota(jnp.int32, (SLOT, 128), 0)
    lane = lax.broadcasted_iota(jnp.int32, (SLOT, 128), 1)
    return (lax.shift_right_logical(place, kind + 7) == lane).astype(F32).astype(BF)


def key_extra(kind, lengths):
    place = lax.broadcasted_iota(jnp.int32, (SLOT, 128), 0)
    lane = lax.broadcasted_iota(jnp.int32, (SLOT, 128), 1)
    size = lax.shift_left(jnp.int32(128), kind)
    within = place & (size - 1)
    limit = jnp.where(
        lane == 0, lengths[0], jnp.where(lane == 1, lengths[1], jnp.where(lane == 2, lengths[2], lengths[3]))
    )
    allowed = (lax.shift_right_logical(place, kind + 7) == lane) & (within < limit)
    return jnp.where(allowed | (lane >= 4), 0.0, MASKED).astype(BF)


def halves():
    lane = lane_index()
    return ((lane < HEAD).astype(F32).astype(BF), (lane >= HEAD).astype(F32).astype(BF))


def future(rows, columns, first):
    row = lax.broadcasted_iota(jnp.int32, (rows, columns), 0)
    column = lax.broadcasted_iota(jnp.int32, (rows, columns), 1) + first
    return row <= column


def pipelined(items, ahead, start, finish):
    waiting = []
    for number, item in enumerate(items):
        while len(waiting) <= ahead and number + len(waiting) < len(items):
            waiting.append(start(*items[number + len(waiting)]))
        finish(*item, waiting.pop(0))


def attend(query_of, key_of, value_of, store, kind, lengths, causal):
    step = 256
    query_lanes = query_extra(kind)
    key_lanes = key_extra(kind, lengths)
    ones = jnp.ones((HEAD, SLOT), BF)
    mask = halves()
    inputs, parts, sums = {}, {}, {}

    def seen(first):
        return first + step if causal else SLOT

    def start(pair, half, first):
        if pair not in inputs:
            queries = query_of(pair) * BF(HEAD**-0.5)
            inputs[pair] = (queries, jnp.concatenate([key_of(pair), key_lanes], 1), value_of(pair).T)
        queries, keys, _ = inputs[pair]
        own = jnp.concatenate([queries[first : first + step] * mask[half], query_lanes[first : first + step]], 1)
        return nt(keys[: seen(first)], own)

    def finish(pair, half, first, scores):
        values = inputs[pair][2]
        if causal:
            scores = jnp.where(future(seen(first), step, first), scores, MASKED)
        largest = jnp.max(scores, 0, keepdims=True)
        powers = jnp.exp(scores - largest).astype(BF)
        head_values = jnp.concatenate([values[:HEAD], ones] if half == 0 else [ones, values[HEAD:]], 0)
        context = nn(head_values[:, : seen(first)], powers)
        total = context[HEAD : HEAD + 1] if half == 0 else context[0:1]
        parts[pair, half, first] = (context[:HEAD] if half == 0 else context[HEAD:]) * (1.0 / total)
        sums[pair, half, first] = largest + jnp.log(total)
        if half == 1 and first == SLOT - step:
            rows = [jnp.concatenate([parts[pair, side, at] for at in range(0, SLOT, step)], 1) for side in range(2)]
            store(pair, jnp.concatenate(rows, 0).T)

    items = [(pair, half, first) for pair in range(PAIRS) for half in range(2) for first in range(0, SLOT, step)]
    pipelined(items, 4, start, finish)
    spread = [
        jnp.broadcast_to(jnp.concatenate([sums[pair, half, at] for at in range(0, SLOT, step)], 1), (GROUP, SLOT))
        for pair in range(PAIRS)
        for half in range(2)
    ]
    return split(jnp.concatenate(spread, 0).T, 4)


def split(values, first):
    lane = lane_index() % GROUP
    high = values.astype(BF).astype(F32)
    rest = values - high
    middle = rest.astype(BF).astype(F32)
    low = rest - middle
    terms = jnp.where(
        lane == first, high, jnp.where(lane == first + 1, middle, jnp.where(lane == first + 2, low, 0.0))
    )
    return (-terms).astype(BF)


def attend_back(query_of, key_of, value_of, grad_of, contexts, grads, store, logsums, kind, lengths, causal):
    step = 256 if causal else SLOT
    query_lanes = query_extra(kind) + logsums
    key_lanes = key_extra(kind, lengths)
    products = grads.astype(F32) * contexts
    high = products.astype(BF)
    low = (products - high.astype(F32)).astype(BF)
    source = lax.broadcasted_iota(jnp.int32, (D, 128), 0) // HEAD
    target = lax.broadcasted_iota(jnp.int32, (D, 128), 1) // GROUP
    picker = (source == target).astype(F32).astype(BF)
    inner_lanes = split(nn(high, picker) + nn(low, picker), 0)
    lane = lane_index()
    within, group = lane % GROUP, lane // GROUP
    mask = halves()
    inputs, heads, results = {}, {}, {}

    def seen(first):
        return first + step if causal else SLOT

    def start(pair, half, first):
        if pair not in inputs:
            inputs[pair] = (query_of(pair) * BF(HEAD**-0.5), key_of(pair), value_of(pair), grad_of(pair), key_of(pair).T)
        queries, keys, values, grad_context, _ = inputs[pair]
        if (pair, half) not in heads:
            head = 2 * pair + half
            sum_lanes = ((group == head) & (within >= 4) & (within < 7)).astype(F32).astype(BF)
            one_lanes = ((group == head) & (within < 3)).astype(F32).astype(BF)
            heads[pair, half] = (
                jnp.concatenate([keys, key_lanes + sum_lanes], 1),
                jnp.concatenate([queries * mask[half], query_lanes], 1),
                jnp.concatenate([values, jnp.broadcast_to(one_lanes, (SLOT, 128))], 1),
                jnp.concatenate([grad_context * mask[half], inner_lanes], 1),
            )
        left, right, value_left, grad_right = heads[pair, half]
        here = slice(first, first + step)
        return nt(left[: seen(first)], right[here]), nt(value_left[: seen(first)], grad_right[here])

    def finish(pair, half, first, products):
        scores, grad_weights = products
        queries, _, _, grad_context, keys_t = inputs[pair]
        if causal:
            scores = jnp.where(future(seen(first), step, first), scores, MASKED)
        weights = jnp.exp(scores)
        grad_scores = (weights * grad_weights).astype(BF)
        here = slice(first, first + step)
        for_queries = nn(keys_t[half * HEAD : half * HEAD + HEAD, : seen(first)], grad_scores)
        for_keys = nn(grad_scores, queries[here] * mask[half])
        for_values = nn(weights.astype(BF), grad_context[here] * mask[half])
        if seen(first) < SLOT:
            none = jnp.zeros((SLOT - seen(first), PAIR), F32)
            for_keys = jnp.concatenate([for_keys, none], 0)
            for_values = jnp.concatenate([for_values, none], 0)
        results[pair, half, first] = (for_queries, for_keys, for_values)
        if half == 1 and first == SLOT - step:
            places = range(0, SLOT, step)
            rows = [jnp.concatenate([results[pair, side, at][0] for at in places], 1) for side in range(2)]
            keys_sum, values_sum = (
                functools.reduce(jnp.add, [results[pair, side, at][number] for side in range(2) for at in places])
                for number in (1, 2)
            )
            store(
                pair,
                (jnp.concatenate(rows, 0) * HEAD**-0.5).T.astype(BF),
                keys_sum.astype(BF),
                values_sum.astype(BF),
            )

    items = [(pair, half, first) for pair in range(PAIRS) for half in range(2) for first in range(0, SLOT, step)]
    pipelined(items, 2 if causal else 1, start, finish)


def lengths_at(ref, slot):
    return [ref[slot, entry] for entry in range(4)]


def at(ref, start):
    return lambda pair: ref[0, :, start + pair * PAIR : start + (pair + 1) * PAIR]


def add_up(ref, value):
    slot = pl.program_id(0)

    @pl.when(slot == 0)
    def _():
        ref[...] = value

    @pl.when(slot > 0)
    def _():
        ref[...] += value


def project_kernel(me_ref, x_ref, w, norm_ref, qkv_ref, weights_ref, sems, *, place, half):
    copies = weight_copies(w, place, half, me_ref[4], weights_ref, sems, SELF_IN, SELF_OUT)
    on_first_slot("start", copies)
    unit, _ = normalize(x_ref[0].astype(F32))
    normed = (unit * norm_ref[0:1] + norm_ref[1:2]).astype(BF)
    on_first_slot("wait", copies)
    for block in range(3):
        qkv_ref[0, :, block * D : (block + 1) * D] = nn(normed, wide(weights_ref, 0, block)).astype(BF)


def keep_context(context_ref, rest_ref):
    def store(pair, context):
        high = context.astype(BF)
        context_ref[0, :, lanes_of(pair)] = high
        rest_ref[0, :, lanes_of(pair)] = (context - high.astype(F32)).astype(BF)

    return store


def self_attend_kernel(
    kind_ref,
    lengths_ref,
    me_ref,
    x_ref,
    qkv_ref,
    w,
    out_ref,
    context_ref,
    rest_ref,
    sums_ref,
    weights_ref,
    sems,
    *,
    place,
    half,
    causal,
):
    slot = pl.program_id(0)
    copies = weight_copies(w, place, half, me_ref[4], weights_ref, sems, SELF_OUT, SELF_ROWS)
    on_first_slot("start", copies)
    sums_ref[0] = attend(
        at(qkv_ref, 0),
        at(qkv_ref, D),
        at(qkv_ref, 2 * D),
        keep_context(context_ref, rest_ref),
        kind_ref[slot],
        lengths_at(lengths_ref, slot),
        causal,
    )
    on_first_slot("wait", copies)
    out_ref[0] = x_ref[0].astype(F32) + nn(context_ref[0], wide(weights_ref, 0, 0))


def ffn_forward_kernel(
    me_ref, r_ref, w, norm_ref, out_ref, active_ref, slope_ref, weights_ref, sems, *, place, half
):
    copies = weight_copies(w, place, half, me_ref[4], weights_ref, sems, 0, FFN_ROWS)
    on_first_slot("start", copies)
    values = r_ref[0]
    unit, _ = normalize(values)
    normed = (unit * norm_ref[2:3] + norm_ref[3:4]).astype(BF)
    total = values
    on_first_slot("wait", copies)
    for block in range(BLOCKS):
        active, slope = gelu_both(nn(normed, wide(weights_ref, FFN_IN, block)))
        active = active.astype(BF)
        active_ref[0, :, block * D : (block + 1) * D] = active
        slope_ref[0, :, block * D : (block + 1) * D] = slope.astype(BF)
        total = total + nn(active, tall(weights_ref, FFN_OUT, block))
    out_ref[0] = total.astype(BF)


def ffn_back(grad_out, unit, scale, normed, gain, active_of, slope_of, w_ref, sums_ref):
    low = grad_out.astype(BF)
    normed_t = normed.T
    grad_normed = None
    for block in range(BLOCKS):
        grad_active = nt(low, tall(w_ref, FFN_OUT, block))
        grad_hidden = (grad_active * slope_of(block)).astype(BF)
        add_up(sums_ref.at[1, block], nn(active_of(block).T, low))
        add_up(sums_ref.at[0, block], nn(normed_t, grad_hidden))
        part = nt(grad_hidden, wide(w_ref, FFN_IN, block))
        grad_normed = part if grad_normed is None else grad_normed + part
    grad, grad_gain, grad_shift = norm_backward(grad_normed, unit, scale, gain)
    return grad_out + grad, grad_gain, grad_shift


def ffn_put(core, sums_ref, grads):
    @pl.when(last_slot())
    def _():
        for block in range(BLOCKS):
            put_wide(core, grads, FFN_IN, block, sums_ref[0, block])
            put_tall(core, grads, FFN_OUT, block, sums_ref[1, block])


def ffn_backward_kernel(
    me_ref,
    grad_out_ref,
    r_ref,
    active_ref,
    slope_ref,
    w,
    norm_ref,
    grad_ref,
    grads,
    norm_grad_ref,
    weights_ref,
    sems,
    sums_ref,
    *,
    place,
    half,
):
    copies = weight_copies(w, place, half, me_ref[4], weights_ref, sems, 0, FFN_ROWS)
    on_first_slot("start", copies)
    unit, scale = normalize(r_ref[0])
    gain = norm_ref[2:3]
    normed = (unit * gain + norm_ref[3:4]).astype(BF)
    on_first_slot("wait", copies)
    grad, grad_gain, grad_shift = ffn_back(
        grad_out_ref[0],
        unit,
        scale,
        normed,
        gain,
        lambda block: active_ref[0, :, block * D : (block + 1) * D],
        lambda block: slope_ref[0, :, block * D : (block + 1) * D].astype(F32),
        weights_ref,
        sums_ref,
    )
    grad_ref[0] = grad
    norm_grad_rows(norm_grad_ref, [grad_gain, grad_shift])
    ffn_put(me_ref[4], sums_ref, grads)


def attend_back_kernel(
    kind_ref,
    lengths_ref,
    me_ref,
    grad_out_ref,
    q_ref,
    kv_ref,
    context_ref,
    rest_ref,
    sums_in_ref,
    w,
    proj_ref,
    weights_ref,
    sems,
    low_ref,
    *,
    place,
    half,
    causal,
    start,
    key_at,
):
    slot = pl.program_id(0)
    copies = weight_copies(w, place, half, me_ref[4], weights_ref, sems, start, start + 16)
    on_first_slot("start", copies)
    on_first_slot("wait", copies)
    low_ref[0] = nt(grad_out_ref[0].astype(BF), wide(weights_ref, 0, 0)).astype(BF)

    def store(pair, grad_query, grad_key, grad_value):
        for number, value in enumerate((grad_query, grad_key, grad_value)):
            proj_ref[0, :, number * D + pair * PAIR : number * D + (pair + 1) * PAIR] = value

    attend_back(
        at(q_ref, 0),
        at(kv_ref, key_at),
        at(kv_ref, key_at + D),
        at(low_ref, 0),
        context_ref[0].astype(F32) + rest_ref[0].astype(F32),
        low_ref[0],
        store,
        sums_in_ref[0],
        kind_ref[slot],
        lengths_at(lengths_ref, slot),
        causal,
    )


def upper_kernel(
    kind_ref,
    lengths_ref,
    me_ref,
    r_ref,
    memory_ref,
    enc_cotangent_ref,
    dec_cotangent_ref,
    w_cross,
    w_ff,
    norm_ref,
    out_ref,
    grad_ref,
    memory_grad_ref,
    ff_grads,
    cross_grads,
    norm_grad_ref,
    cross_ref,
    cross_sems,
    ff_ref,
    ff_sems,
    qkv_ref,
    context_ref,
    low_ref,
    proj_ref,
    active_ref,
    slope_ref,
    second_ref,
    ff_sums_ref,
    sums_ref,
    *,
    cross_place,
    cross_half,
    ff_place,
    ff_half,
):
    slot = pl.program_id(0)
    core = me_ref[4]
    copies = weight_copies(w_cross, cross_place, cross_half, core, cross_ref, cross_sems, 0, CROSS_ROWS)
    ff_copies = weight_copies(w_ff, ff_place, ff_half, core, ff_ref, ff_sems, 0, FFN_ROWS)
    on_first_slot("start", copies + ff_copies)
    kind, lengths = kind_ref[slot], lengths_at(lengths_ref, slot)
    unit, scale = normalize(r_ref[0])
    gain = norm_ref[2:3]
    normed = (unit * gain + norm_ref[3:4]).astype(BF)
    memory = memory_ref[0]
    on_first_slot("wait", copies)
    qkv_ref[0, :, :D] = nn(normed, wide(cross_ref, CROSS_Q, 0)).astype(BF)
    for block in range(2):
        qkv_ref[0, :, (block + 1) * D : (block + 2) * D] = nn(memory, wide(cross_ref, CROSS_KV, block)).astype(BF)

    def keep(pair, context):
        context_ref[:, lanes_of(pair)] = context

    logsums = attend(at(qkv_ref, 0), at(qkv_ref, D), at(qkv_ref, 2 * D), keep, kind, lengths, False)
    second = r_ref[0] + nn(context_ref[...].astype(BF), wide(cross_ref, CROSS_OUT, 0))

    ff_unit, ff_scale = normalize(second)
    ff_gain = norm_ref[4:5]
    ff_normed = (ff_unit * ff_gain + norm_ref[5:6]).astype(BF)
    on_first_slot("wait", ff_copies)
    total = second
    for block in range(BLOCKS):
        active, slope = gelu_both(nn(ff_normed, wide(ff_ref, FFN_IN, block)))
        active = active.astype(BF)
        active_ref[block] = active
        slope_ref[block] = slope.astype(BF)
        total = total + nn(active, tall(ff_ref, FFN_OUT, block))
    out_ref[0] = total.astype(BF)
    grad_second, ff_gain_grad, ff_shift_grad = ffn_back(
        dec_cotangent_ref[0].astype(F32),
        ff_unit,
        ff_scale,
        ff_normed,
        ff_gain,
        lambda block: active_ref[block],
        lambda block: slope_ref[block].astype(F32),
        ff_ref,
        ff_sums_ref,
    )
    second_ref[...] = grad_second
    ffn_put(core, ff_sums_ref, ff_grads)

    low = second_ref[...].astype(BF)
    add_up(sums_ref.at[3], nn(context_ref[...].astype(BF).T, low))
    low_ref[0] = nt(low, wide(cross_ref, CROSS_OUT, 0)).astype(BF)

    def store(pair, grad_query, grad_key, grad_value):
        for number, value in enumerate((grad_query, grad_key, grad_value)):
            proj_ref[number, :, lanes_of(pair)] = value

    attend_back(
        at(qkv_ref, 0),
        at(qkv_ref, D),
        at(qkv_ref, 2 * D),
        at(low_ref, 0),
        context_ref[...],
        low_ref[0],
        store,
        logsums,
        kind,
        lengths,
        False,
    )
    unit, scale = normalize(r_ref[0])
    normed_t = (unit * gain + norm_ref[3:4]).astype(BF).T
    memory_t = memory_ref[0].T
    add_up(sums_ref.at[0], nn(normed_t, proj_ref[0]))
    add_up(sums_ref.at[1], nn(memory_t, proj_ref[1]))
    add_up(sums_ref.at[2], nn(memory_t, proj_ref[2]))
    memory_grad_ref[0] = (
        enc_cotangent_ref[0].astype(F32)
        + nt(proj_ref[1], wide(cross_ref, CROSS_KV, 0))
        + nt(proj_ref[2], wide(cross_ref, CROSS_KV, 1))
    )
    grad, grad_gain, grad_shift = norm_backward(nt(proj_ref[0], wide(cross_ref, CROSS_Q, 0)), unit, scale, gain)
    grad_ref[0] = second_ref[...] + grad
    norm_grad_rows(norm_grad_ref, [grad_gain, grad_shift, ff_gain_grad, ff_shift_grad])

    @pl.when(last_slot())
    def _():
        put_wide(core, cross_grads, CROSS_Q, 0, sums_ref[0])
        put_wide(core, cross_grads, CROSS_KV, 0, sums_ref[1])
        put_wide(core, cross_grads, CROSS_KV, 1, sums_ref[2])
        put_wide(core, cross_grads, CROSS_OUT, 0, sums_ref[3])


def self_weight_kernel(
    me_ref, grad_out_ref, x_ref, context_ref, proj_ref, norm_ref, grads, sums_ref
):
    unit, _ = normalize(x_ref[0].astype(F32))
    normed_t = (unit * norm_ref[0:1] + norm_ref[1:2]).astype(BF).T
    for block in range(3):
        add_up(sums_ref.at[block], nn(normed_t, proj_ref[0, :, block * D : (block + 1) * D]))
    add_up(sums_ref.at[3], nn(context_ref[0].T, grad_out_ref[0].astype(BF)))

    @pl.when(last_slot())
    def _():
        core = me_ref[4]
        for block in range(3):
            put_wide(core, grads, SELF_IN, block, sums_ref[block])
        put_wide(core, grads, SELF_OUT, 0, sums_ref[3])


def self_rows_kernel(
    me_ref,
    grad_out_ref,
    x_ref,
    proj_ref,
    w,
    norm_ref,
    grad_ref,
    norm_grad_ref,
    weights_ref,
    sems,
    *,
    place,
    half,
):
    copies = weight_copies(w, place, half, me_ref[4], weights_ref, sems, SELF_IN, SELF_OUT)
    on_first_slot("start", copies)
    unit, scale = normalize(x_ref[0].astype(F32))
    on_first_slot("wait", copies)
    grad_normed = None
    for block in range(3):
        part = nt(proj_ref[0, :, block * D : (block + 1) * D], wide(weights_ref, 0, block))
        grad_normed = part if grad_normed is None else grad_normed + part
    grad, grad_gain, grad_shift = norm_backward(grad_normed, unit, scale, norm_ref[0:1])
    grad_ref[0] = (grad_out_ref[0] + grad).astype(BF)
    norm_grad_rows(norm_grad_ref, [grad_gain, grad_shift])


def per_slot(*shape):
    return pl.BlockSpec((1,) + shape, lambda slot: (slot,) + (0,) * len(shape))


def whole_block(*shape):
    return pl.BlockSpec(shape, lambda slot: (0,) * len(shape))


def scalars():
    return pl.BlockSpec(memory_space=pltpu.SMEM)


def in_place():
    return pl.BlockSpec(memory_space=pl.ANY)


def in_vmem():
    return pl.BlockSpec(memory_space=pltpu.VMEM)


class Order:
    def __init__(self):
        self.token = ()

    def call(self, kernel, name, steps, ins, outs, scratch, args, megabytes, us):
        leaf = lambda out: isinstance(out[0], pl.BlockSpec)
        shaped = lambda out: pltpu.HBM(*out[1:3]) if out[3:] else jax.ShapeDtypeStruct(*out[1:])
        specs = [out[0] if leaf(out) else tuple(part[0] for part in out) for out in outs]
        shapes = [shaped(out) if leaf(out) else tuple(shaped(part) for part in out) for out in outs]
        place = len(ins) + len(outs)

        def body(before, *refs):
            refs[place][...] = jnp.zeros((8, 128), F32)
            kernel(*refs[:place], *refs[place + 1 :])

        *results, token = pl.pallas_call(
            body,
            name=name,
            grid=(steps,),
            in_specs=[tuple(in_place() for _ in self.token)] + ins,
            out_specs=specs + [whole_block(8, 128)],
            out_shape=shapes + [jax.ShapeDtypeStruct((8, 128), F32)],
            scratch_shapes=scratch,
            cost_estimate=pl.CostEstimate(flops=int(COST * us * 1.15e9), bytes_accessed=1 << 16, transcendentals=0),
            compiler_params=pltpu.CompilerParams(
                vmem_limit_bytes=megabytes << 20, dimension_semantics=("arbitrary",)
            ),
        )(self.token, *args)
        self.token = (token,)
        return results


def slot_array(slots, width, dtype, to_hbm=False):
    return (per_slot(SLOT, width), (slots, SLOT, width), dtype) + (("hbm",) if to_hbm else ())


def stay(*arrays):
    return tuple(pltpu.with_memory_space_constraint(array, pltpu.HBM) for array in arrays)


def grad_group(rows, parted):
    shape, count = ((SHARDS // 2, rows, D), 2) if parted else ((SHARDS // 2, 2, rows, D), 1)
    once = pl.BlockSpec(shape, lambda slot: (0,) * len(shape), pipeline_mode=pl.Buffered(1))
    return ((once, shape, BF),) * count


NORM_GRADS = (whole_block(8, D), (8, D), F32)


def weight_scratch(rows):
    return [pltpu.VMEM((SHARDS // 2, 2, rows, D), BF), pltpu.SemaphoreType.DMA((4,))]


def bound(kernel, weights, **options):
    return functools.partial(kernel, place=weights.place, half=weights.half, **options)


def held(weights):
    return tuple(in_place() for _ in weights.arrays)


def project(order, me, rows, weights, norms, name):
    slots = rows.shape[0]
    return order.call(
        bound(project_kernel, weights),
        name,
        slots,
        [scalars(), per_slot(SLOT, D), held(weights), whole_block(*norms.shape)],
        [slot_array(slots, 3 * D, BF)],
        weight_scratch(SELF_OUT - SELF_IN),
        (me, *stay(rows), stay(*weights.arrays), norms),
        12,
        5,
    )[0]


def self_attend(order, kinds, lengths, me, rows, qkv, weights, causal, name):
    slots = rows.shape[0]
    return order.call(
        bound(self_attend_kernel, weights, causal=causal),
        name,
        slots,
        [scalars(), scalars(), scalars(), per_slot(SLOT, D), per_slot(SLOT, 3 * D), held(weights)],
        [slot_array(slots, D, F32, True)] + [slot_array(slots, D, BF, True)] * 2 + [slot_array(slots, 128, BF, True)],
        weight_scratch(SELF_ROWS - SELF_OUT),
        (kinds, lengths, me, *stay(rows), qkv, stay(*weights.arrays)),
        20,
        10,
    )


def ffn_forward(order, me, rows, weights, norms):
    slots = rows.shape[0]
    return order.call(
        bound(ffn_forward_kernel, weights),
        "ffn_forward",
        slots,
        [scalars(), per_slot(SLOT, D), held(weights), whole_block(*norms.shape)],
        [slot_array(slots, D, BF, True), slot_array(slots, FF, BF, True), slot_array(slots, FF, BF, True)],
        weight_scratch(FFN_ROWS),
        (me, *stay(rows), stay(*weights.arrays), norms),
        24,
        16,
    )


def ffn_backward(order, me, grad_out, rows, active, slope, weights, norms, parted):
    slots = rows.shape[0]
    return order.call(
        bound(ffn_backward_kernel, weights),
        "ffn_backward",
        slots,
        [
            scalars(),
            per_slot(SLOT, D),
            per_slot(SLOT, D),
            per_slot(SLOT, FF),
            per_slot(SLOT, FF),
            held(weights),
            whole_block(*norms.shape),
        ],
        [slot_array(slots, D, F32), grad_group(FFN_ROWS, parted), NORM_GRADS],
        weight_scratch(FFN_ROWS) + [pltpu.VMEM((2, BLOCKS, D, D), F32)],
        (me, *stay(grad_out, rows, active, slope), stay(*weights.arrays), norms),
        38,
        22,
    )


def attend_backward(order, kinds, lengths, me, grad_out, q, kv, kept, weights, causal, start, key_at, name):
    slots = grad_out.shape[0]
    return order.call(
        bound(attend_back_kernel, weights, causal=causal, start=start, key_at=key_at),
        name,
        slots,
        [scalars(), scalars(), scalars(), per_slot(SLOT, D)]
        + [per_slot(SLOT, part.shape[-1]) for part in (q, kv)]
        + [per_slot(SLOT, D), per_slot(SLOT, D), per_slot(SLOT, 128), held(weights)],
        [slot_array(slots, 3 * D, BF)],
        weight_scratch(16) + [pltpu.VMEM((1, SLOT, D), BF)],
        (kinds, lengths, me, grad_out, *stay(q, kv, *kept), stay(*weights.arrays)),
        26,
        16,
    )[0]


def upper(order, kinds, lengths, me, rows, memory, enc_cotangent, dec_cotangent, w_cross, w_ff, norms, parted):
    slots = rows.shape[0]
    return order.call(
        functools.partial(
            upper_kernel, cross_place=w_cross.place, cross_half=w_cross.half, ff_place=w_ff.place, ff_half=w_ff.half
        ),
        "upper_decoder",
        slots,
        [scalars(), scalars(), scalars()]
        + [per_slot(SLOT, D)] * 4
        + [held(w_cross), held(w_ff), whole_block(*norms.shape)],
        [
            slot_array(slots, D, BF, True),
            slot_array(slots, D, F32),
            slot_array(slots, D, F32, True),
            grad_group(FFN_ROWS, parted),
            grad_group(CROSS_ROWS, parted),
            NORM_GRADS,
        ],
        weight_scratch(CROSS_ROWS)
        + weight_scratch(FFN_ROWS)
        + [
            pltpu.VMEM((1, SLOT, 3 * D), BF),
            pltpu.VMEM((SLOT, D), F32),
            pltpu.VMEM((1, SLOT, D), BF),
            pltpu.VMEM((3, SLOT, D), BF),
            pltpu.VMEM((BLOCKS, SLOT, D), BF),
            pltpu.VMEM((BLOCKS, SLOT, D), BF),
            pltpu.VMEM((SLOT, D), F32),
            pltpu.VMEM((2, BLOCKS, D, D), F32),
            pltpu.VMEM((4, D, D), F32),
        ],
        (
            kinds,
            lengths,
            me,
            *stay(rows, memory, enc_cotangent, dec_cotangent),
            stay(*w_cross.arrays),
            stay(*w_ff.arrays),
            norms,
        ),
        UPPER_MB,
        60,
    )


def self_weights(order, me, grad_out, rows, context, proj, norms, parted, name):
    slots = rows.shape[0]
    return order.call(
        self_weight_kernel,
        name,
        slots,
        [scalars()] + [per_slot(SLOT, D)] * 3 + [per_slot(SLOT, 3 * D), whole_block(*norms.shape)],
        [grad_group(SELF_ROWS, parted)],
        [pltpu.VMEM((4, D, D), F32)],
        (me, grad_out, *stay(rows, context), proj, norms),
        20,
        8,
    )[0]


def self_rows(order, me, grad_out, rows, proj, weights, norms, name):
    slots = rows.shape[0]
    return order.call(
        bound(self_rows_kernel, weights),
        name,
        slots,
        [scalars(), per_slot(SLOT, D), per_slot(SLOT, D), per_slot(SLOT, 3 * D), held(weights), whole_block(*norms.shape)],
        [slot_array(slots, D, BF), NORM_GRADS],
        weight_scratch(SELF_OUT - SELF_IN),
        (me, *stay(grad_out, rows), proj, stay(*weights.arrays), norms),
        16,
        7,
    )


def axis_sizes(mesh):
    dp, fsdp = mesh.shape["dp"], mesh.shape["fsdp"]
    core = 2 if fsdp % 2 == 0 else 1
    side = math.isqrt(dp)
    first, second = (side, side) if side * side == dp else (dp, 1)
    return (first, second, fsdp // core, core)


AXES = ("dp", "fsdp")
CUBE = (2, 2, 4, 2)
A_BIT, B_BIT, HIGH_BIT, LOW_BIT, CORE_BIT = 16, 8, 4, 2, 1


def swapped(values, bit):
    return lax.ppermute(values, AXES, [(device, device ^ bit) for device in range(SHARDS)])


def moved(values, sizes, axis, shift):
    stride = math.prod(sizes[axis + 1 :])
    pairs = []
    for device in range(math.prod(sizes)):
        place = device // stride % sizes[axis]
        pairs.append((device, device + ((place + shift) % sizes[axis] - place) * stride))
    return lax.ppermute(values, AXES, pairs)


def sum_everywhere(values, sizes):
    for axis in (3, 1, 0, 2):
        total = values
        for shift in range(1, sizes[axis]):
            total = total + moved(values, sizes, axis, shift)
        values = total
    return values


def packed(flat, rows, columns, devices):
    part = flat.reshape(rows // devices, columns // D, D)
    return jnp.swapaxes(part, 0, 1).reshape(-1, D)


def unpacked(part, rows, columns, devices):
    return jnp.swapaxes(part.reshape(columns // D, rows // devices, D), 0, 1).reshape(-1)


SELF_SHAPES = ((D, 3 * D), (D, D))
FFN_SHAPES = ((D, FF), (FF, D))
CROSS_SHAPES = ((D, D), (D, 2 * D), (D, D))


def rows_of(shapes, devices=SHARDS):
    return sum(rows * columns for rows, columns in shapes) // D // devices


def rows_in(groups):
    return sum(rows_of(shapes) for shapes in groups)


def join_copy_kernel(me_ref, sources, results, sems, *, plan):
    copies = []
    for result, (source, _, bit, axis) in zip(results, plan):
        for other, ref in enumerate(sources[source]):
            place = me_ref[bit] if other == 0 else 1 - me_ref[bit]
            target = result.at[place] if axis == 0 else result.at[:, place]
            copies.append(pltpu.make_async_copy(ref, target, sems.at[len(copies)]))
    for copy in copies:
        copy.start()
    for copy in copies:
        copy.wait()


def join_kernel(me_ref, sources, results, *, plan):
    for result, (source, rows, bit, axis) in zip(results, plan):
        for other, ref in enumerate(sources[source]):
            place = me_ref[bit] if other == 0 else 1 - me_ref[bit]
            if axis == 0:
                result[place] = ref[...]
            else:
                for lead in range(2):
                    result[lead, place] = ref[lead] if rows is None else ref[lead, rows]


def join(order, me, name, sources, plan, to_hbm=False):
    outs = []
    for source, rows, _, axis in plan:
        shape = sources[source][0].shape
        count = shape[-2] if rows is None else rows.stop - rows.start
        shape = (2, *shape[:-2], count, D) if axis == 0 else (shape[0], 2, *shape[1:-2], count, D)
        outs.append((in_place(), shape, BF, "hbm") if to_hbm else (in_vmem(), shape, BF))
    return order.call(
        functools.partial(join_copy_kernel if to_hbm else join_kernel, plan=plan),
        name,
        1,
        [scalars(), [(in_vmem(), in_vmem())] * len(sources)],
        [tuple(outs)],
        [pltpu.SemaphoreType.DMA((2 * len(plan),))] if to_hbm else [],
        (me, sources),
        20,
        1,
    )[0]


def pack_kernel(me_ref, flats, extra, out_ref, *scratch, plan):
    for flat, wide_ref, (rows, blocks, places) in zip(flats, scratch, plan):
        wide_ref[...] = flat[...].astype(F32)
        for block, place in enumerate(places):
            for chunk in range(4):
                part = wide_ref[pl.ds(4 * block + chunk, rows, stride=4 * blocks), :]
                out_ref[place : place + rows, 128 * chunk : 128 * chunk + 128] = part.astype(BF)
    if extra:
        place = out_ref.shape[0] - 16
        out_ref[place:, :] = jnp.broadcast_to(extra[0][...], (16, D))


def pack_groups(order, me, name, groups, extra):
    counts = [rows_of([shape for _, shape in group]) for group in groups]
    total = sum(counts)
    flats, plan, scratch, before = [], [], [], 0
    for group, count in zip(groups, counts):
        first = 0
        for flat, (rows, columns) in group:
            rows, blocks = rows // SHARDS, columns // D
            places = []
            for block in range(blocks):
                at = first + block * rows
                places.append(before + at if at < count // 2 else total // 2 + before + at - count // 2)
            first += rows * blocks
            flats.append(flat.reshape(-1, 128))
            plan.append((rows, blocks, tuple(places)))
            scratch.append(pltpu.VMEM((rows * blocks * 4, 128), F32))
        before += count // 2
    rows = total + (0 if extra is None else 16)
    return order.call(
        functools.partial(pack_kernel, plan=plan),
        name + "_pack",
        1,
        [scalars(), tuple(in_vmem() for _ in flats), () if extra is None else (in_vmem(),)],
        [(in_vmem(), (rows, D), BF)],
        scratch,
        (me, tuple(flats), () if extra is None else (extra,)),
        20,
        1,
    )[0]


def gather_cube(order, me, name, groups, spans, extra, results):
    halves_of = [rows_of([shape for _, shape in group]) // 2 for group in groups]
    count = sum(halves_of)
    values = pack_groups(order, me, name, groups, extra)
    total = values.shape[0]
    yield
    got = swapped(values, HIGH_BIT)
    yield
    (values,) = join(order, me, name + "_join_1", [(values, got)], [(0, None, 2, 0)])
    got = swapped(values, LOW_BIT)
    yield
    plan, members, place = [], [], 0
    for span in spans:
        members.append([halves_of.pop(0) for _ in range(span)])
        end = place + sum(members[-1])
        plan.append((0, slice(place, end), 3, 1))
        plan.append((0, slice(count + place, total if end == count else count + end), 3, 1))
        place = end
    parts = join(order, me, name + "_join_2", [(values, got)], plan)
    for number, held_halves in enumerate(members):
        last = extra is not None and number == len(members) - 1
        results.append(
            Exchange(
                lambda kept, number=number, held_halves=held_halves, last=last: gather_rest(
                    order, me, f"{name}_{number}", parts[2 * number], parts[2 * number + 1], held_halves, last, kept
                )
            )
        )
    yield


def gather_rest(order, me, name, one, two, halves_of, extra, results):
    got = swapped(one, B_BIT), swapped(two, A_BIT)
    yield
    one, two = join(
        order, me, name + "_join_3", [(one, got[0]), (two, got[1])], [(0, None, 1, 0), (1, None, 0, 0)]
    )
    got = swapped(one, A_BIT), swapped(two, B_BIT)
    yield
    one, two = join(
        order, me, name + "_join_4", [(one, got[0]), (two, got[1])], [(0, None, 0, 0), (1, None, 1, 1)], True
    )
    got = swapped(one, CORE_BIT), swapped(two, CORE_BIT)
    arrays = tuple(part.reshape(SHARDS // 2, -1, D) for part in (one, got[0], two, got[1]))
    place = 0
    for half in halves_of:
        results.append(Weights(arrays, place, half))
        place += half
    if extra:
        own, other = arrays[2][:, place], arrays[3][:, place]
        lines = jnp.where(me[4] == 0, jnp.stack([own, other], 1), jnp.stack([other, own], 1))
        results.append(lines.reshape(SHARDS, D))
    yield


def gather_plain(groups, spans, extra, devices, results):
    if devices == SHARDS:
        parts = [packed(flat, *shape, SHARDS) for group in groups for flat, shape in group]
        whole = lax.all_gather(jnp.concatenate(parts, 0), AXES, axis=0)
    else:
        parts = []
        for flat, shape in [pair for group in groups for pair in group]:
            full = lax.all_gather(flat, AXES, axis=0, tiled=True)
            full = full.reshape(SHARDS, shape[0] // SHARDS, shape[1] // D, D)
            parts.append(jnp.swapaxes(full, 1, 2).reshape(SHARDS, -1, D))
        whole = jnp.concatenate(parts, 1)
    whole = whole.reshape(SHARDS // 2, 2, -1, D)
    place, left = 0, list(groups)
    for span in spans:
        results.append(Exchange())
        for _ in range(span):
            count = rows_of([shape for _, shape in left.pop(0)])
            results[-1].results.append(Weights((whole,), place, count // 2))
            place += count
    if extra is not None:
        results[-1].results.append(lax.all_gather(extra[0], AXES, axis=0))


def add_kernel(me_ref, parts, result):
    result[...] = functools.reduce(jnp.add, [part[...] for part in parts])


def sum_cube(order, me, values, results):
    for bits in ((CORE_BIT,), (B_BIT, A_BIT, A_BIT | B_BIT), (LOW_BIT, HIGH_BIT, HIGH_BIT | LOW_BIT)):
        parts = (values, *(swapped(values, bit) for bit in bits))
        yield
        values = order.call(
            add_kernel,
            "small_sum",
            1,
            [scalars(), tuple(in_vmem() for _ in parts)],
            [(in_vmem(), values.shape, F32)],
            [],
            (me, parts),
            8,
            1,
        )[0]
    results.append(values)
    yield


def first_sum_kernel(me_ref, keeps, gots, send_one, keep_one, send_two, keep_two):
    a, b = me_ref[0], me_ref[1]
    place = 0
    for keep, got in zip(keeps, gots):
        half = keep.shape[3] // 2
        low, high, here = slice(0, half), slice(half, 2 * half), slice(place, place + half)
        for other in range(2):
            for ref, pick in ((send_one, 1 - b), (keep_one, b)):
                ref[other, :, here] = keep[other, pick, :, low] + got[other, pick, :, low]
            for ref, pick in ((send_two, 1 - a), (keep_two, a)):
                ref[other, :, here] = keep[pick, other, :, high] + got[pick, other, :, high]
        place += half


def second_sum_kernel(me_ref, keep_one, got_one, keep_two, got_two, send_a, kept_a, send_b, kept_b):
    a, b = me_ref[0], me_ref[1]
    for ref, pick in ((send_a, 1 - a), (kept_a, a)):
        ref[...] = keep_one[pick] + got_one[pick]
    for ref, pick in ((send_b, 1 - b), (kept_b, b)):
        ref[...] = keep_two[pick] + got_two[pick]


def third_sum_kernel(me_ref, keep_one, got_one, keep_two, got_two, send, keep):
    z = me_ref[3]
    half = keep_one.shape[2]
    for high in range(2):
        for ref, pick in ((send, 1 - z), (keep, z)):
            ref[high, :half] = keep_one[high, pick] + got_one[high, pick]
            ref[high, half:] = keep_two[high, pick] + got_two[high, pick]


def fourth_sum_kernel(me_ref, keep, got, send, kept):
    z = me_ref[2]
    for ref, pick in ((send, 1 - z), (kept, z)):
        ref[...] = keep[pick] + got[pick]


def scatter_cube(order, me, name, groups, results):
    got = [swapped(pair[1], CORE_BIT) for pair, _ in groups]
    yield
    keeps = tuple(pair[0].reshape(2, 2, 4, -1, D) for pair, _ in groups)
    got = tuple(part.reshape(2, 2, 4, -1, D) for part in got)
    half = sum(rows_of(shapes) for _, shapes in groups) // 2

    def call(kernel, number, shapes, *args):
        ins = [tuple(in_vmem() for _ in arg) if isinstance(arg, tuple) else in_vmem() for arg in args]
        outs = [(in_vmem(), shape, BF) for shape in shapes]
        return order.call(kernel, f"{name}_sum_{number}", 1, [scalars()] + ins, outs, [], (me, *args), 20, 1)

    send_one, keep_one, send_two, keep_two = call(first_sum_kernel, 1, [(2, 4, half, D)] * 4, keeps, got)
    got = swapped(send_one, B_BIT), swapped(send_two, A_BIT)
    yield
    send_one, keep_one, send_two, keep_two = call(
        second_sum_kernel, 2, [(4, half, D)] * 4, keep_one, got[0], keep_two, got[1]
    )
    got = swapped(send_one, A_BIT), swapped(send_two, B_BIT)
    yield
    views = [part.reshape(2, 2, half, D) for part in (keep_one, got[0], keep_two, got[1])]
    send, keep = call(third_sum_kernel, 3, [(2, 2 * half, D)] * 2, *views)
    got = swapped(send, LOW_BIT)
    yield
    send, keep = call(fourth_sum_kernel, 4, [(2 * half, D)] * 2, keep, got)
    got = swapped(send, HIGH_BIT)
    yield
    plan, outs, place = [], [], 0
    for _, shapes in groups:
        count, first = rows_of(shapes), 0
        for rows, columns in shapes:
            rows, blocks = rows // SHARDS, columns // D
            places = []
            for block in range(blocks):
                at = first + block * rows
                places.append(place + at if at < count // 2 else half + place + at - count // 2)
            first += rows * blocks
            plan.append((rows, blocks, tuple(places)))
            shape = (rows * blocks * 4, 128)
            outs.append((whole_block(*shape), shape, F32))
        place += count // 2
    flat = order.call(
        functools.partial(finish_kernel, plan=plan),
        name + "_finish",
        1,
        [scalars(), in_vmem(), in_vmem()],
        [tuple(outs)],
        [],
        (me, keep, got),
        20,
        1,
    )[0]
    results.extend(part.reshape(-1) for part in flat)
    yield


def finish_kernel(me_ref, keep, got, outs, *, plan):
    for out, (rows, blocks, places) in zip(outs, plan):
        for block, place in enumerate(places):
            part = keep[place : place + rows, :].astype(F32) + got[place : place + rows, :].astype(F32)
            for chunk in range(4):
                out[pl.ds(4 * block + chunk, rows, stride=4 * blocks), :] = part[:, 128 * chunk : 128 * chunk + 128]


def unpack_group(rows, shapes):
    results, first = [], 0
    for shape in shapes:
        count = rows_of((shape,))
        results.append(unpacked(rows[first : first + count], *shape, SHARDS))
        first += count
    return results


def scatter_plain(grads, shapes, devices):
    if devices == SHARDS:
        own = lax.psum_scatter(grads.reshape(-1, D), AXES, scatter_dimension=0, tiled=True)
        return unpack_group(own.astype(F32), shapes)
    grads = grads.reshape(SHARDS, -1, D)
    results, first = [], 0
    for rows, columns in shapes:
        count = rows_of(((rows, columns),))
        part = grads[:, first : first + count].reshape(SHARDS, columns // D, rows // SHARDS, D)
        flat = jnp.swapaxes(part, 1, 2).reshape(devices, -1)
        results.append(lax.psum_scatter(flat, AXES, scatter_dimension=0, tiled=True).reshape(-1).astype(F32))
        first += count
    return results


class Exchange:
    def __init__(self, steps=None):
        self.results = []
        self.steps = None if steps is None else steps(self.results)

    def part(self, number):
        return self.results[number]

    def go(self, count=1):
        if self.steps is not None:
            for _ in range(count):
                next(self.steps)


def count_live(kinds, lengths, ids):
    positions = jnp.arange(SLOT, dtype=jnp.int32)[None, :]
    size = jnp.left_shift(jnp.int32(SLOT // 4), kinds)[:, None]
    sequence = positions // size
    limit = jnp.zeros_like(sequence)
    for entry in range(4):
        limit = jnp.where(sequence == entry, lengths[:, entry : entry + 1], limit)
    live = positions % size < limit
    hits = (ids.reshape(-1)[:, None] == jnp.arange(VOCAB, dtype=jnp.int32)[None, :]) & live.reshape(-1)[:, None]
    return jnp.sum(hits.astype(F32), 0)


def local(
    sizes,
    enc_in,
    dec_in,
    bucket,
    enc_lengths,
    dec_lengths,
    pred_ids,
    running_counts,
    enc_attn_in,
    enc_attn_out,
    enc_ff_in,
    enc_ff_out,
    enc_norms,
    dec_self_in,
    dec_self_out,
    dec_cross_q,
    dec_cross_kv,
    dec_cross_out,
    dec_ff_in,
    dec_ff_out,
    dec_norms,
    enc_cotangent,
    dec_cotangent,
):
    devices = math.prod(sizes)
    cube = sizes == CUBE
    index = lax.axis_index("dp") * lax.axis_size("fsdp") + lax.axis_index("fsdp")
    if cube:
        me = jnp.stack([index >> 4 & 1, index >> 3 & 1, index >> 2 & 1, index >> 1 & 1, index & 1]).astype(jnp.int32)
    else:
        me = jnp.zeros((5,), jnp.int32)

    order = Order()

    def gather(name, groups, spans, extra=None):
        if cube:
            return Exchange(lambda results: gather_cube(order, me, name, groups, spans, extra, results))
        exchange = Exchange()
        gather_plain(groups, spans, extra, devices, exchange.results)
        return exchange

    def scatter(name, *groups):
        if cube and all(len(grads) == 2 for grads, _ in groups):
            return Exchange(lambda results: scatter_cube(order, me, name, groups, results))
        exchange = Exchange()
        for (grads,), shapes in groups:
            exchange.results.extend(scatter_plain(grads, shapes, devices))
        return exchange

    enc_count, dec_count = enc_norms.shape[0], dec_norms.shape[0]
    both = jnp.concatenate([enc_norms, dec_norms])
    norm_part = jnp.pad(both[None, :], ((0, 0), (0, D - both.shape[0])))
    enc_self_group = list(zip((enc_attn_in, enc_attn_out), SELF_SHAPES))
    dec_self_group = list(zip((dec_self_in, dec_self_out), SELF_SHAPES))
    enc_ff_group = list(zip((enc_ff_in, enc_ff_out), FFN_SHAPES))
    cross_group = list(zip((dec_cross_q, dec_cross_kv, dec_cross_out), CROSS_SHAPES))
    dec_ff_group = list(zip((dec_ff_in, dec_ff_out), FFN_SHAPES))
    first = gather("self", [dec_self_group, enc_self_group], [1, 1], norm_part)
    rest = gather("rest", [enc_ff_group, cross_group, dec_ff_group], [1, 2])
    first.go(2)
    rest.go()
    first.go(2)
    dec_chain, enc_chain = first.part(0), first.part(1)
    enc_chain.go()
    dec_chain.go()
    rest.go()
    enc_chain.go()
    dec_chain.go()
    enc_chain.go()
    rest.go()
    dec_chain.go()
    enc_self_w, norm_lines = enc_chain.results
    enc_norm = norm_lines[:, :enc_count].reshape(4, D).astype(F32)
    dec_norm = norm_lines[:, enc_count : enc_count + dec_count].reshape(6, D).astype(F32)

    enc_qkv = project(order, me, enc_in, enc_self_w, enc_norm, "enc_project")
    attended, *enc_kept = self_attend(order, bucket, enc_lengths, me, enc_in, enc_qkv, enc_self_w, False, "enc_attend")
    rest.go()
    ffn_chain, late_chain = rest.part(0), rest.part(1)
    ffn_chain.go()
    late_chain.go()
    (dec_self_w,) = dec_chain.results
    dec_qkv = project(order, me, dec_in, dec_self_w, dec_norm, "dec_project")
    ffn_chain.go()
    first_out, *dec_kept = self_attend(order, bucket, dec_lengths, me, dec_in, dec_qkv, dec_self_w, True, "dec_attend")
    late_chain.go()
    ffn_chain.go()
    (enc_ff_w,) = ffn_chain.results
    memory, active, slope = ffn_forward(order, me, attended, enc_ff_w, enc_norm)
    late_chain.go()
    cross_w, dec_ff_w = late_chain.results
    decoded, grad_first, grad_memory, dec_ff_grads, cross_grads, upper_norm_g = upper(
        order,
        bucket,
        enc_lengths,
        me,
        first_out,
        memory,
        enc_cotangent,
        dec_cotangent,
        cross_w,
        dec_ff_w,
        dec_norm,
        cube,
    )
    fifth = scatter("dec", (dec_ff_grads, FFN_SHAPES), (cross_grads, CROSS_SHAPES))
    fifth.go()
    grad_attended, enc_ff_grads, enc_ffn_norm_g = ffn_backward(
        order, me, grad_memory, attended, active, slope, enc_ff_w, enc_norm, cube
    )
    fifth.go()
    enc_proj = attend_backward(
        order,
        bucket,
        enc_lengths,
        me,
        grad_attended,
        enc_qkv,
        enc_qkv,
        enc_kept,
        enc_self_w,
        False,
        SELF_OUT,
        D,
        "enc_attend_back",
    )
    fifth.go()
    enc_self_grads = self_weights(
        order, me, grad_attended, enc_in, enc_kept[0], enc_proj, enc_norm, cube, "enc_self_weights"
    )
    sixth = scatter("enc", (enc_ff_grads, FFN_SHAPES), (enc_self_grads, SELF_SHAPES))
    sixth.go()
    dec_proj = attend_backward(
        order,
        bucket,
        dec_lengths,
        me,
        grad_first,
        dec_qkv,
        dec_qkv,
        dec_kept,
        dec_self_w,
        True,
        SELF_OUT,
        D,
        "dec_attend_back",
    )
    fifth.go()
    sixth.go()
    dec_self_grads = self_weights(
        order, me, grad_first, dec_in, dec_kept[0], dec_proj, dec_norm, cube, "dec_self_weights"
    )
    seventh = scatter("self", (dec_self_grads, SELF_SHAPES))
    seventh.go()
    fifth.go()
    grad_enc_in, enc_self_norm_g = self_rows(
        order, me, grad_attended, enc_in, enc_proj, enc_self_w, enc_norm, "enc_self_rows"
    )
    seventh.go()
    sixth.go()
    grad_dec_in, dec_self_norm_g = self_rows(order, me, grad_first, dec_in, dec_proj, dec_self_w, dec_norm, "dec_self_rows")
    counted = jnp.pad(count_live(bucket, dec_lengths, pred_ids), (0, 2 * D - VOCAB)).reshape(2, D)
    small = jnp.concatenate(
        [enc_self_norm_g[:2], enc_ffn_norm_g[:2], dec_self_norm_g[:2], upper_norm_g[:4], counted, jnp.zeros((4, D), F32)],
        0,
    )
    if cube:
        summed = Exchange(lambda results: sum_cube(order, me, small, results))
        summed.go()
        seventh.go()
        sixth.go()
        summed.go()
        seventh.go()
        sixth.go()
        summed.go()
        seventh.go()
        fifth.go()
        sixth.go()
        summed.go()
        seventh.go()
        (small,) = summed.results
    else:
        small = sum_everywhere(small, sizes)
    dec_ff_in_g, dec_ff_out_g, cross_q_g, cross_kv_g, cross_out_g = fifth.results
    enc_ff_in_g, enc_ff_out_g, enc_attn_in_g, enc_attn_out_g = sixth.results
    dec_self_in_g, dec_self_out_g = seventh.results

    enc_norm_own = lax.dynamic_slice(small[:4].reshape(-1), (index * enc_count,), (enc_count,))
    dec_norm_own = lax.dynamic_slice(small[4:10].reshape(-1), (index * dec_count,), (dec_count,))
    counts = running_counts + small[10:12].reshape(-1)[:VOCAB].astype(jnp.int32)
    return (
        memory,
        decoded,
        grad_enc_in,
        grad_dec_in,
        enc_attn_in_g,
        enc_attn_out_g,
        enc_ff_in_g,
        enc_ff_out_g,
        enc_norm_own,
        dec_self_in_g,
        dec_self_out_g,
        cross_q_g,
        cross_kv_g,
        cross_out_g,
        dec_ff_in_g,
        dec_ff_out_g,
        dec_norm_own,
        counts,
    )


def solution(mesh):
    rows = P(AXES, None, None)
    pair = P(AXES, None)
    flat = P(AXES)
    return jax.shard_map(
        functools.partial(local, axis_sizes(mesh)),
        mesh=mesh,
        in_specs=(rows, rows, flat, pair, pair, pair, P()) + (flat,) * 13 + (rows, rows),
        out_specs=(rows,) * 4 + (flat,) * 13 + (P(),),
        check_vma=False,
    )
```

```python
import functools
import math
import jax
import jax.numpy as jnp
from jax import lax
from jax.experimental import pallas as pl
from jax.experimental.pallas import tpu as pltpu
from jax.sharding import PartitionSpec as P

D = 512
HEAD = 64
FF = 2048
VOCAB = 523
SLOT = 512
SHARDS = 32
BLOCKS = FF // D
EPS = 1e-05
PAIR = 2 * HEAD
PAIRS = D // PAIR
GROUP = 16
MASKED = -(2.0**30)
COST = 0.5
UPPER_MB = 56
BF = jnp.bfloat16
F32 = jnp.float32

SELF_ROWS, SELF_IN, SELF_OUT = 64, 0, 48
FFN_ROWS, FFN_IN, FFN_OUT = 128, 0, 64
CROSS_ROWS, CROSS_Q, CROSS_KV, CROSS_OUT = 64, 0, 16, 48


def nn(left, right):
    return lax.dot_general(left, right, (((1,), (0,)), ((), ())), preferred_element_type=F32)


def nt(left, right):
    return lax.dot_general(left, right, (((1,), (1,)), ((), ())), preferred_element_type=F32)


def wide(ref, start, block):
    first = start + 16 * block
    return ref[:, :, first : first + 16, :].reshape(D, D)


def tall(ref, start, block):
    return ref[4 * block : 4 * block + 4, :, start : start + 64, :].reshape(D, D)


def put_shards(core, refs, lead, rows, shards):
    if len(refs) == 1:
        refs[0][lead, :, rows, :] = shards.astype(BF)
        return
    refs[0][lead, rows, :] = jnp.where(core == 0, shards[:, 0], shards[:, 1]).astype(BF)
    piece = refs[1].shape[1]
    start = rows.start % piece
    refs[1 + rows.start // piece][lead, start : start + rows.stop - rows.start, :] = jnp.where(
        core == 0, shards[:, 1], shards[:, 0]
    ).astype(BF)


def put_wide(core, refs, start, block, value):
    rows = slice(start + 16 * block, start + 16 * block + 16)
    put_shards(core, refs, slice(0, SHARDS // 2), rows, value.reshape(SHARDS // 2, 2, 16, D))


def put_tall(core, refs, start, block, value):
    put_shards(core, refs, slice(4 * block, 4 * block + 4), slice(start, start + 64), value.reshape(4, 2, 64, D))


class Weights:
    def __init__(self, arrays, place, half):
        self.arrays = arrays
        self.place = place
        self.half = half


def weight_copies(pieces, place, half, core, ref, sems, low, high):
    if len(pieces) == 1:
        return [pltpu.make_async_copy(pieces[0].at[:, :, place + low : place + high, :], ref, sems.at[0])]
    copies = []
    for number in range(2):
        first, last = max(low, number * half), min(high, (number + 1) * half)
        if first < last:
            source = slice(place + first - number * half, place + last - number * half)
            for other in range(2):
                copies.append(
                    pltpu.make_async_copy(
                        pieces[2 * number + other].at[:, source, :],
                        ref.at[:, core if other == 0 else 1 - core, first - low : last - low, :],
                        sems.at[2 * number + other],
                    )
                )
    return copies


def on_first_slot(action, copies):
    @pl.when(pl.program_id(0) == 0)
    def _():
        for copy in copies:
            getattr(copy, action)()


def norm_grad_rows(ref, gains_and_shifts):
    rows = jnp.concatenate(gains_and_shifts + [jnp.zeros((8 - len(gains_and_shifts), D), F32)], 0)
    add_up(ref, rows)


def last_slot():
    return pl.program_id(0) == pl.num_programs(0) - 1


def lanes_of(pair):
    return slice(pair * PAIR, (pair + 1) * PAIR)


def normalize(values):
    centered = values - jnp.mean(values, -1, keepdims=True)
    scale = lax.rsqrt(jnp.mean(centered * centered, -1, keepdims=True) + EPS)
    return centered * scale, scale


def norm_backward(grad_normed, unit, scale, gain):
    grad_unit = grad_normed * gain
    first = jnp.mean(grad_unit, -1, keepdims=True)
    second = jnp.mean(grad_unit * unit, -1, keepdims=True)
    grad_gain = jnp.sum(grad_normed * unit, 0, keepdims=True)
    grad_shift = jnp.sum(grad_normed, 0, keepdims=True)
    return scale * (grad_unit - first - unit * second), grad_gain, grad_shift


def gelu_both(hidden):
    size = jnp.abs(hidden)
    ratio = 1.0 / (1.0 + (0.3275911 / math.sqrt(2.0)) * size)
    bell = jnp.exp(-0.5 * hidden * hidden)
    series = 0.5 * 1.061405429
    for factor in (-1.453152027, 1.421413741, -0.284496736, 0.254829592):
        series = series * ratio + 0.5 * factor
    tail = series * ratio * bell
    share = jnp.where(hidden >= 0, 1.0 - tail, tail)
    return hidden * share, share + hidden * bell * (1.0 / math.sqrt(2.0 * math.pi))


def lane_index():
    return lax.broadcasted_iota(jnp.int32, (1, 128), 1)


def query_extra(kind):
    place = lax.broadcasted_iota(jnp.int32, (SLOT, 128), 0)
    lane = lax.broadcasted_iota(jnp.int32, (SLOT, 128), 1)
    return (lax.shift_right_logical(place, kind + 7) == lane).astype(F32).astype(BF)


def key_extra(kind, lengths):
    place = lax.broadcasted_iota(jnp.int32, (SLOT, 128), 0)
    lane = lax.broadcasted_iota(jnp.int32, (SLOT, 128), 1)
    size = lax.shift_left(jnp.int32(128), kind)
    within = place & (size - 1)
    limit = jnp.where(
        lane == 0, lengths[0], jnp.where(lane == 1, lengths[1], jnp.where(lane == 2, lengths[2], lengths[3]))
    )
    allowed = (lax.shift_right_logical(place, kind + 7) == lane) & (within < limit)
    return jnp.where(allowed | (lane >= 4), 0.0, MASKED).astype(BF)


def halves():
    lane = lane_index()
    return ((lane < HEAD).astype(F32).astype(BF), (lane >= HEAD).astype(F32).astype(BF))


def future(rows, columns, first):
    row = lax.broadcasted_iota(jnp.int32, (rows, columns), 0)
    column = lax.broadcasted_iota(jnp.int32, (rows, columns), 1) + first
    return row <= column


def pipelined(items, ahead, start, finish):
    waiting = []
    for number, item in enumerate(items):
        while len(waiting) <= ahead and number + len(waiting) < len(items):
            waiting.append(start(*items[number + len(waiting)]))
        finish(*item, waiting.pop(0))


def attend(query_of, key_of, value_of, store, kind, lengths, causal):
    step = 256
    query_lanes = query_extra(kind)
    key_lanes = key_extra(kind, lengths)
    ones = jnp.ones((HEAD, SLOT), BF)
    mask = halves()
    inputs, parts, sums = {}, {}, {}

    def seen(first):
        return first + step if causal else SLOT

    def start(pair, half, first):
        if pair not in inputs:
            queries = query_of(pair) * BF(HEAD**-0.5)
            inputs[pair] = (queries, jnp.concatenate([key_of(pair), key_lanes], 1), value_of(pair).T)
        queries, keys, _ = inputs[pair]
        own = jnp.concatenate([queries[first : first + step] * mask[half], query_lanes[first : first + step]], 1)
        return nt(keys[: seen(first)], own)

    def finish(pair, half, first, scores):
        values = inputs[pair][2]
        if causal:
            scores = jnp.where(future(seen(first), step, first), scores, MASKED)
        largest = jnp.max(scores, 0, keepdims=True)
        powers = jnp.exp(scores - largest).astype(BF)
        head_values = jnp.concatenate([values[:HEAD], ones] if half == 0 else [ones, values[HEAD:]], 0)
        context = nn(head_values[:, : seen(first)], powers)
        total = context[HEAD : HEAD + 1] if half == 0 else context[0:1]
        parts[pair, half, first] = (context[:HEAD] if half == 0 else context[HEAD:]) * (1.0 / total)
        sums[pair, half, first] = largest + jnp.log(total)
        if half == 1 and first == SLOT - step:
            rows = [jnp.concatenate([parts[pair, side, at] for at in range(0, SLOT, step)], 1) for side in range(2)]
            store(pair, jnp.concatenate(rows, 0).T)

    items = [(pair, half, first) for pair in range(PAIRS) for half in range(2) for first in range(0, SLOT, step)]
    pipelined(items, 4, start, finish)
    spread = [
        jnp.broadcast_to(jnp.concatenate([sums[pair, half, at] for at in range(0, SLOT, step)], 1), (GROUP, SLOT))
        for pair in range(PAIRS)
        for half in range(2)
    ]
    return split(jnp.concatenate(spread, 0).T, 4)


def split(values, first):
    lane = lane_index() % GROUP
    high = values.astype(BF).astype(F32)
    rest = values - high
    middle = rest.astype(BF).astype(F32)
    low = rest - middle
    terms = jnp.where(
        lane == first, high, jnp.where(lane == first + 1, middle, jnp.where(lane == first + 2, low, 0.0))
    )
    return (-terms).astype(BF)


def attend_back(query_of, key_of, value_of, grad_of, contexts, grads, store, logsums, kind, lengths, causal):
    step = 256 if causal else SLOT
    query_lanes = query_extra(kind) + logsums
    key_lanes = key_extra(kind, lengths)
    products = grads.astype(F32) * contexts
    high = products.astype(BF)
    low = (products - high.astype(F32)).astype(BF)
    source = lax.broadcasted_iota(jnp.int32, (D, 128), 0) // HEAD
    target = lax.broadcasted_iota(jnp.int32, (D, 128), 1) // GROUP
    picker = (source == target).astype(F32).astype(BF)
    inner_lanes = split(nn(high, picker) + nn(low, picker), 0)
    lane = lane_index()
    within, group = lane % GROUP, lane // GROUP
    mask = halves()
    inputs, heads, results = {}, {}, {}

    def seen(first):
        return first + step if causal else SLOT

    def start(pair, half, first):
        if pair not in inputs:
            inputs[pair] = (query_of(pair) * BF(HEAD**-0.5), key_of(pair), value_of(pair), grad_of(pair), key_of(pair).T)
        queries, keys, values, grad_context, _ = inputs[pair]
        if (pair, half) not in heads:
            head = 2 * pair + half
            sum_lanes = ((group == head) & (within >= 4) & (within < 7)).astype(F32).astype(BF)
            one_lanes = ((group == head) & (within < 3)).astype(F32).astype(BF)
            heads[pair, half] = (
                jnp.concatenate([keys, key_lanes + sum_lanes], 1),
                jnp.concatenate([queries * mask[half], query_lanes], 1),
                jnp.concatenate([values, jnp.broadcast_to(one_lanes, (SLOT, 128))], 1),
                jnp.concatenate([grad_context * mask[half], inner_lanes], 1),
            )
        left, right, value_left, grad_right = heads[pair, half]
        here = slice(first, first + step)
        return nt(left[: seen(first)], right[here]), nt(value_left[: seen(first)], grad_right[here])

    def finish(pair, half, first, products):
        scores, grad_weights = products
        queries, _, _, grad_context, keys_t = inputs[pair]
        if causal:
            scores = jnp.where(future(seen(first), step, first), scores, MASKED)
        weights = jnp.exp(scores)
        grad_scores = (weights * grad_weights).astype(BF)
        here = slice(first, first + step)
        for_queries = nn(keys_t[half * HEAD : half * HEAD + HEAD, : seen(first)], grad_scores)
        for_keys = nn(grad_scores, queries[here] * mask[half])
        for_values = nn(weights.astype(BF), grad_context[here] * mask[half])
        if seen(first) < SLOT:
            none = jnp.zeros((SLOT - seen(first), PAIR), F32)
            for_keys = jnp.concatenate([for_keys, none], 0)
            for_values = jnp.concatenate([for_values, none], 0)
        results[pair, half, first] = (for_queries, for_keys, for_values)
        if half == 1 and first == SLOT - step:
            places = range(0, SLOT, step)
            rows = [jnp.concatenate([results[pair, side, at][0] for at in places], 1) for side in range(2)]
            keys_sum, values_sum = (
                functools.reduce(jnp.add, [results[pair, side, at][number] for side in range(2) for at in places])
                for number in (1, 2)
            )
            store(
                pair,
                (jnp.concatenate(rows, 0) * HEAD**-0.5).T.astype(BF),
                keys_sum.astype(BF),
                values_sum.astype(BF),
            )

    items = [(pair, half, first) for pair in range(PAIRS) for half in range(2) for first in range(0, SLOT, step)]
    pipelined(items, 2 if causal else 1, start, finish)


def lengths_at(ref, slot):
    return [ref[slot, entry] for entry in range(4)]


def at(ref, start):
    return lambda pair: ref[0, :, start + pair * PAIR : start + (pair + 1) * PAIR]


def add_up(ref, value):
    ref[...] = jnp.where(pl.program_id(0) == 0, 0.0, ref[...]) + value


def project_kernel(me_ref, x_ref, w, norm_ref, qkv_ref, weights_ref, sems, *, place, half):
    copies = weight_copies(w, place, half, me_ref[4], weights_ref, sems, SELF_IN, SELF_OUT)
    on_first_slot("start", copies)
    unit, _ = normalize(x_ref[0].astype(F32))
    normed = (unit * norm_ref[0:1] + norm_ref[1:2]).astype(BF)
    on_first_slot("wait", copies)
    for block in range(3):
        qkv_ref[0, :, block * D : (block + 1) * D] = nn(normed, wide(weights_ref, 0, block)).astype(BF)


def keep_context(context_ref, rest_ref):
    def store(pair, context):
        high = context.astype(BF)
        context_ref[0, :, lanes_of(pair)] = high
        rest_ref[0, :, lanes_of(pair)] = (context - high.astype(F32)).astype(BF)

    return store


def self_attend_kernel(
    kind_ref,
    lengths_ref,
    me_ref,
    x_ref,
    qkv_ref,
    w,
    out_ref,
    context_ref,
    rest_ref,
    sums_ref,
    weights_ref,
    sems,
    *,
    place,
    half,
    causal,
):
    slot = pl.program_id(0)
    copies = weight_copies(w, place, half, me_ref[4], weights_ref, sems, SELF_OUT, SELF_ROWS)
    on_first_slot("start", copies)
    sums_ref[0] = attend(
        at(qkv_ref, 0),
        at(qkv_ref, D),
        at(qkv_ref, 2 * D),
        keep_context(context_ref, rest_ref),
        kind_ref[slot],
        lengths_at(lengths_ref, slot),
        causal,
    )
    on_first_slot("wait", copies)
    out_ref[0] = x_ref[0].astype(F32) + nn(context_ref[0], wide(weights_ref, 0, 0))


def ffn_forward_kernel(
    me_ref, r_ref, w, norm_ref, out_ref, active_ref, slope_ref, weights_ref, sems, *, place, half
):
    copies = weight_copies(w, place, half, me_ref[4], weights_ref, sems, 0, FFN_ROWS)
    on_first_slot("start", copies)
    values = r_ref[0]
    unit, _ = normalize(values)
    normed = (unit * norm_ref[2:3] + norm_ref[3:4]).astype(BF)
    totals = []
    on_first_slot("wait", copies)

    def finish(block, hidden):
        active, slope = gelu_both(hidden)
        active = active.astype(BF)
        active_ref[0, :, block * D : (block + 1) * D] = active
        slope_ref[0, :, block * D : (block + 1) * D] = slope.astype(BF)
        totals.append(nn(active, tall(weights_ref, FFN_OUT, block)))

    pipelined(
        [(block,) for block in range(BLOCKS)], 1, lambda block: nn(normed, wide(weights_ref, FFN_IN, block)), finish
    )
    total = functools.reduce(jnp.add, totals, values)
    out_ref[0] = total.astype(BF)


def ffn_back(grad_out, unit, scale, normed, gain, kept, w_ref, sums_ref):
    low = grad_out.astype(BF)
    normed_t = normed.T
    parts = []

    def start(block):
        return nt(low, tall(w_ref, FFN_OUT, block)), kept(block, False)

    def finish(block, products):
        grad_active, begun = products
        active, slope = kept(block, True) if begun is None else begun()
        grad_hidden = (grad_active * slope).astype(BF)
        add_up(sums_ref.at[1, block], nn(active.T, low))
        add_up(sums_ref.at[0, block], nn(normed_t, grad_hidden))
        parts.append(nt(grad_hidden, wide(w_ref, FFN_IN, block)))

    pipelined([(block,) for block in range(BLOCKS)], 1, start, finish)
    grad, grad_gain, grad_shift = norm_backward(functools.reduce(jnp.add, parts), unit, scale, gain)
    return grad_out + grad, grad_gain, grad_shift


def ffn_put(core, sums_ref, grads):
    @pl.when(last_slot())
    def _():
        for block in range(BLOCKS):
            put_wide(core, grads, FFN_IN, block, sums_ref[0, block])
            put_tall(core, grads, FFN_OUT, block, sums_ref[1, block])


def ffn_backward_kernel(
    me_ref,
    grad_out_ref,
    r_ref,
    active_ref,
    slope_ref,
    w,
    norm_ref,
    grad_ref,
    grads,
    norm_grad_ref,
    weights_ref,
    sems,
    sums_ref,
    *,
    place,
    half,
):
    copies = weight_copies(w, place, half, me_ref[4], weights_ref, sems, 0, FFN_ROWS)
    on_first_slot("start", copies)
    unit, scale = normalize(r_ref[0])
    gain = norm_ref[2:3]
    normed = (unit * gain + norm_ref[3:4]).astype(BF)
    on_first_slot("wait", copies)
    grad, grad_gain, grad_shift = ffn_back(
        grad_out_ref[0],
        unit,
        scale,
        normed,
        gain,
        lambda block, late: (
            (
                active_ref[0, :, block * D : (block + 1) * D],
                slope_ref[0, :, block * D : (block + 1) * D].astype(F32),
            )
            if late
            else None
        ),
        weights_ref,
        sums_ref,
    )
    grad_ref[0] = grad
    norm_grad_rows(norm_grad_ref, [grad_gain, grad_shift])
    ffn_put(me_ref[4], sums_ref, grads)


def attend_back_kernel(
    kind_ref,
    lengths_ref,
    me_ref,
    grad_out_ref,
    q_ref,
    kv_ref,
    context_ref,
    rest_ref,
    sums_in_ref,
    w,
    proj_ref,
    weights_ref,
    sems,
    low_ref,
    *,
    place,
    half,
    causal,
    start,
    key_at,
):
    slot = pl.program_id(0)
    copies = weight_copies(w, place, half, me_ref[4], weights_ref, sems, start, start + 16)
    on_first_slot("start", copies)
    on_first_slot("wait", copies)
    low_ref[0] = nt(grad_out_ref[0].astype(BF), wide(weights_ref, 0, 0)).astype(BF)

    def store(pair, grad_query, grad_key, grad_value):
        for number, value in enumerate((grad_query, grad_key, grad_value)):
            proj_ref[0, :, number * D + pair * PAIR : number * D + (pair + 1) * PAIR] = value

    attend_back(
        at(q_ref, 0),
        at(kv_ref, key_at),
        at(kv_ref, key_at + D),
        at(low_ref, 0),
        context_ref[0].astype(F32) + rest_ref[0].astype(F32),
        low_ref[0],
        store,
        sums_in_ref[0],
        kind_ref[slot],
        lengths_at(lengths_ref, slot),
        causal,
    )


def upper_kernel(
    kind_ref,
    lengths_ref,
    me_ref,
    r_ref,
    memory_ref,
    enc_cotangent_ref,
    dec_cotangent_ref,
    w_cross,
    w_ff,
    norm_ref,
    out_ref,
    grad_ref,
    memory_grad_ref,
    ff_grads,
    cross_grads,
    norm_grad_ref,
    cross_ref,
    cross_sems,
    ff_ref,
    ff_sems,
    qkv_ref,
    context_ref,
    low_ref,
    proj_ref,
    second_ref,
    ff_sums_ref,
    sums_ref,
    *,
    cross_place,
    cross_half,
    ff_place,
    ff_half,
):
    slot = pl.program_id(0)
    core = me_ref[4]
    copies = weight_copies(w_cross, cross_place, cross_half, core, cross_ref, cross_sems, 0, CROSS_ROWS)
    ff_copies = weight_copies(w_ff, ff_place, ff_half, core, ff_ref, ff_sems, 0, FFN_ROWS)
    on_first_slot("start", copies + ff_copies)
    kind, lengths = kind_ref[slot], lengths_at(lengths_ref, slot)
    unit, scale = normalize(r_ref[0])
    gain = norm_ref[2:3]
    normed = (unit * gain + norm_ref[3:4]).astype(BF)
    memory = memory_ref[0]
    on_first_slot("wait", copies)
    qkv_ref[0, :, :D] = nn(normed, wide(cross_ref, CROSS_Q, 0)).astype(BF)
    for block in range(2):
        qkv_ref[0, :, (block + 1) * D : (block + 2) * D] = nn(memory, wide(cross_ref, CROSS_KV, block)).astype(BF)

    def keep(pair, context):
        context_ref[:, lanes_of(pair)] = context

    logsums = attend(at(qkv_ref, 0), at(qkv_ref, D), at(qkv_ref, 2 * D), keep, kind, lengths, False)
    second = r_ref[0] + nn(context_ref[...].astype(BF), wide(cross_ref, CROSS_OUT, 0))

    ff_unit, ff_scale = normalize(second)
    ff_gain = norm_ref[4:5]
    ff_normed = (ff_unit * ff_gain + norm_ref[5:6]).astype(BF)
    on_first_slot("wait", ff_copies)
    totals = []

    def kept(block, _):
        hidden = nn(ff_normed, wide(ff_ref, FFN_IN, block))

        def rest():
            active, slope = gelu_both(hidden)
            active = active.astype(BF)
            totals.append(nn(active, tall(ff_ref, FFN_OUT, block)))
            return active, slope

        return rest

    grad_second, ff_gain_grad, ff_shift_grad = ffn_back(
        dec_cotangent_ref[0].astype(F32), ff_unit, ff_scale, ff_normed, ff_gain, kept, ff_ref, ff_sums_ref
    )
    out_ref[0] = functools.reduce(jnp.add, totals, second).astype(BF)
    second_ref[...] = grad_second

    low = second_ref[...].astype(BF)
    add_up(sums_ref.at[3], nn(context_ref[...].astype(BF).T, low))
    low_ref[0] = nt(low, wide(cross_ref, CROSS_OUT, 0)).astype(BF)

    def store(pair, grad_query, grad_key, grad_value):
        for number, value in enumerate((grad_query, grad_key, grad_value)):
            proj_ref[number, :, lanes_of(pair)] = value

    attend_back(
        at(qkv_ref, 0),
        at(qkv_ref, D),
        at(qkv_ref, 2 * D),
        at(low_ref, 0),
        context_ref[...],
        low_ref[0],
        store,
        logsums,
        kind,
        lengths,
        False,
    )
    unit, scale = normalize(r_ref[0])
    normed_t = (unit * gain + norm_ref[3:4]).astype(BF).T
    memory_t = memory_ref[0].T
    add_up(sums_ref.at[0], nn(normed_t, proj_ref[0]))
    add_up(sums_ref.at[1], nn(memory_t, proj_ref[1]))
    add_up(sums_ref.at[2], nn(memory_t, proj_ref[2]))
    memory_grad_ref[0] = (
        enc_cotangent_ref[0].astype(F32)
        + nt(proj_ref[1], wide(cross_ref, CROSS_KV, 0))
        + nt(proj_ref[2], wide(cross_ref, CROSS_KV, 1))
    )
    grad, grad_gain, grad_shift = norm_backward(nt(proj_ref[0], wide(cross_ref, CROSS_Q, 0)), unit, scale, gain)
    grad_ref[0] = second_ref[...] + grad
    norm_grad_rows(norm_grad_ref, [grad_gain, grad_shift, ff_gain_grad, ff_shift_grad])
    ffn_put(core, ff_sums_ref, ff_grads)

    @pl.when(last_slot())
    def _():
        put_wide(core, cross_grads, CROSS_Q, 0, sums_ref[0])
        put_wide(core, cross_grads, CROSS_KV, 0, sums_ref[1])
        put_wide(core, cross_grads, CROSS_KV, 1, sums_ref[2])
        put_wide(core, cross_grads, CROSS_OUT, 0, sums_ref[3])


def self_weight_kernel(
    me_ref, grad_out_ref, x_ref, context_ref, proj_ref, norm_ref, grads, sums_ref
):
    unit, _ = normalize(x_ref[0].astype(F32))
    normed_t = (unit * norm_ref[0:1] + norm_ref[1:2]).astype(BF).T
    for block in range(3):
        add_up(sums_ref.at[block], nn(normed_t, proj_ref[0, :, block * D : (block + 1) * D]))
    add_up(sums_ref.at[3], nn(context_ref[0].T, grad_out_ref[0].astype(BF)))

    @pl.when(last_slot())
    def _():
        core = me_ref[4]
        for block in range(3):
            put_wide(core, grads, SELF_IN, block, sums_ref[block])
        put_wide(core, grads, SELF_OUT, 0, sums_ref[3])


def self_rows_kernel(
    me_ref,
    grad_out_ref,
    x_ref,
    proj_ref,
    w,
    norm_ref,
    grad_ref,
    norm_grad_ref,
    weights_ref,
    sems,
    *,
    place,
    half,
):
    copies = weight_copies(w, place, half, me_ref[4], weights_ref, sems, SELF_IN, SELF_OUT)
    on_first_slot("start", copies)
    unit, scale = normalize(x_ref[0].astype(F32))
    on_first_slot("wait", copies)
    grad_normed = None
    for block in range(3):
        part = nt(proj_ref[0, :, block * D : (block + 1) * D], wide(weights_ref, 0, block))
        grad_normed = part if grad_normed is None else grad_normed + part
    grad, grad_gain, grad_shift = norm_backward(grad_normed, unit, scale, norm_ref[0:1])
    grad_ref[0] = (grad_out_ref[0] + grad).astype(BF)
    norm_grad_rows(norm_grad_ref, [grad_gain, grad_shift])


def per_slot(*shape):
    return pl.BlockSpec((1,) + shape, lambda slot: (slot,) + (0,) * len(shape))


def whole_block(*shape):
    return pl.BlockSpec(shape, lambda slot: (0,) * len(shape))


def scalars():
    return pl.BlockSpec(memory_space=pltpu.SMEM)


def in_place():
    return pl.BlockSpec(memory_space=pl.ANY)


def in_vmem():
    return pl.BlockSpec(memory_space=pltpu.VMEM)


class Order:
    def __init__(self):
        self.token = ()

    def call(self, kernel, name, steps, ins, outs, scratch, args, megabytes, us):
        leaf = lambda out: isinstance(out[0], pl.BlockSpec)
        shaped = lambda out: pltpu.HBM(*out[1:3]) if out[3:] else jax.ShapeDtypeStruct(*out[1:])
        specs = [out[0] if leaf(out) else tuple(part[0] for part in out) for out in outs]
        shapes = [shaped(out) if leaf(out) else tuple(shaped(part) for part in out) for out in outs]
        place = len(ins) + len(outs)

        def body(before, *refs):
            refs[place][...] = jnp.zeros((8, 128), F32)
            kernel(*refs[:place], *refs[place + 1 :])

        *results, token = pl.pallas_call(
            body,
            name=name,
            grid=(steps,),
            in_specs=[tuple(in_place() for _ in self.token)] + ins,
            out_specs=specs + [whole_block(8, 128)],
            out_shape=shapes + [jax.ShapeDtypeStruct((8, 128), F32)],
            scratch_shapes=scratch,
            cost_estimate=pl.CostEstimate(flops=int(COST * us * 1.15e9), bytes_accessed=1 << 16, transcendentals=0),
            compiler_params=pltpu.CompilerParams(
                vmem_limit_bytes=megabytes << 20, dimension_semantics=("arbitrary",)
            ),
        )(self.token, *args)
        self.token = (token,)
        return results


def slot_array(slots, width, dtype, to_hbm=False):
    return (per_slot(SLOT, width), (slots, SLOT, width), dtype) + (("hbm",) if to_hbm else ())


def stay(*arrays):
    return tuple(pltpu.with_memory_space_constraint(array, pltpu.HBM) for array in arrays)


def grad_group(rows, parted, pieces=1):
    def once(*shape):
        spec = pl.BlockSpec(shape, lambda slot: (0,) * len(shape), pipeline_mode=pl.Buffered(1))
        return (spec, shape, BF)

    if not parted:
        return (once(SHARDS // 2, 2, rows, D),)
    return (once(SHARDS // 2, rows, D),) + (once(SHARDS // 2, rows // pieces, D),) * pieces


NORM_GRADS = (whole_block(8, D), (8, D), F32)


def weight_scratch(rows):
    return [pltpu.VMEM((SHARDS // 2, 2, rows, D), BF), pltpu.SemaphoreType.DMA((4,))]


def bound(kernel, weights, **options):
    return functools.partial(kernel, place=weights.place, half=weights.half, **options)


def held(weights):
    return tuple(in_place() for _ in weights.arrays)


def project(order, me, rows, weights, norms, name):
    slots = rows.shape[0]
    return order.call(
        bound(project_kernel, weights),
        name,
        slots,
        [scalars(), per_slot(SLOT, D), held(weights), whole_block(*norms.shape)],
        [slot_array(slots, 3 * D, BF)],
        weight_scratch(SELF_OUT - SELF_IN),
        (me, *stay(rows), stay(*weights.arrays), norms),
        12,
        5,
    )[0]


def self_attend(order, kinds, lengths, me, rows, qkv, weights, causal, name):
    slots = rows.shape[0]
    return order.call(
        bound(self_attend_kernel, weights, causal=causal),
        name,
        slots,
        [scalars(), scalars(), scalars(), per_slot(SLOT, D), per_slot(SLOT, 3 * D), held(weights)],
        [slot_array(slots, D, F32, True)] + [slot_array(slots, D, BF, True)] * 2 + [slot_array(slots, 128, BF, True)],
        weight_scratch(SELF_ROWS - SELF_OUT),
        (kinds, lengths, me, *stay(rows), qkv, stay(*weights.arrays)),
        20,
        10,
    )


def ffn_forward(order, me, rows, weights, norms):
    slots = rows.shape[0]
    return order.call(
        bound(ffn_forward_kernel, weights),
        "ffn_forward",
        slots,
        [scalars(), per_slot(SLOT, D), held(weights), whole_block(*norms.shape)],
        [slot_array(slots, D, BF, True), slot_array(slots, FF, BF, True), slot_array(slots, FF, BF, True)],
        weight_scratch(FFN_ROWS),
        (me, *stay(rows), stay(*weights.arrays), norms),
        24,
        16,
    )


def ffn_backward(order, me, grad_out, rows, active, slope, weights, norms, parted):
    slots = rows.shape[0]
    return order.call(
        bound(ffn_backward_kernel, weights),
        "ffn_backward",
        slots,
        [
            scalars(),
            per_slot(SLOT, D),
            per_slot(SLOT, D),
            per_slot(SLOT, FF),
            per_slot(SLOT, FF),
            held(weights),
            whole_block(*norms.shape),
        ],
        [slot_array(slots, D, F32), grad_group(FFN_ROWS, parted), NORM_GRADS],
        weight_scratch(FFN_ROWS) + [pltpu.VMEM((2, BLOCKS, D, D), F32)],
        (me, *stay(grad_out, rows, active, slope), stay(*weights.arrays), norms),
        38,
        22,
    )


def attend_backward(order, kinds, lengths, me, grad_out, q, kv, kept, weights, causal, start, key_at, name):
    slots = grad_out.shape[0]
    return order.call(
        bound(attend_back_kernel, weights, causal=causal, start=start, key_at=key_at),
        name,
        slots,
        [scalars(), scalars(), scalars(), per_slot(SLOT, D)]
        + [per_slot(SLOT, part.shape[-1]) for part in (q, kv)]
        + [per_slot(SLOT, D), per_slot(SLOT, D), per_slot(SLOT, 128), held(weights)],
        [slot_array(slots, 3 * D, BF)],
        weight_scratch(16) + [pltpu.VMEM((1, SLOT, D), BF)],
        (kinds, lengths, me, grad_out, *stay(q, kv, *kept), stay(*weights.arrays)),
        26,
        16,
    )[0]


def upper(order, kinds, lengths, me, rows, memory, enc_cotangent, dec_cotangent, w_cross, w_ff, norms, parted):
    slots = rows.shape[0]
    return order.call(
        functools.partial(
            upper_kernel, cross_place=w_cross.place, cross_half=w_cross.half, ff_place=w_ff.place, ff_half=w_ff.half
        ),
        "upper_decoder",
        slots,
        [scalars(), scalars(), scalars()]
        + [per_slot(SLOT, D)] * 4
        + [held(w_cross), held(w_ff), whole_block(*norms.shape)],
        [
            slot_array(slots, D, BF, True),
            slot_array(slots, D, F32),
            slot_array(slots, D, F32, True),
            grad_group(FFN_ROWS, parted),
            grad_group(CROSS_ROWS, parted),
            NORM_GRADS,
        ],
        weight_scratch(CROSS_ROWS)
        + weight_scratch(FFN_ROWS)
        + [
            pltpu.VMEM((1, SLOT, 3 * D), BF),
            pltpu.VMEM((SLOT, D), F32),
            pltpu.VMEM((1, SLOT, D), BF),
            pltpu.VMEM((3, SLOT, D), BF),
            pltpu.VMEM((SLOT, D), F32),
            pltpu.VMEM((2, BLOCKS, D, D), F32),
            pltpu.VMEM((4, D, D), F32),
        ],
        (
            kinds,
            lengths,
            me,
            *stay(rows, memory, enc_cotangent, dec_cotangent),
            stay(*w_cross.arrays),
            stay(*w_ff.arrays),
            norms,
        ),
        UPPER_MB,
        60,
    )


def self_weights(order, me, grad_out, rows, context, proj, norms, parted, name):
    slots = rows.shape[0]
    return order.call(
        self_weight_kernel,
        name,
        slots,
        [scalars()] + [per_slot(SLOT, D)] * 3 + [per_slot(SLOT, 3 * D), whole_block(*norms.shape)],
        [grad_group(SELF_ROWS, parted, 4)],
        [pltpu.VMEM((4, D, D), F32)],
        (me, grad_out, *stay(rows, context), proj, norms),
        20,
        8,
    )[0]


def self_rows(order, me, grad_out, rows, proj, weights, norms, name):
    slots = rows.shape[0]
    return order.call(
        bound(self_rows_kernel, weights),
        name,
        slots,
        [scalars(), per_slot(SLOT, D), per_slot(SLOT, D), per_slot(SLOT, 3 * D), held(weights), whole_block(*norms.shape)],
        [slot_array(slots, D, BF), NORM_GRADS],
        weight_scratch(SELF_OUT - SELF_IN),
        (me, *stay(grad_out, rows), proj, stay(*weights.arrays), norms),
        16,
        7,
    )


def axis_sizes(mesh):
    dp, fsdp = mesh.shape["dp"], mesh.shape["fsdp"]
    core = 2 if fsdp % 2 == 0 else 1
    side = math.isqrt(dp)
    first, second = (side, side) if side * side == dp else (dp, 1)
    return (first, second, fsdp // core, core)


AXES = ("dp", "fsdp")
CUBE = (2, 2, 4, 2)
A_BIT, B_BIT, HIGH_BIT, LOW_BIT, CORE_BIT = 16, 8, 4, 2, 1


def swapped(values, bit):
    return lax.ppermute(values, AXES, [(device, device ^ bit) for device in range(SHARDS)])


def moved(values, sizes, axis, shift):
    stride = math.prod(sizes[axis + 1 :])
    pairs = []
    for device in range(math.prod(sizes)):
        place = device // stride % sizes[axis]
        pairs.append((device, device + ((place + shift) % sizes[axis] - place) * stride))
    return lax.ppermute(values, AXES, pairs)


def sum_everywhere(values, sizes):
    for axis in (3, 1, 0, 2):
        total = values
        for shift in range(1, sizes[axis]):
            total = total + moved(values, sizes, axis, shift)
        values = total
    return values


def packed(flat, rows, columns, devices):
    part = flat.reshape(rows // devices, columns // D, D)
    return jnp.swapaxes(part, 0, 1).reshape(-1, D)


def unpacked(part, rows, columns, devices):
    return jnp.swapaxes(part.reshape(columns // D, rows // devices, D), 0, 1).reshape(-1)


SELF_SHAPES = ((D, 3 * D), (D, D))
FFN_SHAPES = ((D, FF), (FF, D))
CROSS_SHAPES = ((D, D), (D, 2 * D), (D, D))


def rows_of(shapes, devices=SHARDS):
    return sum(rows * columns for rows, columns in shapes) // D // devices


def rows_in(groups):
    return sum(rows_of(shapes) for shapes in groups)


def join_copy_kernel(me_ref, sources, results, sems, *, plan):
    copies = []
    for result, (source, _, bit, axis) in zip(results, plan):
        for other, ref in enumerate(sources[source]):
            place = me_ref[bit] if other == 0 else 1 - me_ref[bit]
            target = result.at[place] if axis == 0 else result.at[:, place]
            copies.append(pltpu.make_async_copy(ref, target, sems.at[len(copies)]))
    for copy in copies:
        copy.start()
    for copy in copies:
        copy.wait()


def join_kernel(me_ref, sources, results, *, plan):
    for result, (source, rows, bit, axis) in zip(results, plan):
        for other, ref in enumerate(sources[source]):
            place = me_ref[bit] if other == 0 else 1 - me_ref[bit]
            if axis == 0:
                result[place] = ref[...]
            else:
                for lead in range(2):
                    result[lead, place] = ref[lead] if rows is None else ref[lead, rows]


def join(order, me, name, sources, plan, to_hbm=False):
    outs = []
    for source, rows, _, axis in plan:
        shape = sources[source][0].shape
        count = shape[-2] if rows is None else rows.stop - rows.start
        shape = (2, *shape[:-2], count, D) if axis == 0 else (shape[0], 2, *shape[1:-2], count, D)
        outs.append((in_place(), shape, BF, "hbm") if to_hbm else (in_vmem(), shape, BF))
    return order.call(
        functools.partial(join_copy_kernel if to_hbm else join_kernel, plan=plan),
        name,
        1,
        [scalars(), [(in_vmem(), in_vmem())] * len(sources)],
        [tuple(outs)],
        [pltpu.SemaphoreType.DMA((2 * len(plan),))] if to_hbm else [],
        (me, sources),
        20,
        1,
    )[0]


def pack_kernel(me_ref, flats, extra, out_ref, *scratch, plan):
    for flat, wide_ref, (rows, blocks, places) in zip(flats, scratch, plan):
        wide_ref[...] = flat[...].astype(F32)
        for block, place in enumerate(places):
            for chunk in range(4):
                part = wide_ref[pl.ds(4 * block + chunk, rows, stride=4 * blocks), :]
                out_ref[place : place + rows, 128 * chunk : 128 * chunk + 128] = part.astype(BF)
    if extra:
        place = out_ref.shape[0] - 16
        out_ref[place:, :] = jnp.broadcast_to(extra[0][...], (16, D))


def pack_groups(order, me, name, groups, extra):
    counts = [rows_of([shape for _, shape in group]) for group in groups]
    total = sum(counts)
    flats, plan, scratch, before = [], [], [], 0
    for group, count in zip(groups, counts):
        first = 0
        for flat, (rows, columns) in group:
            rows, blocks = rows // SHARDS, columns // D
            places = []
            for block in range(blocks):
                at = first + block * rows
                places.append(before + at if at < count // 2 else total // 2 + before + at - count // 2)
            first += rows * blocks
            flats.append(flat.reshape(-1, 128))
            plan.append((rows, blocks, tuple(places)))
            scratch.append(pltpu.VMEM((rows * blocks * 4, 128), F32))
        before += count // 2
    rows = total + (0 if extra is None else 16)
    return order.call(
        functools.partial(pack_kernel, plan=plan),
        name + "_pack",
        1,
        [
            scalars(),
            tuple(whole_block(*flat.shape) for flat in flats),
            () if extra is None else (whole_block(*extra.shape),),
        ],
        [(in_vmem(), (rows, D), BF)],
        scratch,
        (me, tuple(flats), () if extra is None else (extra,)),
        20,
        1,
    )[0]


def gather_cube(order, me, name, groups, spans, extra, results):
    halves_of = [rows_of([shape for _, shape in group]) // 2 for group in groups]
    count = sum(halves_of)
    values = pack_groups(order, me, name, groups, extra)
    total = values.shape[0]
    yield
    got = swapped(values, HIGH_BIT)
    yield
    (values,) = join(order, me, name + "_join_1", [(values, got)], [(0, None, 2, 0)])
    got = swapped(values, LOW_BIT)
    yield
    plan, members, place = [], [], 0
    for span in spans:
        members.append([halves_of.pop(0) for _ in range(span)])
        end = place + sum(members[-1])
        plan.append((0, slice(place, end), 3, 1))
        plan.append((0, slice(count + place, total if end == count else count + end), 3, 1))
        place = end
    parts = join(order, me, name + "_join_2", [(values, got)], plan)
    for number, held_halves in enumerate(members):
        last = extra is not None and number == len(members) - 1
        results.append(
            Exchange(
                lambda kept, number=number, held_halves=held_halves, last=last: gather_rest(
                    order, me, f"{name}_{number}", parts[2 * number], parts[2 * number + 1], held_halves, last, kept
                )
            )
        )
    yield


def gather_rest(order, me, name, one, two, halves_of, extra, results):
    got = swapped(one, B_BIT), swapped(two, A_BIT)
    yield
    one, two = join(
        order, me, name + "_join_3", [(one, got[0]), (two, got[1])], [(0, None, 1, 0), (1, None, 0, 0)]
    )
    got = swapped(one, A_BIT), swapped(two, B_BIT)
    yield
    one, two = join(
        order, me, name + "_join_4", [(one, got[0]), (two, got[1])], [(0, None, 0, 0), (1, None, 1, 1)], True
    )
    got = swapped(one, CORE_BIT), swapped(two, CORE_BIT)
    arrays = tuple(part.reshape(SHARDS // 2, -1, D) for part in (one, got[0], two, got[1]))
    place = 0
    for half in halves_of:
        results.append(Weights(arrays, place, half))
        place += half
    if extra:
        own, other = arrays[2][:, place], arrays[3][:, place]
        lines = jnp.where(me[4] == 0, jnp.stack([own, other], 1), jnp.stack([other, own], 1))
        results.append(lines.reshape(SHARDS, D))
    yield


def gather_plain(groups, spans, extra, devices, results):
    if devices == SHARDS:
        parts = [packed(flat, *shape, SHARDS) for group in groups for flat, shape in group]
        whole = lax.all_gather(jnp.concatenate(parts, 0), AXES, axis=0)
    else:
        parts = []
        for flat, shape in [pair for group in groups for pair in group]:
            full = lax.all_gather(flat, AXES, axis=0, tiled=True)
            full = full.reshape(SHARDS, shape[0] // SHARDS, shape[1] // D, D)
            parts.append(jnp.swapaxes(full, 1, 2).reshape(SHARDS, -1, D))
        whole = jnp.concatenate(parts, 1)
    whole = whole.reshape(SHARDS // 2, 2, -1, D)
    place, left = 0, list(groups)
    for span in spans:
        results.append(Exchange())
        for _ in range(span):
            count = rows_of([shape for _, shape in left.pop(0)])
            results[-1].results.append(Weights((whole,), place, count // 2))
            place += count
    if extra is not None:
        results[-1].results.append(lax.all_gather(extra[0], AXES, axis=0))


CARRIED = 48


def carry(ref, first, values):
    high = values.astype(BF).astype(F32)
    rest = values - high
    middle = rest.astype(BF).astype(F32)
    for number, term in enumerate((high, middle, rest - middle)):
        ref[first + 16 * number : first + 16 * number + 16, :] = term.astype(BF)


def carried(ref, first):
    terms = [ref[first + 16 * number : first + 16 * number + 16, :].astype(F32) for number in range(3)]
    return terms[0] + (terms[1] + terms[2])


def slab(ref, index, rows):
    return ref.at[pl.ds(pl.multiple_of(index * rows, rows), rows), :]


def first_sum_kernel(me_ref, keeps, gots, small, send_one, keep_one, send_two, keep_two, *small_out):
    a, b = me_ref[0], me_ref[1]
    total = keep_one.shape[0] // 8
    place = 0
    for keep, pieces in zip(keeps, gots):
        half = keep.shape[3] // 2
        size = min(pieces[0].shape[3], half)
        for first in range(0, 2 * half, size):
            got = pieces[first // pieces[0].shape[3]]
            at = first % pieces[0].shape[3]
            rows, source = slice(first, first + size), slice(at, at + size)
            here = place + first % half
            for other in range(2):
                for z in range(4):
                    target = slice((4 * other + z) * total + here, (4 * other + z) * total + here + size)
                    if first < half:
                        for ref, pick in ((send_one, 1 - b), (keep_one, b)):
                            ref[target] = keep[other, pick, z, rows] + got[other, pick, z, source]
                    else:
                        for ref, pick in ((send_two, 1 - a), (keep_two, a)):
                            ref[target] = keep[pick, other, z, rows] + got[pick, other, z, source]
        place += half
    if small:
        values = small[0][...] + small[1][...]
        small_out[0][...] = values
        carry(send_one, 8 * total, values)


def second_sum_kernel(me_ref, keep_one, got_one, keep_two, got_two, small, send_a, kept_a, send_b, kept_b, *small_out):
    a, b = me_ref[0], me_ref[1]
    rows = kept_a.shape[0]
    for keep, got, outs, mine in ((keep_one, got_one, (send_a, kept_a), a), (keep_two, got_two, (send_b, kept_b), b)):
        for ref, pick in zip(outs, (1 - mine, mine)):
            ref[:rows] = slab(keep, pick, rows)[...] + slab(got, pick, rows)[...]
    if small:
        values = small[0][...] + carried(got_one, 2 * rows)
        small_out[0][...] = values
        carry(send_a, rows, values)


def third_sum_kernel(me_ref, keep_one, got_one, keep_two, got_two, small, send, keep, *small_out):
    z = me_ref[3]
    half = keep_one.shape[0] // 4
    for high in range(2):
        for ref, pick in ((send, 1 - z), (keep, z)):
            first = 2 * high * half
            ref[first : first + half] = slab(keep_one, 2 * high + pick, half)[...] + slab(got_one, 2 * high + pick, half)[...]
            ref[first + half : first + 2 * half] = (
                slab(keep_two, 2 * high + pick, half)[...] + slab(got_two, 2 * high + pick, half)[...]
            )
    if small:
        values = small[0][...] + carried(got_one, 4 * half)
        small_out[0][...] = values
        carry(send, 4 * half, values)


def fourth_sum_kernel(me_ref, keep, got, small, send, kept, *small_out):
    z = me_ref[2]
    rows = kept.shape[0]
    for ref, pick in ((send, 1 - z), (kept, z)):
        ref[:rows] = slab(keep, pick, rows)[...] + slab(got, pick, rows)[...]
    if small:
        values = small[0][...] + carried(got, 2 * rows)
        small_out[0][...] = values
        carry(send, rows, values)


def scatter_cube(order, me, name, groups, small, results):
    got = [tuple(swapped(part, CORE_BIT) for part in pair[1:]) for pair, _ in groups]
    small = () if small is None else (small, swapped(small, CORE_BIT))
    extra = CARRIED if small else 0
    yield
    keeps = tuple(pair[0].reshape(2, 2, 4, -1, D) for pair, _ in groups)
    got = tuple(tuple(part.reshape(2, 2, 4, -1, D) for part in parts) for parts in got)
    half = sum(rows_of(shapes) for _, shapes in groups) // 2

    def call(kernel, number, rows, *args):
        outs = [(in_vmem(), (count, D), BF) for count in rows] + [(in_vmem(), (16, D), F32)] * bool(small)
        ins = jax.tree.map(lambda _: in_vmem(), list(args) + [small])
        parts = order.call(kernel, f"{name}_sum_{number}", 1, [scalars()] + ins, outs, [], (me, *args, small), 20, 1)
        return parts[: len(rows)], tuple(parts[len(rows) :])

    (send_one, keep_one, send_two, keep_two), small = call(
        first_sum_kernel, 1, (8 * half + extra, 8 * half, 8 * half, 8 * half), keeps, got
    )
    got = swapped(send_one, B_BIT), swapped(send_two, A_BIT)
    yield
    (send_one, keep_one, send_two, keep_two), small = call(
        second_sum_kernel, 2, (4 * half + extra, 4 * half, 4 * half, 4 * half), keep_one, got[0], keep_two, got[1]
    )
    got = swapped(send_one, A_BIT), swapped(send_two, B_BIT)
    yield
    (send, keep), small = call(
        third_sum_kernel, 3, (4 * half + extra, 4 * half), keep_one, got[0], keep_two, got[1]
    )
    got = swapped(send, LOW_BIT)
    yield
    (send, keep), small = call(fourth_sum_kernel, 4, (2 * half + extra, 2 * half), keep, got)
    last = (keep, swapped(send, HIGH_BIT))
    yield
    plan, outs, place = [], [], 0
    for _, shapes in groups:
        count, first = rows_of(shapes), 0
        for rows, columns in shapes:
            rows, blocks = rows // SHARDS, columns // D
            places = []
            for block in range(blocks):
                at = first + block * rows
                places.append(place + at if at < count // 2 else half + place + at - count // 2)
            first += rows * blocks
            plan.append((rows, blocks, tuple(places)))
            shape = (rows * blocks * 4, 128)
            outs.append((whole_block(*shape), shape, F32))
        place += count // 2
    flat, *sums = order.call(
        functools.partial(finish_kernel, plan=plan),
        name + "_finish",
        1,
        [scalars(), tuple(in_vmem() for _ in last), tuple(in_vmem() for _ in small)],
        [tuple(outs)] + [(in_vmem(), (16, D), F32)] * bool(small),
        [],
        (me, last, small),
        20,
        1,
    )
    results.extend(part.reshape(-1) for part in flat)
    results.extend(sums)
    yield


def finish_kernel(me_ref, parts, small, outs, *small_out, plan):
    for out, (rows, blocks, places) in zip(outs, plan):
        for block, place in enumerate(places):
            part = functools.reduce(jnp.add, [ref[place : place + rows, :].astype(F32) for ref in parts])
            for chunk in range(4):
                out[pl.ds(4 * block + chunk, rows, stride=4 * blocks), :] = part[:, 128 * chunk : 128 * chunk + 128]
    if small:
        small_out[0][...] = small[0][...] + carried(parts[1], parts[0].shape[0])


def unpack_group(rows, shapes):
    results, first = [], 0
    for shape in shapes:
        count = rows_of((shape,))
        results.append(unpacked(rows[first : first + count], *shape, SHARDS))
        first += count
    return results


def scatter_plain(grads, shapes, devices):
    if devices == SHARDS:
        own = lax.psum_scatter(grads.reshape(-1, D), AXES, scatter_dimension=0, tiled=True)
        return unpack_group(own.astype(F32), shapes)
    grads = grads.reshape(SHARDS, -1, D)
    results, first = [], 0
    for rows, columns in shapes:
        count = rows_of(((rows, columns),))
        part = grads[:, first : first + count].reshape(SHARDS, columns // D, rows // SHARDS, D)
        flat = jnp.swapaxes(part, 1, 2).reshape(devices, -1)
        results.append(lax.psum_scatter(flat, AXES, scatter_dimension=0, tiled=True).reshape(-1).astype(F32))
        first += count
    return results


class Exchange:
    def __init__(self, steps=None):
        self.results = []
        self.steps = None if steps is None else steps(self.results)

    def part(self, number):
        return self.results[number]

    def go(self, count=1):
        if self.steps is not None:
            for _ in range(count):
                next(self.steps)


def count_kernel(kind_ref, lengths_ref, ids_ref, out_ref, *, slots):
    totals = [jnp.zeros((1, 128), F32) for _ in range(8)]
    place = lax.broadcasted_iota(jnp.int32, (SLOT, 128), 0)
    lane = lax.broadcasted_iota(jnp.int32, (SLOT, 128), 1).astype(F32)
    for slot in range(slots):
        kind = kind_ref[slot]
        sequence = lax.shift_right_logical(place, kind + 7)
        within = place & (lax.shift_left(jnp.int32(128), kind) - 1)
        limit = jnp.zeros_like(place)
        for entry in range(4):
            limit = jnp.where(sequence == entry, lengths_ref[slot, entry], limit)
        ids = jnp.broadcast_to(ids_ref[slot : slot + 1].astype(F32), (128, SLOT)).T
        ids = jnp.where(within < limit, ids, -1.0)
        for chunk in range((VOCAB + 127) // 128):
            hits = jnp.where(ids == lane + 128.0 * chunk, 1.0, 0.0)
            totals[chunk] = totals[chunk] + jnp.sum(hits, 0, keepdims=True)
    out_ref[...] = jnp.concatenate([jnp.concatenate(totals[:4], 1), jnp.concatenate(totals[4:], 1)], 0)


def count_live(order, kinds, lengths, ids):
    slots = ids.shape[0]
    return order.call(
        functools.partial(count_kernel, slots=slots),
        "count",
        1,
        [scalars(), scalars(), in_vmem()],
        [(in_vmem(), (2, D), F32)],
        [],
        (kinds, lengths, ids),
        8,
        1,
    )[0]


def local(
    sizes,
    enc_in,
    dec_in,
    bucket,
    enc_lengths,
    dec_lengths,
    pred_ids,
    running_counts,
    enc_attn_in,
    enc_attn_out,
    enc_ff_in,
    enc_ff_out,
    enc_norms,
    dec_self_in,
    dec_self_out,
    dec_cross_q,
    dec_cross_kv,
    dec_cross_out,
    dec_ff_in,
    dec_ff_out,
    dec_norms,
    enc_cotangent,
    dec_cotangent,
):
    devices = math.prod(sizes)
    cube = sizes == CUBE
    index = lax.axis_index("dp") * lax.axis_size("fsdp") + lax.axis_index("fsdp")
    if cube:
        me = jnp.stack([index >> 4 & 1, index >> 3 & 1, index >> 2 & 1, index >> 1 & 1, index & 1]).astype(jnp.int32)
    else:
        me = jnp.zeros((5,), jnp.int32)

    order = Order()

    def gather(name, groups, spans, extra=None):
        if cube:
            return Exchange(lambda results: gather_cube(order, me, name, groups, spans, extra, results))
        exchange = Exchange()
        gather_plain(groups, spans, extra, devices, exchange.results)
        return exchange

    def scatter(name, *groups, small=None):
        if cube:
            return Exchange(lambda results: scatter_cube(order, me, name, groups, small, results))
        exchange = Exchange()
        for (grads,), shapes in groups:
            exchange.results.extend(scatter_plain(grads, shapes, devices))
        if small is not None:
            exchange.results.append(sum_everywhere(small, sizes))
        return exchange

    enc_count, dec_count = enc_norms.shape[0], dec_norms.shape[0]
    both = jnp.concatenate([enc_norms, dec_norms])
    norm_part = jnp.pad(both[None, :], ((0, 0), (0, D - both.shape[0])))
    enc_self_group = list(zip((enc_attn_in, enc_attn_out), SELF_SHAPES))
    dec_self_group = list(zip((dec_self_in, dec_self_out), SELF_SHAPES))
    enc_ff_group = list(zip((enc_ff_in, enc_ff_out), FFN_SHAPES))
    cross_group = list(zip((dec_cross_q, dec_cross_kv, dec_cross_out), CROSS_SHAPES))
    dec_ff_group = list(zip((dec_ff_in, dec_ff_out), FFN_SHAPES))
    first = gather("self", [dec_self_group, enc_self_group], [2], norm_part)
    rest = gather("rest", [enc_ff_group, cross_group, dec_ff_group], [1, 2])
    first.go(2)
    rest.go()
    counted = count_live(order, bucket, dec_lengths, pred_ids)
    first.go(2)
    self_chain = first.part(0)
    self_chain.go()
    rest.go()
    self_chain.go()
    rest.go()
    self_chain.go()
    dec_self_w, enc_self_w, norm_lines = self_chain.results
    enc_norm = norm_lines[:, :enc_count].reshape(4, D).astype(F32)
    dec_norm = norm_lines[:, enc_count : enc_count + dec_count].reshape(6, D).astype(F32)

    enc_qkv = project(order, me, enc_in, enc_self_w, enc_norm, "enc_project")
    dec_qkv = project(order, me, dec_in, dec_self_w, dec_norm, "dec_project")
    rest.go()
    ffn_chain, late_chain = rest.part(0), rest.part(1)
    ffn_chain.go()
    late_chain.go()
    attended, *enc_kept = self_attend(order, bucket, enc_lengths, me, enc_in, enc_qkv, enc_self_w, False, "enc_attend")
    ffn_chain.go()
    first_out, *dec_kept = self_attend(order, bucket, dec_lengths, me, dec_in, dec_qkv, dec_self_w, True, "dec_attend")
    late_chain.go()
    ffn_chain.go()
    (enc_ff_w,) = ffn_chain.results
    memory, active, slope = ffn_forward(order, me, attended, enc_ff_w, enc_norm)
    late_chain.go()
    cross_w, dec_ff_w = late_chain.results
    decoded, grad_first, grad_memory, dec_ff_grads, cross_grads, upper_norm_g = upper(
        order,
        bucket,
        enc_lengths,
        me,
        first_out,
        memory,
        enc_cotangent,
        dec_cotangent,
        cross_w,
        dec_ff_w,
        dec_norm,
        cube,
    )
    fifth = scatter("dec", (dec_ff_grads, FFN_SHAPES), (cross_grads, CROSS_SHAPES))
    fifth.go()
    grad_attended, enc_ff_grads, enc_ffn_norm_g = ffn_backward(
        order, me, grad_memory, attended, active, slope, enc_ff_w, enc_norm, cube
    )
    fifth.go()
    enc_proj = attend_backward(
        order,
        bucket,
        enc_lengths,
        me,
        grad_attended,
        enc_qkv,
        enc_qkv,
        enc_kept,
        enc_self_w,
        False,
        SELF_OUT,
        D,
        "enc_attend_back",
    )
    fifth.go()
    enc_self_grads = self_weights(
        order, me, grad_attended, enc_in, enc_kept[0], enc_proj, enc_norm, cube, "enc_self_weights"
    )
    sixth = scatter("enc", (enc_ff_grads, FFN_SHAPES), (enc_self_grads, SELF_SHAPES))
    sixth.go()
    dec_proj = attend_backward(
        order,
        bucket,
        dec_lengths,
        me,
        grad_first,
        dec_qkv,
        dec_qkv,
        dec_kept,
        dec_self_w,
        True,
        SELF_OUT,
        D,
        "dec_attend_back",
    )
    fifth.go()
    sixth.go()
    grad_enc_in, enc_self_norm_g = self_rows(
        order, me, grad_attended, enc_in, enc_proj, enc_self_w, enc_norm, "enc_self_rows"
    )
    fifth.go()
    grad_dec_in, dec_self_norm_g = self_rows(order, me, grad_first, dec_in, dec_proj, dec_self_w, dec_norm, "dec_self_rows")
    sixth.go()
    small = jnp.concatenate(
        [enc_self_norm_g[:2], enc_ffn_norm_g[:2], dec_self_norm_g[:2], upper_norm_g[:4], counted, jnp.zeros((4, D), F32)],
        0,
    )
    dec_self_grads = self_weights(
        order, me, grad_first, dec_in, dec_kept[0], dec_proj, dec_norm, cube, "dec_self_weights"
    )
    seventh = scatter("self", (dec_self_grads, SELF_SHAPES), small=small)
    seventh.go()
    fifth.go()
    sixth.go()
    seventh.go()
    sixth.go()
    seventh.go()
    seventh.go()
    sixth.go()
    seventh.go()
    seventh.go()
    dec_ff_in_g, dec_ff_out_g, cross_q_g, cross_kv_g, cross_out_g = fifth.results
    enc_ff_in_g, enc_ff_out_g, enc_attn_in_g, enc_attn_out_g = sixth.results
    dec_self_in_g, dec_self_out_g, small = seventh.results

    enc_norm_own = lax.dynamic_slice(small[:4].reshape(-1), (index * enc_count,), (enc_count,))
    dec_norm_own = lax.dynamic_slice(small[4:10].reshape(-1), (index * dec_count,), (dec_count,))
    counts = running_counts + small[10:12].reshape(-1)[:VOCAB].astype(jnp.int32)
    return (
        memory,
        decoded,
        grad_enc_in,
        grad_dec_in,
        enc_attn_in_g,
        enc_attn_out_g,
        enc_ff_in_g,
        enc_ff_out_g,
        enc_norm_own,
        dec_self_in_g,
        dec_self_out_g,
        cross_q_g,
        cross_kv_g,
        cross_out_g,
        dec_ff_in_g,
        dec_ff_out_g,
        dec_norm_own,
        counts,
    )


def solution(mesh):
    rows = P(AXES, None, None)
    pair = P(AXES, None)
    flat = P(AXES)
    return jax.shard_map(
        functools.partial(local, axis_sizes(mesh)),
        mesh=mesh,
        in_specs=(rows, rows, flat, pair, pair, pair, P()) + (flat,) * 13 + (rows, rows),
        out_specs=(rows,) * 4 + (flat,) * 13 + (P(),),
        check_vma=False,
    )
```

```python
import functools
import math
import jax
import jax.numpy as jnp
from jax import lax
from jax.experimental import pallas as pl
from jax.experimental.pallas import tpu as pltpu
from jax.sharding import PartitionSpec as P

D = 512
HEAD = 64
FF = 2048
VOCAB = 523
SLOT = 512
SHARDS = 32
BLOCKS = FF // D
EPS = 1e-05
PAIR = 2 * HEAD
PAIRS = D // PAIR
GROUP = 16
MASKED = -(2.0**30)
COST = 0.5
UPPER_MB = 50
BF = jnp.bfloat16
F32 = jnp.float32

SELF_ROWS, SELF_IN, SELF_OUT = 64, 0, 48
FFN_ROWS, FFN_IN, FFN_OUT = 128, 0, 64
CROSS_ROWS, CROSS_Q, CROSS_KV, CROSS_OUT = 64, 0, 16, 48


def nn(left, right):
    return lax.dot_general(left, right, (((1,), (0,)), ((), ())), preferred_element_type=F32)


def nt(left, right):
    return lax.dot_general(left, right, (((1,), (1,)), ((), ())), preferred_element_type=F32)


def wide(ref, start, block):
    first = start + 16 * block
    return ref[:, :, first : first + 16, :].reshape(D, D)


def tall(ref, start, block):
    return ref[4 * block : 4 * block + 4, :, start : start + 64, :].reshape(D, D)


def put_shards(core, refs, lead, rows, shards):
    if len(refs) == 1:
        refs[0][lead, :, rows, :] = shards.astype(BF)
        return
    refs[0][lead, rows, :] = jnp.where(core == 0, shards[:, 0], shards[:, 1]).astype(BF)
    piece = refs[1].shape[1]
    start = rows.start % piece
    refs[1 + rows.start // piece][lead, start : start + rows.stop - rows.start, :] = jnp.where(
        core == 0, shards[:, 1], shards[:, 0]
    ).astype(BF)


def put_wide(core, refs, start, block, value):
    rows = slice(start + 16 * block, start + 16 * block + 16)
    put_shards(core, refs, slice(0, SHARDS // 2), rows, value.reshape(SHARDS // 2, 2, 16, D))


def put_tall(core, refs, start, block, value):
    put_shards(core, refs, slice(4 * block, 4 * block + 4), slice(start, start + 64), value.reshape(4, 2, 64, D))


class Weights:
    def __init__(self, arrays, place, half):
        self.arrays = arrays
        self.place = place
        self.half = half


def weight_copies(pieces, place, half, core, ref, sems, low, high):
    if len(pieces) == 1:
        return [pltpu.make_async_copy(pieces[0].at[:, :, place + low : place + high, :], ref, sems.at[0])]
    copies = []
    for number in range(2):
        first, last = max(low, number * half), min(high, (number + 1) * half)
        if first < last:
            source = slice(place + first - number * half, place + last - number * half)
            for other in range(2):
                copies.append(
                    pltpu.make_async_copy(
                        pieces[2 * number + other].at[:, source, :],
                        ref.at[:, core if other == 0 else 1 - core, first - low : last - low, :],
                        sems.at[2 * number + other],
                    )
                )
    return copies


def on_first_slot(action, copies):
    @pl.when(pl.program_id(0) == 0)
    def _():
        for copy in copies:
            getattr(copy, action)()


def norm_grad_rows(ref, gains_and_shifts):
    rows = jnp.concatenate(gains_and_shifts + [jnp.zeros((8 - len(gains_and_shifts), D), F32)], 0)
    add_up(ref, rows)


def last_slot():
    return pl.program_id(0) == pl.num_programs(0) - 1


def lanes_of(pair):
    return slice(pair * PAIR, (pair + 1) * PAIR)


def normalize(values):
    centered = values - jnp.mean(values, -1, keepdims=True)
    scale = lax.rsqrt(jnp.mean(centered * centered, -1, keepdims=True) + EPS)
    return centered * scale, scale


def norm_backward(grad_normed, unit, scale, gain):
    grad_unit = grad_normed * gain
    first = jnp.mean(grad_unit, -1, keepdims=True)
    second = jnp.mean(grad_unit * unit, -1, keepdims=True)
    grad_gain = jnp.sum(grad_normed * unit, 0, keepdims=True)
    grad_shift = jnp.sum(grad_normed, 0, keepdims=True)
    return scale * (grad_unit - first - unit * second), grad_gain, grad_shift


def gelu_both(hidden):
    size = jnp.abs(hidden)
    ratio = 1.0 / (1.0 + (0.3275911 / math.sqrt(2.0)) * size)
    bell = jnp.exp(-0.5 * hidden * hidden)
    series = 0.5 * 1.061405429
    for factor in (-1.453152027, 1.421413741, -0.284496736, 0.254829592):
        series = series * ratio + 0.5 * factor
    tail = series * ratio * bell
    share = jnp.where(hidden >= 0, 1.0 - tail, tail)
    return hidden * share, share + hidden * bell * (1.0 / math.sqrt(2.0 * math.pi))


def lane_index():
    return lax.broadcasted_iota(jnp.int32, (1, 128), 1)


def query_extra(kind):
    place = lax.broadcasted_iota(jnp.int32, (SLOT, 128), 0)
    lane = lax.broadcasted_iota(jnp.int32, (SLOT, 128), 1)
    return (lax.shift_right_logical(place, kind + 7) == lane).astype(F32).astype(BF)


def key_extra(kind, lengths):
    place = lax.broadcasted_iota(jnp.int32, (SLOT, 128), 0)
    lane = lax.broadcasted_iota(jnp.int32, (SLOT, 128), 1)
    size = lax.shift_left(jnp.int32(128), kind)
    within = place & (size - 1)
    limit = jnp.where(
        lane == 0, lengths[0], jnp.where(lane == 1, lengths[1], jnp.where(lane == 2, lengths[2], lengths[3]))
    )
    allowed = (lax.shift_right_logical(place, kind + 7) == lane) & (within < limit)
    return jnp.where(allowed | (lane >= 4), 0.0, MASKED).astype(BF)


def halves():
    lane = lane_index()
    return ((lane < HEAD).astype(F32).astype(BF), (lane >= HEAD).astype(F32).astype(BF))


def future(rows, columns, first):
    row = lax.broadcasted_iota(jnp.int32, (rows, columns), 0)
    column = lax.broadcasted_iota(jnp.int32, (rows, columns), 1) + first
    return row <= column


def pipelined(items, ahead, start, finish):
    waiting = []
    for number, item in enumerate(items):
        while len(waiting) <= ahead and number + len(waiting) < len(items):
            waiting.append(start(*items[number + len(waiting)]))
        finish(*item, waiting.pop(0))


def attend(query_of, key_of, value_of, store, kind, lengths, causal):
    step = 256
    query_lanes = query_extra(kind)
    key_lanes = key_extra(kind, lengths)
    ones = jnp.ones((HEAD, SLOT), BF)
    mask = halves()
    inputs, parts, sums = {}, {}, {}

    def seen(first):
        return first + step if causal else SLOT

    def start(pair, half, first):
        if pair not in inputs:
            queries = query_of(pair) * BF(HEAD**-0.5)
            inputs[pair] = (queries, jnp.concatenate([key_of(pair), key_lanes], 1), value_of(pair).T)
        queries, keys, _ = inputs[pair]
        own = jnp.concatenate([queries[first : first + step] * mask[half], query_lanes[first : first + step]], 1)
        return nt(keys[: seen(first)], own)

    def finish(pair, half, first, scores):
        values = inputs[pair][2]
        if causal:
            scores = jnp.where(future(seen(first), step, first), scores, MASKED)
        largest = jnp.max(scores, 0, keepdims=True)
        powers = jnp.exp(scores - largest).astype(BF)
        head_values = jnp.concatenate([values[:HEAD], ones] if half == 0 else [ones, values[HEAD:]], 0)
        context = nn(head_values[:, : seen(first)], powers)
        total = context[HEAD : HEAD + 1] if half == 0 else context[0:1]
        parts[pair, half, first] = (context[:HEAD] if half == 0 else context[HEAD:]) * (1.0 / total)
        sums[pair, half, first] = largest + jnp.log(total)
        if half == 1 and first == SLOT - step:
            rows = [jnp.concatenate([parts[pair, side, at] for at in range(0, SLOT, step)], 1) for side in range(2)]
            store(pair, jnp.concatenate(rows, 0).T)

    items = [(pair, half, first) for pair in range(PAIRS) for half in range(2) for first in range(0, SLOT, step)]
    pipelined(items, 4, start, finish)
    spread = [
        jnp.broadcast_to(jnp.concatenate([sums[pair, half, at] for at in range(0, SLOT, step)], 1), (GROUP, SLOT))
        for pair in range(PAIRS)
        for half in range(2)
    ]
    return split(jnp.concatenate(spread, 0).T, 4)


def split(values, first):
    lane = lane_index() % GROUP
    high = values.astype(BF).astype(F32)
    rest = values - high
    middle = rest.astype(BF).astype(F32)
    low = rest - middle
    terms = jnp.where(
        lane == first, high, jnp.where(lane == first + 1, middle, jnp.where(lane == first + 2, low, 0.0))
    )
    return (-terms).astype(BF)


def attend_back(query_of, key_of, value_of, grad_of, contexts, grads, store, logsums, kind, lengths, causal):
    step = 256 if causal else SLOT
    query_lanes = query_extra(kind) + logsums
    key_lanes = key_extra(kind, lengths)
    products = grads.astype(F32) * contexts
    high = products.astype(BF)
    low = (products - high.astype(F32)).astype(BF)
    source = lax.broadcasted_iota(jnp.int32, (D, 128), 0) // HEAD
    target = lax.broadcasted_iota(jnp.int32, (D, 128), 1) // GROUP
    picker = (source == target).astype(F32).astype(BF)
    inner_lanes = split(nn(high, picker) + nn(low, picker), 0)
    lane = lane_index()
    within, group = lane % GROUP, lane // GROUP
    mask = halves()
    inputs, heads, results = {}, {}, {}

    def seen(first):
        return first + step if causal else SLOT

    def start(pair, half, first):
        if pair not in inputs:
            inputs[pair] = (query_of(pair) * BF(HEAD**-0.5), key_of(pair), value_of(pair), grad_of(pair), key_of(pair).T)
        queries, keys, values, grad_context, _ = inputs[pair]
        if (pair, half) not in heads:
            head = 2 * pair + half
            sum_lanes = ((group == head) & (within >= 4) & (within < 7)).astype(F32).astype(BF)
            one_lanes = ((group == head) & (within < 3)).astype(F32).astype(BF)
            heads[pair, half] = (
                jnp.concatenate([keys, key_lanes + sum_lanes], 1),
                jnp.concatenate([queries * mask[half], query_lanes], 1),
                jnp.concatenate([values, jnp.broadcast_to(one_lanes, (SLOT, 128))], 1),
                jnp.concatenate([grad_context * mask[half], inner_lanes], 1),
            )
        left, right, value_left, grad_right = heads[pair, half]
        here = slice(first, first + step)
        return nt(left[: seen(first)], right[here]), nt(value_left[: seen(first)], grad_right[here])

    def finish(pair, half, first, products):
        scores, grad_weights = products
        queries, _, _, grad_context, keys_t = inputs[pair]
        if causal:
            scores = jnp.where(future(seen(first), step, first), scores, MASKED)
        weights = jnp.exp(scores)
        grad_scores = (weights * grad_weights).astype(BF)
        here = slice(first, first + step)
        for_queries = nn(keys_t[half * HEAD : half * HEAD + HEAD, : seen(first)], grad_scores)
        for_keys = nn(grad_scores, queries[here] * mask[half])
        for_values = nn(weights.astype(BF), grad_context[here] * mask[half])
        if seen(first) < SLOT:
            none = jnp.zeros((SLOT - seen(first), PAIR), F32)
            for_keys = jnp.concatenate([for_keys, none], 0)
            for_values = jnp.concatenate([for_values, none], 0)
        results[pair, half, first] = (for_queries, for_keys, for_values)
        if half == 1 and first == SLOT - step:
            places = range(0, SLOT, step)
            rows = [jnp.concatenate([results[pair, side, at][0] for at in places], 1) for side in range(2)]
            keys_sum, values_sum = (
                functools.reduce(jnp.add, [results[pair, side, at][number] for side in range(2) for at in places])
                for number in (1, 2)
            )
            store(
                pair,
                (jnp.concatenate(rows, 0) * HEAD**-0.5).T.astype(BF),
                keys_sum.astype(BF),
                values_sum.astype(BF),
            )

    items = [(pair, half, first) for pair in range(PAIRS) for half in range(2) for first in range(0, SLOT, step)]
    pipelined(items, 2 if causal else 1, start, finish)


def lengths_at(ref, slot):
    return [ref[slot, entry] for entry in range(4)]


def at(ref, start):
    return lambda pair: ref[0, :, start + pair * PAIR : start + (pair + 1) * PAIR]


def add_up(ref, value):
    ref[...] = jnp.where(pl.program_id(0) == 0, 0.0, ref[...]) + value


def project_kernel(
    me_ref,
    x_refs,
    weights,
    norm_refs,
    qkv_refs,
    enc_ref,
    enc_sems,
    dec_ref,
    dec_sems,
    *,
    places,
    halves_of,
    slots,
):
    step = pl.program_id(0)
    held = ((enc_ref, enc_sems), (dec_ref, dec_sems))
    sides = []
    for side, (ref, sems) in enumerate(held):
        sides.append(
            weight_copies(
                weights[side], places[side], halves_of[side], me_ref[4], ref, sems, SELF_IN, SELF_OUT
            )
        )
    on_first_slot("start", sides[0] + sides[1])
    for side, (ref, _) in enumerate(held):

        @pl.when((step >= side * slots) & (step < (side + 1) * slots))
        def _(side=side, ref=ref):
            unit, _ = normalize(x_refs[side][0].astype(F32))
            normed = (unit * norm_refs[side][0:1] + norm_refs[side][1:2]).astype(BF)

            @pl.when(step == side * slots)
            def _():
                for copy in sides[side]:
                    copy.wait()

            for block in range(3):
                qkv_refs[side][0, :, block * D : (block + 1) * D] = nn(normed, wide(ref, 0, block)).astype(BF)


def keep_context(context_ref, rest_ref):
    def store(pair, context):
        high = context.astype(BF)
        context_ref[0, :, lanes_of(pair)] = high
        rest_ref[0, :, lanes_of(pair)] = (context - high.astype(F32)).astype(BF)

    return store


def self_attend_kernel(
    kind_ref,
    lengths_ref,
    me_ref,
    x_ref,
    qkv_ref,
    w,
    out_ref,
    context_ref,
    rest_ref,
    sums_ref,
    weights_ref,
    sems,
    *,
    place,
    half,
    causal,
):
    slot = pl.program_id(0)
    copies = weight_copies(w, place, half, me_ref[4], weights_ref, sems, SELF_OUT, SELF_ROWS)
    on_first_slot("start", copies)
    sums_ref[0] = attend(
        at(qkv_ref, 0),
        at(qkv_ref, D),
        at(qkv_ref, 2 * D),
        keep_context(context_ref, rest_ref),
        kind_ref[slot],
        lengths_at(lengths_ref, slot),
        causal,
    )
    on_first_slot("wait", copies)
    out_ref[0] = x_ref[0].astype(F32) + nn(context_ref[0], wide(weights_ref, 0, 0))


def ffn_forward_kernel(
    me_ref, r_ref, w, norm_ref, out_ref, active_ref, slope_ref, weights_ref, sems, *, place, half
):
    copies = weight_copies(w, place, half, me_ref[4], weights_ref, sems, 0, FFN_ROWS)
    on_first_slot("start", copies)
    values = r_ref[0]
    unit, _ = normalize(values)
    normed = (unit * norm_ref[2:3] + norm_ref[3:4]).astype(BF)
    totals = []
    on_first_slot("wait", copies)

    def finish(block, hidden):
        active, slope = gelu_both(hidden)
        active = active.astype(BF)
        active_ref[0, :, block * D : (block + 1) * D] = active
        slope_ref[0, :, block * D : (block + 1) * D] = slope.astype(BF)
        totals.append(nn(active, tall(weights_ref, FFN_OUT, block)))

    pipelined(
        [(block,) for block in range(BLOCKS)], 1, lambda block: nn(normed, wide(weights_ref, FFN_IN, block)), finish
    )
    total = functools.reduce(jnp.add, totals, values)
    out_ref[0] = total.astype(BF)


def ffn_back(grad_out, unit, scale, normed, gain, kept, w_ref, sums_ref):
    low = grad_out.astype(BF)
    normed_t = normed.T
    parts = []

    def start(block):
        return nt(low, tall(w_ref, FFN_OUT, block)), kept(block, False)

    def finish(block, products):
        grad_active, begun = products
        active, slope = kept(block, True) if begun is None else begun()
        grad_hidden = (grad_active * slope).astype(BF)
        add_up(sums_ref.at[1, block], nn(active.T, low))
        add_up(sums_ref.at[0, block], nn(normed_t, grad_hidden))
        parts.append(nt(grad_hidden, wide(w_ref, FFN_IN, block)))

    pipelined([(block,) for block in range(BLOCKS)], 1, start, finish)
    grad, grad_gain, grad_shift = norm_backward(functools.reduce(jnp.add, parts), unit, scale, gain)
    return grad_out + grad, grad_gain, grad_shift


def ffn_put(core, sums_ref, grads):
    @pl.when(last_slot())
    def _():
        for block in range(BLOCKS):
            put_wide(core, grads, FFN_IN, block, sums_ref[0, block])
            put_tall(core, grads, FFN_OUT, block, sums_ref[1, block])


def ffn_backward_kernel(
    me_ref,
    grad_out_ref,
    r_ref,
    active_ref,
    slope_ref,
    w,
    norm_ref,
    grad_ref,
    grads,
    norm_grad_ref,
    weights_ref,
    sems,
    sums_ref,
    *,
    place,
    half,
):
    copies = weight_copies(w, place, half, me_ref[4], weights_ref, sems, 0, FFN_ROWS)
    on_first_slot("start", copies)
    unit, scale = normalize(r_ref[0])
    gain = norm_ref[2:3]
    normed = (unit * gain + norm_ref[3:4]).astype(BF)
    on_first_slot("wait", copies)
    grad, grad_gain, grad_shift = ffn_back(
        grad_out_ref[0],
        unit,
        scale,
        normed,
        gain,
        lambda block, late: (
            (
                active_ref[0, :, block * D : (block + 1) * D],
                slope_ref[0, :, block * D : (block + 1) * D].astype(F32),
            )
            if late
            else None
        ),
        weights_ref,
        sums_ref,
    )
    grad_ref[0] = grad
    norm_grad_rows(norm_grad_ref, [grad_gain, grad_shift])
    ffn_put(me_ref[4], sums_ref, grads)


def attend_back_kernel(
    kind_ref,
    lengths_ref,
    me_ref,
    grad_out_ref,
    q_ref,
    kv_ref,
    context_ref,
    rest_ref,
    sums_in_ref,
    w,
    proj_ref,
    weights_ref,
    sems,
    low_ref,
    *,
    place,
    half,
    causal,
    start,
    key_at,
):
    slot = pl.program_id(0)
    copies = weight_copies(w, place, half, me_ref[4], weights_ref, sems, start, start + 16)
    on_first_slot("start", copies)
    on_first_slot("wait", copies)
    low_ref[0] = nt(grad_out_ref[0].astype(BF), wide(weights_ref, 0, 0)).astype(BF)

    def store(pair, grad_query, grad_key, grad_value):
        for number, value in enumerate((grad_query, grad_key, grad_value)):
            proj_ref[0, :, number * D + pair * PAIR : number * D + (pair + 1) * PAIR] = value

    attend_back(
        at(q_ref, 0),
        at(kv_ref, key_at),
        at(kv_ref, key_at + D),
        at(low_ref, 0),
        context_ref[0].astype(F32) + rest_ref[0].astype(F32),
        low_ref[0],
        store,
        sums_in_ref[0],
        kind_ref[slot],
        lengths_at(lengths_ref, slot),
        causal,
    )


def upper_kernel(
    kind_ref,
    lengths_ref,
    me_ref,
    r_ref,
    memory_ref,
    enc_cotangent_ref,
    dec_cotangent_ref,
    w_cross,
    w_ff,
    norm_ref,
    out_ref,
    grad_ref,
    memory_grad_ref,
    ff_grads,
    cross_grads,
    norm_grad_ref,
    cross_ref,
    cross_sems,
    ff_ref,
    ff_sems,
    qkv_ref,
    context_ref,
    low_ref,
    proj_ref,
    second_ref,
    ff_sums_ref,
    sums_ref,
    *,
    cross_place,
    cross_half,
    ff_place,
    ff_half,
):
    slot = pl.program_id(0)
    core = me_ref[4]
    copies = weight_copies(w_cross, cross_place, cross_half, core, cross_ref, cross_sems, 0, CROSS_ROWS)
    ff_copies = weight_copies(w_ff, ff_place, ff_half, core, ff_ref, ff_sems, 0, FFN_ROWS)
    on_first_slot("start", copies + ff_copies)
    kind, lengths = kind_ref[slot], lengths_at(lengths_ref, slot)
    unit, scale = normalize(r_ref[0])
    gain = norm_ref[2:3]
    normed = (unit * gain + norm_ref[3:4]).astype(BF)
    memory = memory_ref[0]
    on_first_slot("wait", copies)
    qkv_ref[0, :, :D] = nn(normed, wide(cross_ref, CROSS_Q, 0)).astype(BF)
    for block in range(2):
        qkv_ref[0, :, (block + 1) * D : (block + 2) * D] = nn(memory, wide(cross_ref, CROSS_KV, block)).astype(BF)

    def keep(pair, context):
        context_ref[:, lanes_of(pair)] = context

    logsums = attend(at(qkv_ref, 0), at(qkv_ref, D), at(qkv_ref, 2 * D), keep, kind, lengths, False)
    second = r_ref[0] + nn(context_ref[...].astype(BF), wide(cross_ref, CROSS_OUT, 0))

    ff_unit, ff_scale = normalize(second)
    ff_gain = norm_ref[4:5]
    ff_normed = (ff_unit * ff_gain + norm_ref[5:6]).astype(BF)
    on_first_slot("wait", ff_copies)
    totals = []

    def kept(block, _):
        hidden = nn(ff_normed, wide(ff_ref, FFN_IN, block))

        def rest():
            active, slope = gelu_both(hidden)
            active = active.astype(BF)
            totals.append(nn(active, tall(ff_ref, FFN_OUT, block)))
            return active, slope

        return rest

    grad_second, ff_gain_grad, ff_shift_grad = ffn_back(
        dec_cotangent_ref[0].astype(F32), ff_unit, ff_scale, ff_normed, ff_gain, kept, ff_ref, ff_sums_ref
    )
    out_ref[0] = functools.reduce(jnp.add, totals, second).astype(BF)
    second_ref[...] = grad_second

    low = second_ref[...].astype(BF)
    add_up(sums_ref.at[3], nn(context_ref[...].astype(BF).T, low))
    low_ref[0] = nt(low, wide(cross_ref, CROSS_OUT, 0)).astype(BF)

    def store(pair, grad_query, grad_key, grad_value):
        for number, value in enumerate((grad_query, grad_key, grad_value)):
            proj_ref[number, :, lanes_of(pair)] = value

    attend_back(
        at(qkv_ref, 0),
        at(qkv_ref, D),
        at(qkv_ref, 2 * D),
        at(low_ref, 0),
        context_ref[...],
        low_ref[0],
        store,
        logsums,
        kind,
        lengths,
        False,
    )
    unit, scale = normalize(r_ref[0])
    normed_t = (unit * gain + norm_ref[3:4]).astype(BF).T
    memory_t = memory_ref[0].T
    add_up(sums_ref.at[0], nn(normed_t, proj_ref[0]))
    add_up(sums_ref.at[1], nn(memory_t, proj_ref[1]))
    add_up(sums_ref.at[2], nn(memory_t, proj_ref[2]))
    memory_grad_ref[0] = (
        enc_cotangent_ref[0].astype(F32)
        + nt(proj_ref[1], wide(cross_ref, CROSS_KV, 0))
        + nt(proj_ref[2], wide(cross_ref, CROSS_KV, 1))
    )
    grad, grad_gain, grad_shift = norm_backward(nt(proj_ref[0], wide(cross_ref, CROSS_Q, 0)), unit, scale, gain)
    grad_ref[0] = second_ref[...] + grad
    norm_grad_rows(norm_grad_ref, [grad_gain, grad_shift, ff_gain_grad, ff_shift_grad])
    ffn_put(core, ff_sums_ref, ff_grads)

    @pl.when(last_slot())
    def _():
        put_wide(core, cross_grads, CROSS_Q, 0, sums_ref[0])
        put_wide(core, cross_grads, CROSS_KV, 0, sums_ref[1])
        put_wide(core, cross_grads, CROSS_KV, 1, sums_ref[2])
        put_wide(core, cross_grads, CROSS_OUT, 0, sums_ref[3])


def self_weight_kernel(
    me_ref, grad_out_ref, x_ref, context_ref, proj_ref, norm_ref, grads, sums_ref
):
    unit, _ = normalize(x_ref[0].astype(F32))
    normed_t = (unit * norm_ref[0:1] + norm_ref[1:2]).astype(BF).T
    for block in range(3):
        add_up(sums_ref.at[block], nn(normed_t, proj_ref[0, :, block * D : (block + 1) * D]))
    add_up(sums_ref.at[3], nn(context_ref[0].T, grad_out_ref[0].astype(BF)))

    @pl.when(last_slot())
    def _():
        core = me_ref[4]
        for block in range(3):
            put_wide(core, grads, SELF_IN, block, sums_ref[block])
        put_wide(core, grads, SELF_OUT, 0, sums_ref[3])


def self_rows_kernel(
    me_ref,
    grad_out_ref,
    x_ref,
    proj_ref,
    w,
    norm_ref,
    grad_ref,
    norm_grad_ref,
    weights_ref,
    sems,
    *,
    place,
    half,
):
    copies = weight_copies(w, place, half, me_ref[4], weights_ref, sems, SELF_IN, SELF_OUT)
    on_first_slot("start", copies)
    unit, scale = normalize(x_ref[0].astype(F32))
    on_first_slot("wait", copies)
    grad_normed = None
    for block in range(3):
        part = nt(proj_ref[0, :, block * D : (block + 1) * D], wide(weights_ref, 0, block))
        grad_normed = part if grad_normed is None else grad_normed + part
    grad, grad_gain, grad_shift = norm_backward(grad_normed, unit, scale, norm_ref[0:1])
    grad_ref[0] = (grad_out_ref[0] + grad).astype(BF)
    norm_grad_rows(norm_grad_ref, [grad_gain, grad_shift])


def per_slot(*shape):
    return pl.BlockSpec((1,) + shape, lambda slot: (slot,) + (0,) * len(shape))


def whole_block(*shape):
    return pl.BlockSpec(shape, lambda slot: (0,) * len(shape))


def scalars():
    return pl.BlockSpec(memory_space=pltpu.SMEM)


def in_place():
    return pl.BlockSpec(memory_space=pl.ANY)


def in_vmem():
    return pl.BlockSpec(memory_space=pltpu.VMEM)


class Order:
    def __init__(self):
        self.token = ()

    def call(self, kernel, name, steps, ins, outs, scratch, args, megabytes, us):
        leaf = lambda out: isinstance(out[0], pl.BlockSpec)
        shaped = lambda out: pltpu.HBM(*out[1:3]) if out[3:] else jax.ShapeDtypeStruct(*out[1:])
        specs = [out[0] if leaf(out) else tuple(part[0] for part in out) for out in outs]
        shapes = [shaped(out) if leaf(out) else tuple(shaped(part) for part in out) for out in outs]
        place = len(ins) + len(outs)

        def body(before, *refs):
            refs[place][...] = jnp.zeros((8, 128), F32)
            kernel(*refs[:place], *refs[place + 1 :])

        *results, token = pl.pallas_call(
            body,
            name=name,
            grid=(steps,),
            in_specs=[tuple(in_place() for _ in self.token)] + ins,
            out_specs=specs + [whole_block(8, 128)],
            out_shape=shapes + [jax.ShapeDtypeStruct((8, 128), F32)],
            scratch_shapes=scratch,
            cost_estimate=pl.CostEstimate(flops=int(COST * us * 1.15e9), bytes_accessed=1 << 16, transcendentals=0),
            compiler_params=pltpu.CompilerParams(
                vmem_limit_bytes=megabytes << 20, dimension_semantics=("arbitrary",)
            ),
        )(self.token, *args)
        self.token = (token,)
        return results


def slot_array(slots, width, dtype, to_hbm=False):
    return (per_slot(SLOT, width), (slots, SLOT, width), dtype) + (("hbm",) if to_hbm else ())


def stay(*arrays):
    return tuple(pltpu.with_memory_space_constraint(array, pltpu.HBM) for array in arrays)


def stay_own(weights):
    if len(weights.arrays) == 1:
        return stay(*weights.arrays)
    return tuple(stay(array)[0] if number % 2 == 0 else array for number, array in enumerate(weights.arrays))


def grad_group(rows, parted, pieces=1):
    def once(*shape):
        spec = pl.BlockSpec(shape, lambda slot: (0,) * len(shape), pipeline_mode=pl.Buffered(1))
        return (spec, shape, BF)

    if not parted:
        return (once(SHARDS // 2, 2, rows, D),)
    return (once(SHARDS // 2, rows, D),) + (once(SHARDS // 2, rows // pieces, D),) * pieces


NORM_GRADS = (whole_block(8, D), (8, D), F32)


def weight_scratch(rows):
    return [pltpu.VMEM((SHARDS // 2, 2, rows, D), BF), pltpu.SemaphoreType.DMA((4,))]


def bound(kernel, weights, **options):
    return functools.partial(kernel, place=weights.place, half=weights.half, **options)


def held(weights):
    return tuple(in_place() for _ in weights.arrays)


def project(order, me, rows, weights, norms):
    slots = rows[0].shape[0]

    def turn(side, width):
        first = side * slots
        return pl.BlockSpec(
            (1, SLOT, width), lambda step: (jnp.minimum(jnp.maximum(step - first, 0), slots - 1), 0, 0)
        )

    return order.call(
        functools.partial(
            project_kernel,
            places=tuple(part.place for part in weights),
            halves_of=tuple(part.half for part in weights),
            slots=slots,
        ),
        "project",
        2 * slots,
        [
            scalars(),
            tuple(turn(side, D) for side in range(2)),
            tuple(held(part) for part in weights),
            tuple(whole_block(*part.shape) for part in norms),
        ],
        [tuple((turn(side, 3 * D), (slots, SLOT, 3 * D), BF, "hbm") for side in range(2))],
        weight_scratch(SELF_OUT - SELF_IN) * 2,
        (me, stay(*rows), tuple(stay_own(part) for part in weights), tuple(norms)),
        20,
        8,
    )[0]


def self_attend(order, kinds, lengths, me, rows, qkv, weights, causal, name):
    slots = rows.shape[0]
    return order.call(
        bound(self_attend_kernel, weights, causal=causal),
        name,
        slots,
        [scalars(), scalars(), scalars(), per_slot(SLOT, D), per_slot(SLOT, 3 * D), held(weights)],
        [slot_array(slots, D, F32, True)] + [slot_array(slots, D, BF, True)] * 2 + [slot_array(slots, 128, BF, True)],
        weight_scratch(SELF_ROWS - SELF_OUT),
        (kinds, lengths, me, *stay(rows, qkv), stay_own(weights)),
        14,
        10,
    )


def ffn_forward(order, me, rows, weights, norms):
    slots = rows.shape[0]
    return order.call(
        bound(ffn_forward_kernel, weights),
        "ffn_forward",
        slots,
        [scalars(), per_slot(SLOT, D), held(weights), whole_block(*norms.shape)],
        [slot_array(slots, D, BF, True), slot_array(slots, FF, BF, True), slot_array(slots, FF, BF, True)],
        weight_scratch(FFN_ROWS),
        (me, *stay(rows), stay_own(weights), norms),
        24,
        16,
    )


def ffn_backward(order, me, grad_out, rows, active, slope, weights, norms, parted):
    slots = rows.shape[0]
    return order.call(
        bound(ffn_backward_kernel, weights),
        "ffn_backward",
        slots,
        [
            scalars(),
            per_slot(SLOT, D),
            per_slot(SLOT, D),
            per_slot(SLOT, FF),
            per_slot(SLOT, FF),
            held(weights),
            whole_block(*norms.shape),
        ],
        [slot_array(slots, D, F32), grad_group(FFN_ROWS, parted), NORM_GRADS],
        weight_scratch(FFN_ROWS) + [pltpu.VMEM((2, BLOCKS, D, D), F32)],
        (me, *stay(grad_out, rows, active, slope), stay_own(weights), norms),
        30,
        22,
    )


def attend_backward(order, kinds, lengths, me, grad_out, q, kv, kept, weights, causal, start, key_at, name):
    slots = grad_out.shape[0]
    return order.call(
        bound(attend_back_kernel, weights, causal=causal, start=start, key_at=key_at),
        name,
        slots,
        [scalars(), scalars(), scalars(), per_slot(SLOT, D)]
        + [per_slot(SLOT, part.shape[-1]) for part in (q, kv)]
        + [per_slot(SLOT, D), per_slot(SLOT, D), per_slot(SLOT, 128), held(weights)],
        [slot_array(slots, 3 * D, BF)],
        weight_scratch(16) + [pltpu.VMEM((1, SLOT, D), BF)],
        (kinds, lengths, me, grad_out, *stay(q, kv, *kept), stay_own(weights)),
        18,
        16,
    )[0]


def upper(order, kinds, lengths, me, rows, memory, enc_cotangent, dec_cotangent, w_cross, w_ff, norms, parted):
    slots = rows.shape[0]
    return order.call(
        functools.partial(
            upper_kernel, cross_place=w_cross.place, cross_half=w_cross.half, ff_place=w_ff.place, ff_half=w_ff.half
        ),
        "upper_decoder",
        slots,
        [scalars(), scalars(), scalars()]
        + [per_slot(SLOT, D)] * 4
        + [held(w_cross), held(w_ff), whole_block(*norms.shape)],
        [
            slot_array(slots, D, BF, True),
            slot_array(slots, D, F32),
            slot_array(slots, D, F32, True),
            grad_group(FFN_ROWS, parted),
            grad_group(CROSS_ROWS, parted),
            NORM_GRADS,
        ],
        weight_scratch(CROSS_ROWS)
        + weight_scratch(FFN_ROWS)
        + [
            pltpu.VMEM((1, SLOT, 3 * D), BF),
            pltpu.VMEM((SLOT, D), F32),
            pltpu.VMEM((1, SLOT, D), BF),
            pltpu.VMEM((3, SLOT, D), BF),
            pltpu.VMEM((SLOT, D), F32),
            pltpu.VMEM((2, BLOCKS, D, D), F32),
            pltpu.VMEM((4, D, D), F32),
        ],
        (
            kinds,
            lengths,
            me,
            *stay(rows, memory, enc_cotangent, dec_cotangent),
            stay_own(w_cross),
            stay_own(w_ff),
            norms,
        ),
        UPPER_MB,
        60,
    )


def self_weights(order, me, grad_out, rows, context, proj, norms, parted, name):
    slots = rows.shape[0]
    return order.call(
        self_weight_kernel,
        name,
        slots,
        [scalars()] + [per_slot(SLOT, D)] * 3 + [per_slot(SLOT, 3 * D), whole_block(*norms.shape)],
        [grad_group(SELF_ROWS, parted, 4)],
        [pltpu.VMEM((4, D, D), F32)],
        (me, grad_out, *stay(rows, context), proj, norms),
        14,
        8,
    )[0]


def self_rows(order, me, grad_out, rows, proj, weights, norms, name):
    slots = rows.shape[0]
    return order.call(
        bound(self_rows_kernel, weights),
        name,
        slots,
        [scalars(), per_slot(SLOT, D), per_slot(SLOT, D), per_slot(SLOT, 3 * D), held(weights), whole_block(*norms.shape)],
        [slot_array(slots, D, BF), NORM_GRADS],
        weight_scratch(SELF_OUT - SELF_IN),
        (me, *stay(grad_out, rows), proj, stay_own(weights), norms),
        16,
        7,
    )


def axis_sizes(mesh):
    dp, fsdp = mesh.shape["dp"], mesh.shape["fsdp"]
    core = 2 if fsdp % 2 == 0 else 1
    side = math.isqrt(dp)
    first, second = (side, side) if side * side == dp else (dp, 1)
    return (first, second, fsdp // core, core)


AXES = ("dp", "fsdp")
CUBE = (2, 2, 4, 2)
A_BIT, B_BIT, HIGH_BIT, LOW_BIT, CORE_BIT = 16, 8, 4, 2, 1


def swapped(values, bit):
    return lax.ppermute(values, AXES, [(device, device ^ bit) for device in range(SHARDS)])


def moved(values, sizes, axis, shift):
    stride = math.prod(sizes[axis + 1 :])
    pairs = []
    for device in range(math.prod(sizes)):
        place = device // stride % sizes[axis]
        pairs.append((device, device + ((place + shift) % sizes[axis] - place) * stride))
    return lax.ppermute(values, AXES, pairs)


def sum_everywhere(values, sizes):
    for axis in (3, 1, 0, 2):
        total = values
        for shift in range(1, sizes[axis]):
            total = total + moved(values, sizes, axis, shift)
        values = total
    return values


def packed(flat, rows, columns, devices):
    part = flat.reshape(rows // devices, columns // D, D)
    return jnp.swapaxes(part, 0, 1).reshape(-1, D)


def unpacked(part, rows, columns, devices):
    return jnp.swapaxes(part.reshape(columns // D, rows // devices, D), 0, 1).reshape(-1)


SELF_SHAPES = ((D, 3 * D), (D, D))
FFN_SHAPES = ((D, FF), (FF, D))
CROSS_SHAPES = ((D, D), (D, 2 * D), (D, D))


def rows_of(shapes, devices=SHARDS):
    return sum(rows * columns for rows, columns in shapes) // D // devices


def rows_in(groups):
    return sum(rows_of(shapes) for shapes in groups)


def join_copy_kernel(me_ref, sources, results, sems, *, plan):
    copies = []
    for result, (source, _, bit, axis) in zip(results, plan):
        for other, ref in enumerate(sources[source]):
            place = me_ref[bit] if other == 0 else 1 - me_ref[bit]
            target = result.at[place] if axis == 0 else result.at[:, place]
            copies.append(pltpu.make_async_copy(ref, target, sems.at[len(copies)]))
    for copy in copies:
        copy.start()
    for copy in copies:
        copy.wait()


def join_kernel(me_ref, sources, results, *, plan):
    for result, (source, rows, bit, axis) in zip(results, plan):
        for other, ref in enumerate(sources[source]):
            place = me_ref[bit] if other == 0 else 1 - me_ref[bit]
            if axis == 0:
                result[place] = ref[...]
            else:
                for lead in range(2):
                    result[lead, place] = ref[lead] if rows is None else ref[lead, rows]


def join(order, me, name, sources, plan, to_hbm=False):
    outs = []
    for source, rows, _, axis in plan:
        shape = sources[source][0].shape
        count = shape[-2] if rows is None else rows.stop - rows.start
        shape = (2, *shape[:-2], count, D) if axis == 0 else (shape[0], 2, *shape[1:-2], count, D)
        outs.append((in_place(), shape, BF, "hbm") if to_hbm else (in_vmem(), shape, BF))
    return order.call(
        functools.partial(join_copy_kernel if to_hbm else join_kernel, plan=plan),
        name,
        1,
        [scalars(), [(in_vmem(), in_vmem())] * len(sources)],
        [tuple(outs)],
        [pltpu.SemaphoreType.DMA((2 * len(plan),))] if to_hbm else [],
        (me, sources),
        20,
        1,
    )[0]


def pack_kernel(me_ref, flats, extra, out_ref, *scratch, plan):
    for flat, wide_ref, (rows, blocks, places) in zip(flats, scratch, plan):
        wide_ref[...] = flat[...].astype(F32)
        for block, place in enumerate(places):
            for chunk in range(4):
                part = wide_ref[pl.ds(4 * block + chunk, rows, stride=4 * blocks), :]
                out_ref[place : place + rows, 128 * chunk : 128 * chunk + 128] = part.astype(BF)
    if extra:
        place = out_ref.shape[0] - 16
        out_ref[place:, :] = jnp.broadcast_to(extra[0][...], (16, D))


def pack_groups(order, me, name, groups, extra):
    counts = [rows_of([shape for _, shape in group]) for group in groups]
    total = sum(counts)
    flats, plan, scratch, before = [], [], [], 0
    for group, count in zip(groups, counts):
        first = 0
        for flat, (rows, columns) in group:
            rows, blocks = rows // SHARDS, columns // D
            places = []
            for block in range(blocks):
                at = first + block * rows
                places.append(before + at if at < count // 2 else total // 2 + before + at - count // 2)
            first += rows * blocks
            flats.append(flat.reshape(-1, 128))
            plan.append((rows, blocks, tuple(places)))
            scratch.append(pltpu.VMEM((rows * blocks * 4, 128), F32))
        before += count // 2
    rows = total + (0 if extra is None else 16)
    return order.call(
        functools.partial(pack_kernel, plan=plan),
        name + "_pack",
        1,
        [
            scalars(),
            tuple(whole_block(*flat.shape) for flat in flats),
            () if extra is None else (whole_block(*extra.shape),),
        ],
        [(in_vmem(), (rows, D), BF)],
        scratch,
        (me, tuple(flats), () if extra is None else (extra,)),
        20,
        1,
    )[0]


def gather_cube(order, me, name, groups, spans, extra, results):
    halves_of = [rows_of([shape for _, shape in group]) // 2 for group in groups]
    count = sum(halves_of)
    values = pack_groups(order, me, name, groups, extra)
    total = values.shape[0]
    yield
    got = swapped(values, HIGH_BIT)
    yield
    (values,) = join(order, me, name + "_join_1", [(values, got)], [(0, None, 2, 0)])
    got = swapped(values, LOW_BIT)
    yield
    plan, members, place = [], [], 0
    for span in spans:
        members.append([halves_of.pop(0) for _ in range(span)])
        end = place + sum(members[-1])
        plan.append((0, slice(place, end), 3, 1))
        plan.append((0, slice(count + place, total if end == count else count + end), 3, 1))
        place = end
    parts = join(order, me, name + "_join_2", [(values, got)], plan)
    for number, held_halves in enumerate(members):
        last = extra is not None and number == len(members) - 1
        results.append(
            Exchange(
                lambda kept, number=number, held_halves=held_halves, last=last: gather_rest(
                    order, me, f"{name}_{number}", parts[2 * number], parts[2 * number + 1], held_halves, last, kept
                )
            )
        )
    yield


def gather_rest(order, me, name, one, two, halves_of, extra, results):
    got = swapped(one, B_BIT), swapped(two, A_BIT)
    yield
    one, two = join(
        order, me, name + "_join_3", [(one, got[0]), (two, got[1])], [(0, None, 1, 0), (1, None, 0, 0)]
    )
    got = swapped(one, A_BIT), swapped(two, B_BIT)
    yield
    one, two = join(
        order, me, name + "_join_4", [(one, got[0]), (two, got[1])], [(0, None, 0, 0), (1, None, 1, 1)], True
    )
    got = swapped(one, CORE_BIT), swapped(two, CORE_BIT)
    arrays = tuple(part.reshape(SHARDS // 2, -1, D) for part in (one, got[0], two, got[1]))
    place = 0
    for half in halves_of:
        results.append(Weights(arrays, place, half))
        place += half
    if extra:
        own, other = arrays[2][:, place], arrays[3][:, place]
        lines = jnp.where(me[4] == 0, jnp.stack([own, other], 1), jnp.stack([other, own], 1))
        results.append(lines.reshape(SHARDS, D))
    yield


def gather_plain(groups, spans, extra, devices, results):
    if devices == SHARDS:
        parts = [packed(flat, *shape, SHARDS) for group in groups for flat, shape in group]
        whole = lax.all_gather(jnp.concatenate(parts, 0), AXES, axis=0)
    else:
        parts = []
        for flat, shape in [pair for group in groups for pair in group]:
            full = lax.all_gather(flat, AXES, axis=0, tiled=True)
            full = full.reshape(SHARDS, shape[0] // SHARDS, shape[1] // D, D)
            parts.append(jnp.swapaxes(full, 1, 2).reshape(SHARDS, -1, D))
        whole = jnp.concatenate(parts, 1)
    whole = whole.reshape(SHARDS // 2, 2, -1, D)
    place, left = 0, list(groups)
    for span in spans:
        results.append(Exchange())
        for _ in range(span):
            count = rows_of([shape for _, shape in left.pop(0)])
            results[-1].results.append(Weights((whole,), place, count // 2))
            place += count
    if extra is not None:
        results[-1].results.append(lax.all_gather(extra[0], AXES, axis=0))


CARRIED = 48


def carry(ref, first, values):
    high = values.astype(BF).astype(F32)
    rest = values - high
    middle = rest.astype(BF).astype(F32)
    for number, term in enumerate((high, middle, rest - middle)):
        ref[first + 16 * number : first + 16 * number + 16, :] = term.astype(BF)


def carried(ref, first):
    terms = [ref[first + 16 * number : first + 16 * number + 16, :].astype(F32) for number in range(3)]
    return terms[0] + (terms[1] + terms[2])


def slab(ref, index, rows):
    return ref.at[pl.ds(pl.multiple_of(index * rows, rows), rows), :]


def first_sum_kernel(me_ref, keeps, gots, small, send_one, keep_one, send_two, keep_two, *small_out):
    a, b = me_ref[0], me_ref[1]
    total = keep_one.shape[0] // 8
    place = 0
    for keep, pieces in zip(keeps, gots):
        half = keep.shape[3] // 2
        size = min(pieces[0].shape[3], half)
        for first in range(0, 2 * half, size):
            got = pieces[first // pieces[0].shape[3]]
            at = first % pieces[0].shape[3]
            rows, source = slice(first, first + size), slice(at, at + size)
            here = place + first % half
            for other in range(2):
                for z in range(4):
                    target = slice((4 * other + z) * total + here, (4 * other + z) * total + here + size)
                    if first < half:
                        for ref, pick in ((send_one, 1 - b), (keep_one, b)):
                            ref[target] = keep[other, pick, z, rows] + got[other, pick, z, source]
                    else:
                        for ref, pick in ((send_two, 1 - a), (keep_two, a)):
                            ref[target] = keep[pick, other, z, rows] + got[pick, other, z, source]
        place += half
    if small:
        values = small[0][...] + small[1][...]
        small_out[0][...] = values
        carry(send_one, 8 * total, values)


def second_sum_kernel(me_ref, keep_one, got_one, keep_two, got_two, small, send_a, kept_a, send_b, kept_b, *small_out):
    a, b = me_ref[0], me_ref[1]
    rows = kept_a.shape[0]
    for keep, got, outs, mine in ((keep_one, got_one, (send_a, kept_a), a), (keep_two, got_two, (send_b, kept_b), b)):
        for ref, pick in zip(outs, (1 - mine, mine)):
            ref[:rows] = slab(keep, pick, rows)[...] + slab(got, pick, rows)[...]
    if small:
        values = small[0][...] + carried(got_one, 2 * rows)
        small_out[0][...] = values
        carry(send_a, rows, values)


def third_sum_kernel(me_ref, keep_one, got_one, keep_two, got_two, small, send, keep, *small_out):
    z = me_ref[3]
    half = keep_one.shape[0] // 4
    for high in range(2):
        for ref, pick in ((send, 1 - z), (keep, z)):
            first = 2 * high * half
            ref[first : first + half] = slab(keep_one, 2 * high + pick, half)[...] + slab(got_one, 2 * high + pick, half)[...]
            ref[first + half : first + 2 * half] = (
                slab(keep_two, 2 * high + pick, half)[...] + slab(got_two, 2 * high + pick, half)[...]
            )
    if small:
        values = small[0][...] + carried(got_one, 4 * half)
        small_out[0][...] = values
        carry(send, 4 * half, values)


def fourth_sum_kernel(me_ref, keep, got, small, send, kept, *small_out):
    z = me_ref[2]
    rows = kept.shape[0]
    for ref, pick in ((send, 1 - z), (kept, z)):
        ref[:rows] = slab(keep, pick, rows)[...] + slab(got, pick, rows)[...]
    if small:
        values = small[0][...] + carried(got, 2 * rows)
        small_out[0][...] = values
        carry(send, rows, values)


def scatter_cube(order, me, name, groups, small, results):
    got = [tuple(swapped(part, CORE_BIT) for part in pair[1:]) for pair, _ in groups]
    small = () if small is None else (small, swapped(small, CORE_BIT))
    extra = CARRIED if small else 0
    yield
    keeps = tuple(pair[0].reshape(2, 2, 4, -1, D) for pair, _ in groups)
    got = tuple(tuple(part.reshape(2, 2, 4, -1, D) for part in parts) for parts in got)
    half = sum(rows_of(shapes) for _, shapes in groups) // 2

    def call(kernel, number, rows, *args):
        outs = [(in_vmem(), (count, D), BF) for count in rows] + [(in_vmem(), (16, D), F32)] * bool(small)
        ins = jax.tree.map(lambda _: in_vmem(), list(args) + [small])
        parts = order.call(kernel, f"{name}_sum_{number}", 1, [scalars()] + ins, outs, [], (me, *args, small), 20, 1)
        return parts[: len(rows)], tuple(parts[len(rows) :])

    (send_one, keep_one, send_two, keep_two), small = call(
        first_sum_kernel, 1, (8 * half + extra, 8 * half, 8 * half, 8 * half), keeps, got
    )
    got = swapped(send_one, B_BIT), swapped(send_two, A_BIT)
    yield
    (send_one, keep_one, send_two, keep_two), small = call(
        second_sum_kernel, 2, (4 * half + extra, 4 * half, 4 * half, 4 * half), keep_one, got[0], keep_two, got[1]
    )
    got = swapped(send_one, A_BIT), swapped(send_two, B_BIT)
    yield
    (send, keep), small = call(
        third_sum_kernel, 3, (4 * half + extra, 4 * half), keep_one, got[0], keep_two, got[1]
    )
    got = swapped(send, LOW_BIT)
    yield
    (send, keep), small = call(fourth_sum_kernel, 4, (2 * half + extra, 2 * half), keep, got)
    last = (keep, swapped(send, HIGH_BIT))
    yield
    plan, outs, place = [], [], 0
    for _, shapes in groups:
        count, first = rows_of(shapes), 0
        for rows, columns in shapes:
            rows, blocks = rows // SHARDS, columns // D
            places = []
            for block in range(blocks):
                at = first + block * rows
                places.append(place + at if at < count // 2 else half + place + at - count // 2)
            first += rows * blocks
            plan.append((rows, blocks, tuple(places)))
            shape = (rows * blocks * 4, 128)
            outs.append((whole_block(*shape), shape, F32))
        place += count // 2
    flat, *sums = order.call(
        functools.partial(finish_kernel, plan=plan),
        name + "_finish",
        1,
        [scalars(), tuple(in_vmem() for _ in last), tuple(in_vmem() for _ in small)],
        [tuple(outs)] + [(in_vmem(), (16, D), F32)] * bool(small),
        [],
        (me, last, small),
        20,
        1,
    )
    results.extend(part.reshape(-1) for part in flat)
    results.extend(sums)
    yield


def finish_kernel(me_ref, parts, small, outs, *small_out, plan):
    for out, (rows, blocks, places) in zip(outs, plan):
        for block, place in enumerate(places):
            part = functools.reduce(jnp.add, [ref[place : place + rows, :].astype(F32) for ref in parts])
            for chunk in range(4):
                out[pl.ds(4 * block + chunk, rows, stride=4 * blocks), :] = part[:, 128 * chunk : 128 * chunk + 128]
    if small:
        small_out[0][...] = small[0][...] + carried(parts[1], parts[0].shape[0])


def unpack_group(rows, shapes):
    results, first = [], 0
    for shape in shapes:
        count = rows_of((shape,))
        results.append(unpacked(rows[first : first + count], *shape, SHARDS))
        first += count
    return results


def scatter_plain(grads, shapes, devices):
    if devices == SHARDS:
        own = lax.psum_scatter(grads.reshape(-1, D), AXES, scatter_dimension=0, tiled=True)
        return unpack_group(own.astype(F32), shapes)
    grads = grads.reshape(SHARDS, -1, D)
    results, first = [], 0
    for rows, columns in shapes:
        count = rows_of(((rows, columns),))
        part = grads[:, first : first + count].reshape(SHARDS, columns // D, rows // SHARDS, D)
        flat = jnp.swapaxes(part, 1, 2).reshape(devices, -1)
        results.append(lax.psum_scatter(flat, AXES, scatter_dimension=0, tiled=True).reshape(-1).astype(F32))
        first += count
    return results


class Exchange:
    def __init__(self, steps=None):
        self.results = []
        self.steps = None if steps is None else steps(self.results)

    def part(self, number):
        return self.results[number]

    def go(self, count=1):
        if self.steps is not None:
            for _ in range(count):
                next(self.steps)


def count_kernel(kind_ref, lengths_ref, ids_ref, out_ref, *, slots):
    totals = [jnp.zeros((1, 128), F32) for _ in range(8)]
    place = lax.broadcasted_iota(jnp.int32, (SLOT, 128), 0)
    lane = lax.broadcasted_iota(jnp.int32, (SLOT, 128), 1).astype(F32)
    for slot in range(slots):
        kind = kind_ref[slot]
        sequence = lax.shift_right_logical(place, kind + 7)
        within = place & (lax.shift_left(jnp.int32(128), kind) - 1)
        limit = jnp.zeros_like(place)
        for entry in range(4):
            limit = jnp.where(sequence == entry, lengths_ref[slot, entry], limit)
        ids = jnp.broadcast_to(ids_ref[slot : slot + 1].astype(F32), (128, SLOT)).T
        ids = jnp.where(within < limit, ids, -1.0)
        for chunk in range((VOCAB + 127) // 128):
            hits = jnp.where(ids == lane + 128.0 * chunk, 1.0, 0.0)
            totals[chunk] = totals[chunk] + jnp.sum(hits, 0, keepdims=True)
    out_ref[...] = jnp.concatenate([jnp.concatenate(totals[:4], 1), jnp.concatenate(totals[4:], 1)], 0)


def count_live(order, kinds, lengths, ids):
    slots = ids.shape[0]
    return order.call(
        functools.partial(count_kernel, slots=slots),
        "count",
        1,
        [scalars(), scalars(), in_vmem()],
        [(in_vmem(), (2, D), F32)],
        [],
        (kinds, lengths, ids),
        8,
        1,
    )[0]


def local(
    sizes,
    enc_in,
    dec_in,
    bucket,
    enc_lengths,
    dec_lengths,
    pred_ids,
    running_counts,
    enc_attn_in,
    enc_attn_out,
    enc_ff_in,
    enc_ff_out,
    enc_norms,
    dec_self_in,
    dec_self_out,
    dec_cross_q,
    dec_cross_kv,
    dec_cross_out,
    dec_ff_in,
    dec_ff_out,
    dec_norms,
    enc_cotangent,
    dec_cotangent,
):
    devices = math.prod(sizes)
    cube = sizes == CUBE
    index = lax.axis_index("dp") * lax.axis_size("fsdp") + lax.axis_index("fsdp")
    if cube:
        me = jnp.stack([index >> 4 & 1, index >> 3 & 1, index >> 2 & 1, index >> 1 & 1, index & 1]).astype(jnp.int32)
    else:
        me = jnp.zeros((5,), jnp.int32)

    order = Order()

    def gather(name, groups, spans, extra=None):
        if cube:
            return Exchange(lambda results: gather_cube(order, me, name, groups, spans, extra, results))
        exchange = Exchange()
        gather_plain(groups, spans, extra, devices, exchange.results)
        return exchange

    def scatter(name, *groups, small=None):
        if cube:
            return Exchange(lambda results: scatter_cube(order, me, name, groups, small, results))
        exchange = Exchange()
        for (grads,), shapes in groups:
            exchange.results.extend(scatter_plain(grads, shapes, devices))
        if small is not None:
            exchange.results.append(sum_everywhere(small, sizes))
        return exchange

    enc_count, dec_count = enc_norms.shape[0], dec_norms.shape[0]
    both = jnp.concatenate([enc_norms, dec_norms])
    norm_part = jnp.pad(both[None, :], ((0, 0), (0, D - both.shape[0])))
    enc_self_group = list(zip((enc_attn_in, enc_attn_out), SELF_SHAPES))
    dec_self_group = list(zip((dec_self_in, dec_self_out), SELF_SHAPES))
    enc_ff_group = list(zip((enc_ff_in, enc_ff_out), FFN_SHAPES))
    cross_group = list(zip((dec_cross_q, dec_cross_kv, dec_cross_out), CROSS_SHAPES))
    dec_ff_group = list(zip((dec_ff_in, dec_ff_out), FFN_SHAPES))
    first = gather("self", [dec_self_group, enc_self_group], [2], norm_part)
    ffn = gather("ffn", [enc_ff_group], [1])
    late = gather("late", [cross_group, dec_ff_group], [2])
    first.go(2)
    ffn.go()
    late.go()
    counted = count_live(order, bucket, dec_lengths, pred_ids)
    first.go(2)
    self_chain = first.part(0)
    self_chain.go()
    ffn.go(2)
    self_chain.go()
    late.go()
    ffn.go()
    ffn_chain = ffn.part(0)
    self_chain.go()
    ffn_chain.go()
    dec_self_w, enc_self_w, norm_lines = self_chain.results
    enc_norm = norm_lines[:, :enc_count].reshape(4, D).astype(F32)
    dec_norm = norm_lines[:, enc_count : enc_count + dec_count].reshape(6, D).astype(F32)

    enc_qkv, dec_qkv = project(order, me, (enc_in, dec_in), (enc_self_w, dec_self_w), (enc_norm, dec_norm))
    late.go()
    ffn_chain.go()
    attended, *enc_kept = self_attend(order, bucket, enc_lengths, me, enc_in, enc_qkv, enc_self_w, False, "enc_attend")
    late.go()
    late_chain = late.part(0)
    late_chain.go()
    ffn_chain.go()
    first_out, *dec_kept = self_attend(order, bucket, dec_lengths, me, dec_in, dec_qkv, dec_self_w, True, "dec_attend")
    late_chain.go()
    (enc_ff_w,) = ffn_chain.results
    memory, active, slope = ffn_forward(order, me, attended, enc_ff_w, enc_norm)
    late_chain.go()
    cross_w, dec_ff_w = late_chain.results
    decoded, grad_first, grad_memory, dec_ff_grads, cross_grads, upper_norm_g = upper(
        order,
        bucket,
        enc_lengths,
        me,
        first_out,
        memory,
        enc_cotangent,
        dec_cotangent,
        cross_w,
        dec_ff_w,
        dec_norm,
        cube,
    )
    fifth = scatter("dec", (dec_ff_grads, FFN_SHAPES), (cross_grads, CROSS_SHAPES))
    fifth.go()
    grad_attended, enc_ff_grads, enc_ffn_norm_g = ffn_backward(
        order, me, grad_memory, attended, active, slope, enc_ff_w, enc_norm, cube
    )
    fifth.go()
    enc_proj = attend_backward(
        order,
        bucket,
        enc_lengths,
        me,
        grad_attended,
        enc_qkv,
        enc_qkv,
        enc_kept,
        enc_self_w,
        False,
        SELF_OUT,
        D,
        "enc_attend_back",
    )
    fifth.go()
    enc_self_grads = self_weights(
        order, me, grad_attended, enc_in, enc_kept[0], enc_proj, enc_norm, cube, "enc_self_weights"
    )
    sixth = scatter("enc", (enc_ff_grads, FFN_SHAPES), (enc_self_grads, SELF_SHAPES))
    sixth.go()
    dec_proj = attend_backward(
        order,
        bucket,
        dec_lengths,
        me,
        grad_first,
        dec_qkv,
        dec_qkv,
        dec_kept,
        dec_self_w,
        True,
        SELF_OUT,
        D,
        "dec_attend_back",
    )
    fifth.go()
    sixth.go()
    grad_enc_in, enc_self_norm_g = self_rows(
        order, me, grad_attended, enc_in, enc_proj, enc_self_w, enc_norm, "enc_self_rows"
    )
    fifth.go()
    grad_dec_in, dec_self_norm_g = self_rows(order, me, grad_first, dec_in, dec_proj, dec_self_w, dec_norm, "dec_self_rows")
    sixth.go()
    small = jnp.concatenate(
        [enc_self_norm_g[:2], enc_ffn_norm_g[:2], dec_self_norm_g[:2], upper_norm_g[:4], counted, jnp.zeros((4, D), F32)],
        0,
    )
    dec_self_grads = self_weights(
        order, me, grad_first, dec_in, dec_kept[0], dec_proj, dec_norm, cube, "dec_self_weights"
    )
    seventh = scatter("self", (dec_self_grads, SELF_SHAPES), small=small)
    seventh.go()
    fifth.go()
    sixth.go()
    seventh.go()
    sixth.go()
    seventh.go()
    seventh.go()
    sixth.go()
    seventh.go()
    seventh.go()
    dec_ff_in_g, dec_ff_out_g, cross_q_g, cross_kv_g, cross_out_g = fifth.results
    enc_ff_in_g, enc_ff_out_g, enc_attn_in_g, enc_attn_out_g = sixth.results
    dec_self_in_g, dec_self_out_g, small = seventh.results

    enc_norm_own = lax.dynamic_slice(small[:4].reshape(-1), (index * enc_count,), (enc_count,))
    dec_norm_own = lax.dynamic_slice(small[4:10].reshape(-1), (index * dec_count,), (dec_count,))
    counts = running_counts + small[10:12].reshape(-1)[:VOCAB].astype(jnp.int32)
    return (
        memory,
        decoded,
        grad_enc_in,
        grad_dec_in,
        enc_attn_in_g,
        enc_attn_out_g,
        enc_ff_in_g,
        enc_ff_out_g,
        enc_norm_own,
        dec_self_in_g,
        dec_self_out_g,
        cross_q_g,
        cross_kv_g,
        cross_out_g,
        dec_ff_in_g,
        dec_ff_out_g,
        dec_norm_own,
        counts,
    )


def solution(mesh):
    rows = P(AXES, None, None)
    pair = P(AXES, None)
    flat = P(AXES)
    return jax.shard_map(
        functools.partial(local, axis_sizes(mesh)),
        mesh=mesh,
        in_specs=(rows, rows, flat, pair, pair, pair, P()) + (flat,) * 13 + (rows, rows),
        out_specs=(rows,) * 4 + (flat,) * 13 + (P(),),
        check_vma=False,
    )
```

```python
import functools
import math
import jax
import jax.numpy as jnp
from jax import lax
from jax.experimental import pallas as pl
from jax.experimental.pallas import tpu as pltpu
from jax.sharding import PartitionSpec as P

D = 512
HEAD = 64
FF = 2048
VOCAB = 523
SLOT = 512
SHARDS = 32
BLOCKS = FF // D
EPS = 1e-05
PAIR = 2 * HEAD
PAIRS = D // PAIR
GROUP = 16
MASKED = -(2.0**30)
COST = 0.5
UPPER_MB = 50
BF = jnp.bfloat16
F32 = jnp.float32

SELF_ROWS, SELF_IN, SELF_OUT = 64, 0, 48
FFN_ROWS, FFN_IN, FFN_OUT = 128, 0, 64
CROSS_ROWS, CROSS_Q, CROSS_KV, CROSS_OUT = 64, 0, 16, 48


def nn(left, right):
    return lax.dot_general(left, right, (((1,), (0,)), ((), ())), preferred_element_type=F32)


def nt(left, right):
    return lax.dot_general(left, right, (((1,), (1,)), ((), ())), preferred_element_type=F32)


def wide(ref, start, block):
    first = start + 16 * block
    return ref[:, :, first : first + 16, :].reshape(D, D)


def tall(ref, start, block):
    return ref[4 * block : 4 * block + 4, :, start : start + 64, :].reshape(D, D)


def put_shards(core, refs, lead, rows, shards):
    if len(refs) == 1:
        refs[0][lead, :, rows, :] = shards.astype(BF)
        return
    refs[0][lead, rows, :] = jnp.where(core == 0, shards[:, 0], shards[:, 1]).astype(BF)
    piece = refs[1].shape[1]
    start = rows.start % piece
    refs[1 + rows.start // piece][lead, start : start + rows.stop - rows.start, :] = jnp.where(
        core == 0, shards[:, 1], shards[:, 0]
    ).astype(BF)


def put_wide(core, refs, start, block, value):
    rows = slice(start + 16 * block, start + 16 * block + 16)
    put_shards(core, refs, slice(0, SHARDS // 2), rows, value.reshape(SHARDS // 2, 2, 16, D))


def put_tall(core, refs, start, block, value):
    put_shards(core, refs, slice(4 * block, 4 * block + 4), slice(start, start + 64), value.reshape(4, 2, 64, D))


class Weights:
    def __init__(self, arrays, place, half):
        self.arrays = arrays
        self.place = place
        self.half = half


def weight_copies(pieces, place, half, core, ref, sems, low, high):
    if len(pieces) == 1:
        return [pltpu.make_async_copy(pieces[0].at[:, :, place + low : place + high, :], ref, sems.at[0])]
    copies = []
    for number in range(2):
        first, last = max(low, number * half), min(high, (number + 1) * half)
        if first < last:
            source = slice(place + first - number * half, place + last - number * half)
            for other in range(2):
                copies.append(
                    pltpu.make_async_copy(
                        pieces[2 * number + other].at[:, source, :],
                        ref.at[:, core if other == 0 else 1 - core, first - low : last - low, :],
                        sems.at[2 * number + other],
                    )
                )
    return copies


def on_first_slot(action, copies):
    @pl.when(pl.program_id(0) == 0)
    def _():
        for copy in copies:
            getattr(copy, action)()


def norm_grad_rows(ref, gains_and_shifts):
    rows = jnp.concatenate(gains_and_shifts + [jnp.zeros((8 - len(gains_and_shifts), D), F32)], 0)
    add_up(ref, rows)


def last_slot():
    return pl.program_id(0) == pl.num_programs(0) - 1


def lanes_of(pair):
    return slice(pair * PAIR, (pair + 1) * PAIR)


def normalize(values):
    centered = values - jnp.mean(values, -1, keepdims=True)
    scale = lax.rsqrt(jnp.mean(centered * centered, -1, keepdims=True) + EPS)
    return centered * scale, scale


def norm_backward(grad_normed, unit, scale, gain):
    grad_unit = grad_normed * gain
    first = jnp.mean(grad_unit, -1, keepdims=True)
    second = jnp.mean(grad_unit * unit, -1, keepdims=True)
    grad_gain = jnp.sum(grad_normed * unit, 0, keepdims=True)
    grad_shift = jnp.sum(grad_normed, 0, keepdims=True)
    return scale * (grad_unit - first - unit * second), grad_gain, grad_shift


def gelu_both(hidden):
    size = jnp.abs(hidden)
    ratio = 1.0 / (1.0 + (0.3275911 / math.sqrt(2.0)) * size)
    bell = jnp.exp(-0.5 * hidden * hidden)
    series = 0.5 * 1.061405429
    for factor in (-1.453152027, 1.421413741, -0.284496736, 0.254829592):
        series = series * ratio + 0.5 * factor
    tail = series * ratio * bell
    share = jnp.where(hidden >= 0, 1.0 - tail, tail)
    return hidden * share, share + hidden * bell * (1.0 / math.sqrt(2.0 * math.pi))


def lane_index():
    return lax.broadcasted_iota(jnp.int32, (1, 128), 1)


def query_extra(kind):
    place = lax.broadcasted_iota(jnp.int32, (SLOT, 128), 0)
    lane = lax.broadcasted_iota(jnp.int32, (SLOT, 128), 1)
    return (lax.shift_right_logical(place, kind + 7) == lane).astype(F32).astype(BF)


def key_extra(kind, lengths):
    place = lax.broadcasted_iota(jnp.int32, (SLOT, 128), 0)
    lane = lax.broadcasted_iota(jnp.int32, (SLOT, 128), 1)
    size = lax.shift_left(jnp.int32(128), kind)
    within = place & (size - 1)
    limit = jnp.where(
        lane == 0, lengths[0], jnp.where(lane == 1, lengths[1], jnp.where(lane == 2, lengths[2], lengths[3]))
    )
    allowed = (lax.shift_right_logical(place, kind + 7) == lane) & (within < limit)
    return jnp.where(allowed | (lane >= 4), 0.0, MASKED).astype(BF)


def halves():
    lane = lane_index()
    return ((lane < HEAD).astype(F32).astype(BF), (lane >= HEAD).astype(F32).astype(BF))


def future(rows, columns, first):
    row = lax.broadcasted_iota(jnp.int32, (rows, columns), 0)
    column = lax.broadcasted_iota(jnp.int32, (rows, columns), 1) + first
    return row <= column


def pipelined(items, ahead, start, finish):
    waiting = []
    for number, item in enumerate(items):
        while len(waiting) <= ahead and number + len(waiting) < len(items):
            waiting.append(start(*items[number + len(waiting)]))
        finish(*item, waiting.pop(0))


def attend(query_of, key_of, value_of, store, kind, lengths, causal):
    step = 256
    query_lanes = query_extra(kind)
    key_lanes = key_extra(kind, lengths)
    ones = jnp.ones((HEAD, SLOT), BF)
    mask = halves()
    inputs, parts, sums = {}, {}, {}

    def seen(first):
        return first + step if causal else SLOT

    def start(pair, half, first):
        if pair not in inputs:
            queries = query_of(pair) * BF(HEAD**-0.5)
            inputs[pair] = (queries, jnp.concatenate([key_of(pair), key_lanes], 1), value_of(pair).T)
        queries, keys, _ = inputs[pair]
        own = jnp.concatenate([queries[first : first + step] * mask[half], query_lanes[first : first + step]], 1)
        return nt(keys[: seen(first)], own)

    def finish(pair, half, first, scores):
        values = inputs[pair][2]
        if causal:
            scores = jnp.where(future(seen(first), step, first), scores, MASKED)
        largest = jnp.max(scores, 0, keepdims=True)
        powers = jnp.exp(scores - largest).astype(BF)
        head_values = jnp.concatenate([values[:HEAD], ones] if half == 0 else [ones, values[HEAD:]], 0)
        context = nn(head_values[:, : seen(first)], powers)
        total = context[HEAD : HEAD + 1] if half == 0 else context[0:1]
        parts[pair, half, first] = (context[:HEAD] if half == 0 else context[HEAD:]) * (1.0 / total)
        sums[pair, half, first] = largest + jnp.log(total)
        if half == 1 and first == SLOT - step:
            rows = [jnp.concatenate([parts[pair, side, at] for at in range(0, SLOT, step)], 1) for side in range(2)]
            store(pair, jnp.concatenate(rows, 0).T)

    items = [(pair, half, first) for pair in range(PAIRS) for half in range(2) for first in range(0, SLOT, step)]
    pipelined(items, 4, start, finish)
    spread = [
        jnp.broadcast_to(jnp.concatenate([sums[pair, half, at] for at in range(0, SLOT, step)], 1), (GROUP, SLOT))
        for pair in range(PAIRS)
        for half in range(2)
    ]
    return split(jnp.concatenate(spread, 0).T, 4)


def split(values, first):
    lane = lane_index() % GROUP
    high = values.astype(BF).astype(F32)
    rest = values - high
    middle = rest.astype(BF).astype(F32)
    low = rest - middle
    terms = jnp.where(
        lane == first, high, jnp.where(lane == first + 1, middle, jnp.where(lane == first + 2, low, 0.0))
    )
    return (-terms).astype(BF)


def attend_back(query_of, key_of, value_of, grad_of, contexts, grads, store, logsums, kind, lengths, causal):
    step = 256 if causal else SLOT
    query_lanes = query_extra(kind) + logsums
    key_lanes = key_extra(kind, lengths)
    products = grads.astype(F32) * contexts
    high = products.astype(BF)
    low = (products - high.astype(F32)).astype(BF)
    source = lax.broadcasted_iota(jnp.int32, (D, 128), 0) // HEAD
    target = lax.broadcasted_iota(jnp.int32, (D, 128), 1) // GROUP
    picker = (source == target).astype(F32).astype(BF)
    inner_lanes = split(nn(high, picker) + nn(low, picker), 0)
    lane = lane_index()
    within, group = lane % GROUP, lane // GROUP
    mask = halves()
    inputs, heads, results = {}, {}, {}

    def seen(first):
        return first + step if causal else SLOT

    def start(pair, half, first):
        if pair not in inputs:
            inputs[pair] = (query_of(pair) * BF(HEAD**-0.5), key_of(pair), value_of(pair), grad_of(pair), key_of(pair).T)
        queries, keys, values, grad_context, _ = inputs[pair]
        if (pair, half) not in heads:
            head = 2 * pair + half
            sum_lanes = ((group == head) & (within >= 4) & (within < 7)).astype(F32).astype(BF)
            one_lanes = ((group == head) & (within < 3)).astype(F32).astype(BF)
            heads[pair, half] = (
                jnp.concatenate([keys, key_lanes + sum_lanes], 1),
                jnp.concatenate([queries * mask[half], query_lanes], 1),
                jnp.concatenate([values, jnp.broadcast_to(one_lanes, (SLOT, 128))], 1),
                jnp.concatenate([grad_context * mask[half], inner_lanes], 1),
            )
        left, right, value_left, grad_right = heads[pair, half]
        here = slice(first, first + step)
        return nt(left[: seen(first)], right[here]), nt(value_left[: seen(first)], grad_right[here])

    def finish(pair, half, first, products):
        scores, grad_weights = products
        queries, _, _, grad_context, keys_t = inputs[pair]
        if causal:
            scores = jnp.where(future(seen(first), step, first), scores, MASKED)
        weights = jnp.exp(scores)
        grad_scores = (weights * grad_weights).astype(BF)
        here = slice(first, first + step)
        for_queries = nn(keys_t[half * HEAD : half * HEAD + HEAD, : seen(first)], grad_scores)
        for_keys = nn(grad_scores, queries[here] * mask[half])
        for_values = nn(weights.astype(BF), grad_context[here] * mask[half])
        if seen(first) < SLOT:
            none = jnp.zeros((SLOT - seen(first), PAIR), F32)
            for_keys = jnp.concatenate([for_keys, none], 0)
            for_values = jnp.concatenate([for_values, none], 0)
        results[pair, half, first] = (for_queries, for_keys, for_values)
        if half == 1 and first == SLOT - step:
            places = range(0, SLOT, step)
            rows = [jnp.concatenate([results[pair, side, at][0] for at in places], 1) for side in range(2)]
            keys_sum, values_sum = (
                functools.reduce(jnp.add, [results[pair, side, at][number] for side in range(2) for at in places])
                for number in (1, 2)
            )
            store(
                pair,
                (jnp.concatenate(rows, 0) * HEAD**-0.5).T.astype(BF),
                keys_sum.astype(BF),
                values_sum.astype(BF),
            )

    items = [(pair, half, first) for pair in range(PAIRS) for half in range(2) for first in range(0, SLOT, step)]
    pipelined(items, 2 if causal else 1, start, finish)


def lengths_at(ref, slot):
    return [ref[slot, entry] for entry in range(4)]


def at(ref, start):
    return lambda pair: ref[0, :, start + pair * PAIR : start + (pair + 1) * PAIR]


def add_up(ref, value):
    ref[...] = jnp.where(pl.program_id(0) == 0, 0.0, ref[...]) + value


def project_kernel(
    me_ref,
    x_refs,
    weights,
    norm_refs,
    qkv_refs,
    enc_ref,
    enc_sems,
    dec_ref,
    dec_sems,
    *,
    places,
    halves_of,
    slots,
):
    step = pl.program_id(0)
    held = ((enc_ref, enc_sems), (dec_ref, dec_sems))
    sides = []
    for side, (ref, sems) in enumerate(held):
        sides.append(
            weight_copies(
                weights[side], places[side], halves_of[side], me_ref[4], ref, sems, SELF_IN, SELF_OUT
            )
        )
    on_first_slot("start", sides[0] + sides[1])
    for side, (ref, _) in enumerate(held):

        @pl.when((step >= side * slots) & (step < (side + 1) * slots))
        def _(side=side, ref=ref):
            unit, _ = normalize(x_refs[side][0].astype(F32))
            normed = (unit * norm_refs[side][0:1] + norm_refs[side][1:2]).astype(BF)

            @pl.when(step == side * slots)
            def _():
                for copy in sides[side]:
                    copy.wait()

            for block in range(3):
                qkv_refs[side][0, :, block * D : (block + 1) * D] = nn(normed, wide(ref, 0, block)).astype(BF)


def keep_context(context_ref, rest_ref):
    def store(pair, context):
        high = context.astype(BF)
        context_ref[0, :, lanes_of(pair)] = high
        rest_ref[0, :, lanes_of(pair)] = (context - high.astype(F32)).astype(BF)

    return store


def self_attend_kernel(
    kind_ref,
    lengths_ref,
    me_ref,
    x_ref,
    qkv_ref,
    w,
    out_ref,
    context_ref,
    rest_ref,
    sums_ref,
    weights_ref,
    sems,
    *,
    place,
    half,
    causal,
):
    slot = pl.program_id(0)
    copies = weight_copies(w, place, half, me_ref[4], weights_ref, sems, SELF_OUT, SELF_ROWS)
    on_first_slot("start", copies)
    sums_ref[0] = attend(
        at(qkv_ref, 0),
        at(qkv_ref, D),
        at(qkv_ref, 2 * D),
        keep_context(context_ref, rest_ref),
        kind_ref[slot],
        lengths_at(lengths_ref, slot),
        causal,
    )
    on_first_slot("wait", copies)
    out_ref[0] = x_ref[0].astype(F32) + nn(context_ref[0], wide(weights_ref, 0, 0))


def ffn_forward_kernel(
    me_ref, r_ref, w, norm_ref, out_ref, active_ref, slope_ref, weights_ref, sems, *, place, half
):
    copies = weight_copies(w, place, half, me_ref[4], weights_ref, sems, 0, FFN_ROWS)
    on_first_slot("start", copies)
    values = r_ref[0]
    unit, _ = normalize(values)
    normed = (unit * norm_ref[2:3] + norm_ref[3:4]).astype(BF)
    totals = []
    on_first_slot("wait", copies)

    def finish(block, hidden):
        active, slope = gelu_both(hidden)
        active = active.astype(BF)
        active_ref[0, :, block * D : (block + 1) * D] = active
        slope_ref[0, :, block * D : (block + 1) * D] = slope.astype(BF)
        totals.append(nn(active, tall(weights_ref, FFN_OUT, block)))

    pipelined(
        [(block,) for block in range(BLOCKS)], 1, lambda block: nn(normed, wide(weights_ref, FFN_IN, block)), finish
    )
    total = functools.reduce(jnp.add, totals, values)
    out_ref[0] = total.astype(BF)


def ffn_back(grad_out, unit, scale, normed, gain, kept, w_ref, sums_ref):
    low = grad_out.astype(BF)
    normed_t = normed.T
    parts = []

    def start(block):
        return nt(low, tall(w_ref, FFN_OUT, block)), kept(block, False)

    def finish(block, products):
        grad_active, begun = products
        active, slope = kept(block, True) if begun is None else begun()
        grad_hidden = (grad_active * slope).astype(BF)
        add_up(sums_ref.at[1, block], nn(active.T, low))
        add_up(sums_ref.at[0, block], nn(normed_t, grad_hidden))
        parts.append(nt(grad_hidden, wide(w_ref, FFN_IN, block)))

    pipelined([(block,) for block in range(BLOCKS)], 1, start, finish)
    grad, grad_gain, grad_shift = norm_backward(functools.reduce(jnp.add, parts), unit, scale, gain)
    return grad_out + grad, grad_gain, grad_shift


def ffn_put(core, sums_ref, grads):
    @pl.when(last_slot())
    def _():
        for block in range(BLOCKS):
            put_wide(core, grads, FFN_IN, block, sums_ref[0, block])
            put_tall(core, grads, FFN_OUT, block, sums_ref[1, block])


def ffn_backward_kernel(
    me_ref,
    grad_out_ref,
    r_ref,
    active_ref,
    slope_ref,
    w,
    norm_ref,
    grad_ref,
    grads,
    norm_grad_ref,
    weights_ref,
    sems,
    sums_ref,
    *,
    place,
    half,
):
    copies = weight_copies(w, place, half, me_ref[4], weights_ref, sems, 0, FFN_ROWS)
    on_first_slot("start", copies)
    unit, scale = normalize(r_ref[0])
    gain = norm_ref[2:3]
    normed = (unit * gain + norm_ref[3:4]).astype(BF)
    on_first_slot("wait", copies)
    grad, grad_gain, grad_shift = ffn_back(
        grad_out_ref[0],
        unit,
        scale,
        normed,
        gain,
        lambda block, late: (
            (
                active_ref[0, :, block * D : (block + 1) * D],
                slope_ref[0, :, block * D : (block + 1) * D].astype(F32),
            )
            if late
            else None
        ),
        weights_ref,
        sums_ref,
    )
    grad_ref[0] = grad
    norm_grad_rows(norm_grad_ref, [grad_gain, grad_shift])
    ffn_put(me_ref[4], sums_ref, grads)


def attend_back_kernel(
    kind_ref,
    lengths_ref,
    me_ref,
    grad_out_ref,
    q_ref,
    kv_ref,
    context_ref,
    rest_ref,
    sums_in_ref,
    w,
    proj_ref,
    weights_ref,
    sems,
    low_ref,
    *,
    place,
    half,
    causal,
    start,
    key_at,
):
    slot = pl.program_id(0)
    copies = weight_copies(w, place, half, me_ref[4], weights_ref, sems, start, start + 16)
    on_first_slot("start", copies)
    on_first_slot("wait", copies)
    low_ref[0] = nt(grad_out_ref[0].astype(BF), wide(weights_ref, 0, 0)).astype(BF)

    def store(pair, grad_query, grad_key, grad_value):
        for number, value in enumerate((grad_query, grad_key, grad_value)):
            proj_ref[0, :, number * D + pair * PAIR : number * D + (pair + 1) * PAIR] = value

    attend_back(
        at(q_ref, 0),
        at(kv_ref, key_at),
        at(kv_ref, key_at + D),
        at(low_ref, 0),
        context_ref[0].astype(F32) + rest_ref[0].astype(F32),
        low_ref[0],
        store,
        sums_in_ref[0],
        kind_ref[slot],
        lengths_at(lengths_ref, slot),
        causal,
    )


def upper_kernel(
    kind_ref,
    lengths_ref,
    me_ref,
    r_ref,
    memory_ref,
    enc_cotangent_ref,
    dec_cotangent_ref,
    w_cross,
    w_ff,
    norm_ref,
    out_ref,
    grad_ref,
    memory_grad_ref,
    ff_grads,
    cross_grads,
    norm_grad_ref,
    cross_ref,
    cross_sems,
    ff_ref,
    ff_sems,
    qkv_ref,
    context_ref,
    low_ref,
    proj_ref,
    second_ref,
    ff_sums_ref,
    sums_ref,
    *,
    cross_place,
    cross_half,
    ff_place,
    ff_half,
):
    slot = pl.program_id(0)
    core = me_ref[4]
    copies = weight_copies(w_cross, cross_place, cross_half, core, cross_ref, cross_sems, 0, CROSS_ROWS)
    ff_copies = weight_copies(w_ff, ff_place, ff_half, core, ff_ref, ff_sems, 0, FFN_ROWS)
    on_first_slot("start", copies + ff_copies)
    kind, lengths = kind_ref[slot], lengths_at(lengths_ref, slot)
    unit, scale = normalize(r_ref[0])
    gain = norm_ref[2:3]
    normed = (unit * gain + norm_ref[3:4]).astype(BF)
    memory = memory_ref[0]
    on_first_slot("wait", copies)
    qkv_ref[0, :, :D] = nn(normed, wide(cross_ref, CROSS_Q, 0)).astype(BF)
    for block in range(2):
        qkv_ref[0, :, (block + 1) * D : (block + 2) * D] = nn(memory, wide(cross_ref, CROSS_KV, block)).astype(BF)

    def keep(pair, context):
        context_ref[:, lanes_of(pair)] = context

    logsums = attend(at(qkv_ref, 0), at(qkv_ref, D), at(qkv_ref, 2 * D), keep, kind, lengths, False)
    second = r_ref[0] + nn(context_ref[...].astype(BF), wide(cross_ref, CROSS_OUT, 0))

    ff_unit, ff_scale = normalize(second)
    ff_gain = norm_ref[4:5]
    ff_normed = (ff_unit * ff_gain + norm_ref[5:6]).astype(BF)
    on_first_slot("wait", ff_copies)
    totals = []

    def kept(block, _):
        hidden = nn(ff_normed, wide(ff_ref, FFN_IN, block))

        def rest():
            active, slope = gelu_both(hidden)
            active = active.astype(BF)
            totals.append(nn(active, tall(ff_ref, FFN_OUT, block)))
            return active, slope

        return rest

    grad_second, ff_gain_grad, ff_shift_grad = ffn_back(
        dec_cotangent_ref[0].astype(F32), ff_unit, ff_scale, ff_normed, ff_gain, kept, ff_ref, ff_sums_ref
    )
    out_ref[0] = functools.reduce(jnp.add, totals, second).astype(BF)
    second_ref[...] = grad_second

    low = second_ref[...].astype(BF)
    add_up(sums_ref.at[3], nn(context_ref[...].astype(BF).T, low))
    low_ref[0] = nt(low, wide(cross_ref, CROSS_OUT, 0)).astype(BF)

    def store(pair, grad_query, grad_key, grad_value):
        for number, value in enumerate((grad_query, grad_key, grad_value)):
            proj_ref[number, :, lanes_of(pair)] = value

    attend_back(
        at(qkv_ref, 0),
        at(qkv_ref, D),
        at(qkv_ref, 2 * D),
        at(low_ref, 0),
        context_ref[...],
        low_ref[0],
        store,
        logsums,
        kind,
        lengths,
        False,
    )
    unit, scale = normalize(r_ref[0])
    normed_t = (unit * gain + norm_ref[3:4]).astype(BF).T
    memory_t = memory_ref[0].T
    add_up(sums_ref.at[0], nn(normed_t, proj_ref[0]))
    add_up(sums_ref.at[1], nn(memory_t, proj_ref[1]))
    add_up(sums_ref.at[2], nn(memory_t, proj_ref[2]))
    memory_grad_ref[0] = (
        enc_cotangent_ref[0].astype(F32)
        + nt(proj_ref[1], wide(cross_ref, CROSS_KV, 0))
        + nt(proj_ref[2], wide(cross_ref, CROSS_KV, 1))
    )
    grad, grad_gain, grad_shift = norm_backward(nt(proj_ref[0], wide(cross_ref, CROSS_Q, 0)), unit, scale, gain)
    grad_ref[0] = second_ref[...] + grad
    norm_grad_rows(norm_grad_ref, [grad_gain, grad_shift, ff_gain_grad, ff_shift_grad])
    ffn_put(core, ff_sums_ref, ff_grads)

    @pl.when(last_slot())
    def _():
        put_wide(core, cross_grads, CROSS_Q, 0, sums_ref[0])
        put_wide(core, cross_grads, CROSS_KV, 0, sums_ref[1])
        put_wide(core, cross_grads, CROSS_KV, 1, sums_ref[2])
        put_wide(core, cross_grads, CROSS_OUT, 0, sums_ref[3])


def self_weight_kernel(
    me_ref, grad_out_ref, x_ref, context_ref, proj_ref, norm_ref, grads, sums_ref
):
    unit, _ = normalize(x_ref[0].astype(F32))
    normed_t = (unit * norm_ref[0:1] + norm_ref[1:2]).astype(BF).T
    for block in range(3):
        add_up(sums_ref.at[block], nn(normed_t, proj_ref[0, :, block * D : (block + 1) * D]))
    add_up(sums_ref.at[3], nn(context_ref[0].T, grad_out_ref[0].astype(BF)))

    @pl.when(last_slot())
    def _():
        core = me_ref[4]
        for block in range(3):
            put_wide(core, grads, SELF_IN, block, sums_ref[block])
        put_wide(core, grads, SELF_OUT, 0, sums_ref[3])


def self_rows_kernel(
    me_ref,
    grad_out_ref,
    x_ref,
    proj_ref,
    w,
    norm_ref,
    grad_ref,
    norm_grad_ref,
    weights_ref,
    sems,
    *,
    place,
    half,
):
    copies = weight_copies(w, place, half, me_ref[4], weights_ref, sems, SELF_IN, SELF_OUT)
    on_first_slot("start", copies)
    unit, scale = normalize(x_ref[0].astype(F32))
    on_first_slot("wait", copies)
    grad_normed = None
    for block in range(3):
        part = nt(proj_ref[0, :, block * D : (block + 1) * D], wide(weights_ref, 0, block))
        grad_normed = part if grad_normed is None else grad_normed + part
    grad, grad_gain, grad_shift = norm_backward(grad_normed, unit, scale, norm_ref[0:1])
    grad_ref[0] = (grad_out_ref[0] + grad).astype(BF)
    norm_grad_rows(norm_grad_ref, [grad_gain, grad_shift])


def per_slot(*shape):
    return pl.BlockSpec((1,) + shape, lambda slot: (slot,) + (0,) * len(shape))


def whole_block(*shape):
    return pl.BlockSpec(shape, lambda slot: (0,) * len(shape))


def scalars():
    return pl.BlockSpec(memory_space=pltpu.SMEM)


def in_place():
    return pl.BlockSpec(memory_space=pl.ANY)


def in_vmem():
    return pl.BlockSpec(memory_space=pltpu.VMEM)


class Order:
    def __init__(self):
        self.token = ()

    def call(self, kernel, name, steps, ins, outs, scratch, args, megabytes, us):
        leaf = lambda out: isinstance(out[0], pl.BlockSpec)
        shaped = lambda out: pltpu.HBM(*out[1:3]) if out[3:] else jax.ShapeDtypeStruct(*out[1:])
        specs = [out[0] if leaf(out) else tuple(part[0] for part in out) for out in outs]
        shapes = [shaped(out) if leaf(out) else tuple(shaped(part) for part in out) for out in outs]
        place = len(ins) + len(outs)

        def body(before, *refs):
            refs[place][...] = jnp.zeros((8, 128), F32)
            kernel(*refs[:place], *refs[place + 1 :])

        *results, token = pl.pallas_call(
            body,
            name=name,
            grid=(steps,),
            in_specs=[tuple(in_place() for _ in self.token)] + ins,
            out_specs=specs + [whole_block(8, 128)],
            out_shape=shapes + [jax.ShapeDtypeStruct((8, 128), F32)],
            scratch_shapes=scratch,
            cost_estimate=pl.CostEstimate(flops=int(COST * us * 1.15e9), bytes_accessed=1 << 16, transcendentals=0),
            compiler_params=pltpu.CompilerParams(
                vmem_limit_bytes=megabytes << 20, dimension_semantics=("arbitrary",)
            ),
        )(self.token, *args)
        self.token = (token,)
        return results


def slot_array(slots, width, dtype, to_hbm=False):
    return (per_slot(SLOT, width), (slots, SLOT, width), dtype) + (("hbm",) if to_hbm else ())


def stay(*arrays):
    return tuple(pltpu.with_memory_space_constraint(array, pltpu.HBM) for array in arrays)


def stay_own(weights):
    if len(weights.arrays) == 1:
        return stay(*weights.arrays)
    return tuple(stay(array)[0] if number % 2 == 0 else array for number, array in enumerate(weights.arrays))


def grad_group(rows, parted, pieces=1):
    def once(*shape):
        spec = pl.BlockSpec(shape, lambda slot: (0,) * len(shape), pipeline_mode=pl.Buffered(1))
        return (spec, shape, BF)

    if not parted:
        return (once(SHARDS // 2, 2, rows, D),)
    return (once(SHARDS // 2, rows, D),) + (once(SHARDS // 2, rows // pieces, D),) * pieces


NORM_GRADS = (whole_block(8, D), (8, D), F32)


def weight_scratch(rows):
    return [pltpu.VMEM((SHARDS // 2, 2, rows, D), BF), pltpu.SemaphoreType.DMA((4,))]


def bound(kernel, weights, **options):
    return functools.partial(kernel, place=weights.place, half=weights.half, **options)


def held(weights):
    return tuple(in_place() for _ in weights.arrays)


def project(order, me, rows, weights, norms):
    slots = rows[0].shape[0]

    def turn(side, width):
        first = side * slots
        return pl.BlockSpec(
            (1, SLOT, width), lambda step: (jnp.minimum(jnp.maximum(step - first, 0), slots - 1), 0, 0)
        )

    return order.call(
        functools.partial(
            project_kernel,
            places=tuple(part.place for part in weights),
            halves_of=tuple(part.half for part in weights),
            slots=slots,
        ),
        "project",
        2 * slots,
        [
            scalars(),
            tuple(turn(side, D) for side in range(2)),
            tuple(held(part) for part in weights),
            tuple(whole_block(*part.shape) for part in norms),
        ],
        [tuple((turn(side, 3 * D), (slots, SLOT, 3 * D), BF, "hbm") for side in range(2))],
        weight_scratch(SELF_OUT - SELF_IN) * 2,
        (me, stay(*rows), tuple(stay_own(part) for part in weights), tuple(norms)),
        20,
        8,
    )[0]


def self_attend(order, kinds, lengths, me, rows, qkv, weights, causal, name):
    slots = rows.shape[0]
    return order.call(
        bound(self_attend_kernel, weights, causal=causal),
        name,
        slots,
        [scalars(), scalars(), scalars(), per_slot(SLOT, D), per_slot(SLOT, 3 * D), held(weights)],
        [slot_array(slots, D, F32, True)] + [slot_array(slots, D, BF, True)] * 2 + [slot_array(slots, 128, BF, True)],
        weight_scratch(SELF_ROWS - SELF_OUT),
        (kinds, lengths, me, *stay(rows, qkv), stay_own(weights)),
        14,
        10,
    )


def ffn_forward(order, me, rows, weights, norms):
    slots = rows.shape[0]
    return order.call(
        bound(ffn_forward_kernel, weights),
        "ffn_forward",
        slots,
        [scalars(), per_slot(SLOT, D), held(weights), whole_block(*norms.shape)],
        [slot_array(slots, D, BF, True), slot_array(slots, FF, BF, True), slot_array(slots, FF, BF, True)],
        weight_scratch(FFN_ROWS),
        (me, *stay(rows), stay_own(weights), norms),
        24,
        16,
    )


def ffn_backward(order, me, grad_out, rows, active, slope, weights, norms, parted):
    slots = rows.shape[0]
    return order.call(
        bound(ffn_backward_kernel, weights),
        "ffn_backward",
        slots,
        [
            scalars(),
            per_slot(SLOT, D),
            per_slot(SLOT, D),
            per_slot(SLOT, FF),
            per_slot(SLOT, FF),
            held(weights),
            whole_block(*norms.shape),
        ],
        [slot_array(slots, D, F32), grad_group(FFN_ROWS, parted), NORM_GRADS],
        weight_scratch(FFN_ROWS) + [pltpu.VMEM((2, BLOCKS, D, D), F32)],
        (me, *stay(grad_out, rows, active, slope), stay_own(weights), norms),
        30,
        22,
    )


def attend_backward(order, kinds, lengths, me, grad_out, q, kv, kept, weights, causal, start, key_at, name):
    slots = grad_out.shape[0]
    return order.call(
        bound(attend_back_kernel, weights, causal=causal, start=start, key_at=key_at),
        name,
        slots,
        [scalars(), scalars(), scalars(), per_slot(SLOT, D)]
        + [per_slot(SLOT, part.shape[-1]) for part in (q, kv)]
        + [per_slot(SLOT, D), per_slot(SLOT, D), per_slot(SLOT, 128), held(weights)],
        [slot_array(slots, 3 * D, BF)],
        weight_scratch(16) + [pltpu.VMEM((1, SLOT, D), BF)],
        (kinds, lengths, me, grad_out, *stay(q, kv, *kept), stay_own(weights)),
        18,
        16,
    )[0]


def upper(order, kinds, lengths, me, rows, memory, enc_cotangent, dec_cotangent, w_cross, w_ff, norms, parted):
    slots = rows.shape[0]
    return order.call(
        functools.partial(
            upper_kernel, cross_place=w_cross.place, cross_half=w_cross.half, ff_place=w_ff.place, ff_half=w_ff.half
        ),
        "upper_decoder",
        slots,
        [scalars(), scalars(), scalars()]
        + [per_slot(SLOT, D)] * 4
        + [held(w_cross), held(w_ff), whole_block(*norms.shape)],
        [
            slot_array(slots, D, BF, True),
            slot_array(slots, D, F32),
            slot_array(slots, D, F32, True),
            grad_group(FFN_ROWS, parted),
            grad_group(CROSS_ROWS, parted),
            NORM_GRADS,
        ],
        weight_scratch(CROSS_ROWS)
        + weight_scratch(FFN_ROWS)
        + [
            pltpu.VMEM((1, SLOT, 3 * D), BF),
            pltpu.VMEM((SLOT, D), F32),
            pltpu.VMEM((1, SLOT, D), BF),
            pltpu.VMEM((3, SLOT, D), BF),
            pltpu.VMEM((SLOT, D), F32),
            pltpu.VMEM((2, BLOCKS, D, D), F32),
            pltpu.VMEM((4, D, D), F32),
        ],
        (
            kinds,
            lengths,
            me,
            *stay(rows, memory, enc_cotangent, dec_cotangent),
            stay_own(w_cross),
            stay_own(w_ff),
            norms,
        ),
        UPPER_MB,
        60,
    )


def self_weights(order, me, grad_out, rows, context, proj, norms, parted, name):
    slots = rows.shape[0]
    return order.call(
        self_weight_kernel,
        name,
        slots,
        [scalars()] + [per_slot(SLOT, D)] * 3 + [per_slot(SLOT, 3 * D), whole_block(*norms.shape)],
        [grad_group(SELF_ROWS, parted, 4)],
        [pltpu.VMEM((4, D, D), F32)],
        (me, grad_out, *stay(rows, context), proj, norms),
        14,
        8,
    )[0]


def self_rows(order, me, grad_out, rows, proj, weights, norms, name):
    slots = rows.shape[0]
    return order.call(
        bound(self_rows_kernel, weights),
        name,
        slots,
        [scalars(), per_slot(SLOT, D), per_slot(SLOT, D), per_slot(SLOT, 3 * D), held(weights), whole_block(*norms.shape)],
        [slot_array(slots, D, BF), NORM_GRADS],
        weight_scratch(SELF_OUT - SELF_IN),
        (me, *stay(grad_out, rows), proj, stay_own(weights), norms),
        16,
        7,
    )


def axis_sizes(mesh):
    dp, fsdp = mesh.shape["dp"], mesh.shape["fsdp"]
    core = 2 if fsdp % 2 == 0 else 1
    side = math.isqrt(dp)
    first, second = (side, side) if side * side == dp else (dp, 1)
    return (first, second, fsdp // core, core)


AXES = ("dp", "fsdp")
CUBE = (2, 2, 4, 2)
A_BIT, B_BIT, HIGH_BIT, LOW_BIT, CORE_BIT = 16, 8, 4, 2, 1


def swapped(values, bit):
    return lax.ppermute(values, AXES, [(device, device ^ bit) for device in range(SHARDS)])


def moved(values, sizes, axis, shift):
    stride = math.prod(sizes[axis + 1 :])
    pairs = []
    for device in range(math.prod(sizes)):
        place = device // stride % sizes[axis]
        pairs.append((device, device + ((place + shift) % sizes[axis] - place) * stride))
    return lax.ppermute(values, AXES, pairs)


def sum_everywhere(values, sizes):
    for axis in (3, 1, 0, 2):
        total = values
        for shift in range(1, sizes[axis]):
            total = total + moved(values, sizes, axis, shift)
        values = total
    return values


def packed(flat, rows, columns, devices):
    part = flat.reshape(rows // devices, columns // D, D)
    return jnp.swapaxes(part, 0, 1).reshape(-1, D)


def unpacked(part, rows, columns, devices):
    return jnp.swapaxes(part.reshape(columns // D, rows // devices, D), 0, 1).reshape(-1)


SELF_SHAPES = ((D, 3 * D), (D, D))
FFN_SHAPES = ((D, FF), (FF, D))
CROSS_SHAPES = ((D, D), (D, 2 * D), (D, D))


def rows_of(shapes, devices=SHARDS):
    return sum(rows * columns for rows, columns in shapes) // D // devices


def rows_in(groups):
    return sum(rows_of(shapes) for shapes in groups)


def join_copy_kernel(me_ref, sources, results, sems, *, plan):
    copies = []
    for result, (source, _, bit, axis) in zip(results, plan):
        for other, ref in enumerate(sources[source]):
            place = me_ref[bit] if other == 0 else 1 - me_ref[bit]
            target = result.at[place] if axis == 0 else result.at[:, place]
            copies.append(pltpu.make_async_copy(ref, target, sems.at[len(copies)]))
    for copy in copies:
        copy.start()
    for copy in copies:
        copy.wait()


def join_kernel(me_ref, sources, results, *, plan):
    for result, (source, rows, bit, axis) in zip(results, plan):
        for other, ref in enumerate(sources[source]):
            place = me_ref[bit] if other == 0 else 1 - me_ref[bit]
            if axis == 0:
                result[place] = ref[...]
            else:
                for lead in range(2):
                    result[lead, place] = ref[lead] if rows is None else ref[lead, rows]


def join(order, me, name, sources, plan, to_hbm=False):
    outs = []
    for source, rows, _, axis in plan:
        shape = sources[source][0].shape
        count = shape[-2] if rows is None else rows.stop - rows.start
        shape = (2, *shape[:-2], count, D) if axis == 0 else (shape[0], 2, *shape[1:-2], count, D)
        outs.append((in_place(), shape, BF, "hbm") if to_hbm else (in_vmem(), shape, BF))
    return order.call(
        functools.partial(join_copy_kernel if to_hbm else join_kernel, plan=plan),
        name,
        1,
        [scalars(), [(in_vmem(), in_vmem())] * len(sources)],
        [tuple(outs)],
        [pltpu.SemaphoreType.DMA((2 * len(plan),))] if to_hbm else [],
        (me, sources),
        20,
        1,
    )[0]


def pack_kernel(me_ref, flats, extra, out_ref, *scratch, plan):
    for flat, wide_ref, (rows, blocks, places) in zip(flats, scratch, plan):
        wide_ref[...] = flat[...].astype(F32)
        for block, place in enumerate(places):
            for chunk in range(4):
                part = wide_ref[pl.ds(4 * block + chunk, rows, stride=4 * blocks), :]
                out_ref[place : place + rows, 128 * chunk : 128 * chunk + 128] = part.astype(BF)
    if extra:
        place = out_ref.shape[0] - 16
        out_ref[place:, :] = jnp.broadcast_to(extra[0][...], (16, D))


def pack_groups(order, me, name, groups, extra):
    counts = [rows_of([shape for _, shape in group]) for group in groups]
    total = sum(counts)
    flats, plan, scratch, before = [], [], [], 0
    for group, count in zip(groups, counts):
        first = 0
        for flat, (rows, columns) in group:
            rows, blocks = rows // SHARDS, columns // D
            places = []
            for block in range(blocks):
                at = first + block * rows
                places.append(before + at if at < count // 2 else total // 2 + before + at - count // 2)
            first += rows * blocks
            flats.extend(stay(flat.reshape(-1, 128)))
            plan.append((rows, blocks, tuple(places)))
            scratch.append(pltpu.VMEM((rows * blocks * 4, 128), F32))
        before += count // 2
    rows = total + (0 if extra is None else 16)
    return order.call(
        functools.partial(pack_kernel, plan=plan),
        name + "_pack",
        1,
        [
            scalars(),
            tuple(whole_block(*flat.shape) for flat in flats),
            () if extra is None else (whole_block(*extra.shape),),
        ],
        [(in_vmem(), (rows, D), BF)],
        scratch,
        (me, tuple(flats), () if extra is None else (extra,)),
        20,
        1,
    )[0]


def gather_cube(order, me, name, groups, spans, extra, results):
    halves_of = [rows_of([shape for _, shape in group]) // 2 for group in groups]
    count = sum(halves_of)
    values = pack_groups(order, me, name, groups, extra)
    total = values.shape[0]
    yield
    got = swapped(values, HIGH_BIT)
    yield
    (values,) = join(order, me, name + "_join_1", [(values, got)], [(0, None, 2, 0)])
    got = swapped(values, LOW_BIT)
    yield
    plan, members, place = [], [], 0
    for span in spans:
        members.append([halves_of.pop(0) for _ in range(span)])
        end = place + sum(members[-1])
        plan.append((0, slice(place, end), 3, 1))
        plan.append((0, slice(count + place, total if end == count else count + end), 3, 1))
        place = end
    parts = join(order, me, name + "_join_2", [(values, got)], plan)
    for number, held_halves in enumerate(members):
        last = extra is not None and number == len(members) - 1
        results.append(
            Exchange(
                lambda kept, number=number, held_halves=held_halves, last=last: gather_rest(
                    order, me, f"{name}_{number}", parts[2 * number], parts[2 * number + 1], held_halves, last, kept
                )
            )
        )
    yield


def gather_rest(order, me, name, one, two, halves_of, extra, results):
    got = swapped(one, B_BIT), swapped(two, A_BIT)
    yield
    one, two = join(
        order, me, name + "_join_3", [(one, got[0]), (two, got[1])], [(0, None, 1, 0), (1, None, 0, 0)]
    )
    got = swapped(one, A_BIT), swapped(two, B_BIT)
    yield
    one, two = join(
        order, me, name + "_join_4", [(one, got[0]), (two, got[1])], [(0, None, 0, 0), (1, None, 1, 1)], True
    )
    got = swapped(one, CORE_BIT), swapped(two, CORE_BIT)
    arrays = tuple(part.reshape(SHARDS // 2, -1, D) for part in (one, got[0], two, got[1]))
    place = 0
    for half in halves_of:
        results.append(Weights(arrays, place, half))
        place += half
    if extra:
        own, other = arrays[2][:, place], arrays[3][:, place]
        lines = jnp.where(me[4] == 0, jnp.stack([own, other], 1), jnp.stack([other, own], 1))
        results.append(lines.reshape(SHARDS, D))
    yield


def gather_plain(groups, spans, extra, devices, results):
    if devices == SHARDS:
        parts = [packed(flat, *shape, SHARDS) for group in groups for flat, shape in group]
        whole = lax.all_gather(jnp.concatenate(parts, 0), AXES, axis=0)
    else:
        parts = []
        for flat, shape in [pair for group in groups for pair in group]:
            full = lax.all_gather(flat, AXES, axis=0, tiled=True)
            full = full.reshape(SHARDS, shape[0] // SHARDS, shape[1] // D, D)
            parts.append(jnp.swapaxes(full, 1, 2).reshape(SHARDS, -1, D))
        whole = jnp.concatenate(parts, 1)
    whole = whole.reshape(SHARDS // 2, 2, -1, D)
    place, left = 0, list(groups)
    for span in spans:
        results.append(Exchange())
        for _ in range(span):
            count = rows_of([shape for _, shape in left.pop(0)])
            results[-1].results.append(Weights((whole,), place, count // 2))
            place += count
    if extra is not None:
        results[-1].results.append(lax.all_gather(extra[0], AXES, axis=0))


CARRIED = 48


def carry(ref, first, values):
    high = values.astype(BF).astype(F32)
    rest = values - high
    middle = rest.astype(BF).astype(F32)
    for number, term in enumerate((high, middle, rest - middle)):
        ref[first + 16 * number : first + 16 * number + 16, :] = term.astype(BF)


def carried(ref, first):
    terms = [ref[first + 16 * number : first + 16 * number + 16, :].astype(F32) for number in range(3)]
    return terms[0] + (terms[1] + terms[2])


def slab(ref, index, rows):
    return ref.at[pl.ds(pl.multiple_of(index * rows, rows), rows), :]


def first_sum_kernel(me_ref, keeps, gots, small, send_one, keep_one, send_two, keep_two, *small_out):
    a, b = me_ref[0], me_ref[1]
    total = keep_one.shape[0] // 8
    place = 0
    for keep, pieces in zip(keeps, gots):
        half = keep.shape[3] // 2
        size = min(pieces[0].shape[3], half)
        for first in range(0, 2 * half, size):
            got = pieces[first // pieces[0].shape[3]]
            at = first % pieces[0].shape[3]
            rows, source = slice(first, first + size), slice(at, at + size)
            here = place + first % half
            for other in range(2):
                for z in range(4):
                    target = slice((4 * other + z) * total + here, (4 * other + z) * total + here + size)
                    if first < half:
                        for ref, pick in ((send_one, 1 - b), (keep_one, b)):
                            ref[target] = keep[other, pick, z, rows] + got[other, pick, z, source]
                    else:
                        for ref, pick in ((send_two, 1 - a), (keep_two, a)):
                            ref[target] = keep[pick, other, z, rows] + got[pick, other, z, source]
        place += half
    if small:
        values = small[0][...] + small[1][...]
        small_out[0][...] = values
        carry(send_one, 8 * total, values)


def second_sum_kernel(me_ref, keep_one, got_one, keep_two, got_two, small, send_a, kept_a, send_b, kept_b, *small_out):
    a, b = me_ref[0], me_ref[1]
    rows = kept_a.shape[0]
    for keep, got, outs, mine in ((keep_one, got_one, (send_a, kept_a), a), (keep_two, got_two, (send_b, kept_b), b)):
        for ref, pick in zip(outs, (1 - mine, mine)):
            ref[:rows] = slab(keep, pick, rows)[...] + slab(got, pick, rows)[...]
    if small:
        values = small[0][...] + carried(got_one, 2 * rows)
        small_out[0][...] = values
        carry(send_a, rows, values)


def third_sum_kernel(me_ref, keep_one, got_one, keep_two, got_two, small, send, keep, *small_out):
    z = me_ref[3]
    half = keep_one.shape[0] // 4
    for high in range(2):
        for ref, pick in ((send, 1 - z), (keep, z)):
            first = 2 * high * half
            ref[first : first + half] = slab(keep_one, 2 * high + pick, half)[...] + slab(got_one, 2 * high + pick, half)[...]
            ref[first + half : first + 2 * half] = (
                slab(keep_two, 2 * high + pick, half)[...] + slab(got_two, 2 * high + pick, half)[...]
            )
    if small:
        values = small[0][...] + carried(got_one, 4 * half)
        small_out[0][...] = values
        carry(send, 4 * half, values)


def fourth_sum_kernel(me_ref, keep, got, small, send, kept, *small_out):
    z = me_ref[2]
    rows = kept.shape[0]
    for ref, pick in ((send, 1 - z), (kept, z)):
        ref[:rows] = slab(keep, pick, rows)[...] + slab(got, pick, rows)[...]
    if small:
        values = small[0][...] + carried(got, 2 * rows)
        small_out[0][...] = values
        carry(send, rows, values)


def scatter_cube(order, me, name, groups, small, results):
    got = [tuple(swapped(part, CORE_BIT) for part in pair[1:]) for pair, _ in groups]
    small = () if small is None else (small, swapped(small, CORE_BIT))
    extra = CARRIED if small else 0
    yield
    keeps = tuple(pair[0].reshape(2, 2, 4, -1, D) for pair, _ in groups)
    got = tuple(tuple(part.reshape(2, 2, 4, -1, D) for part in parts) for parts in got)
    half = sum(rows_of(shapes) for _, shapes in groups) // 2

    def call(kernel, number, rows, *args):
        outs = [(in_vmem(), (count, D), BF) for count in rows] + [(in_vmem(), (16, D), F32)] * bool(small)
        ins = jax.tree.map(lambda _: in_vmem(), list(args) + [small])
        parts = order.call(kernel, f"{name}_sum_{number}", 1, [scalars()] + ins, outs, [], (me, *args, small), 20, 1)
        return parts[: len(rows)], tuple(parts[len(rows) :])

    (send_one, keep_one, send_two, keep_two), small = call(
        first_sum_kernel, 1, (8 * half + extra, 8 * half, 8 * half, 8 * half), keeps, got
    )
    got = swapped(send_one, B_BIT), swapped(send_two, A_BIT)
    yield
    (send_one, keep_one, send_two, keep_two), small = call(
        second_sum_kernel, 2, (4 * half + extra, 4 * half, 4 * half, 4 * half), keep_one, got[0], keep_two, got[1]
    )
    got = swapped(send_one, A_BIT), swapped(send_two, B_BIT)
    yield
    (send, keep), small = call(
        third_sum_kernel, 3, (4 * half + extra, 4 * half), keep_one, got[0], keep_two, got[1]
    )
    got = swapped(send, LOW_BIT)
    yield
    (send, keep), small = call(fourth_sum_kernel, 4, (2 * half + extra, 2 * half), keep, got)
    last = (keep, swapped(send, HIGH_BIT))
    yield
    plan, outs, place = [], [], 0
    for _, shapes in groups:
        count, first = rows_of(shapes), 0
        for rows, columns in shapes:
            rows, blocks = rows // SHARDS, columns // D
            places = []
            for block in range(blocks):
                at = first + block * rows
                places.append(place + at if at < count // 2 else half + place + at - count // 2)
            first += rows * blocks
            plan.append((rows, blocks, tuple(places)))
            shape = (rows * blocks * 4, 128)
            outs.append((whole_block(*shape), shape, F32))
        place += count // 2
    flat, *sums = order.call(
        functools.partial(finish_kernel, plan=plan),
        name + "_finish",
        1,
        [scalars(), tuple(in_vmem() for _ in last), tuple(in_vmem() for _ in small)],
        [tuple(outs)] + [(in_vmem(), (16, D), F32)] * bool(small),
        [],
        (me, last, small),
        20,
        1,
    )
    results.extend(part.reshape(-1) for part in flat)
    results.extend(sums)
    yield


def finish_kernel(me_ref, parts, small, outs, *small_out, plan):
    for out, (rows, blocks, places) in zip(outs, plan):
        for block, place in enumerate(places):
            part = functools.reduce(jnp.add, [ref[place : place + rows, :].astype(F32) for ref in parts])
            for chunk in range(4):
                out[pl.ds(4 * block + chunk, rows, stride=4 * blocks), :] = part[:, 128 * chunk : 128 * chunk + 128]
    if small:
        small_out[0][...] = small[0][...] + carried(parts[1], parts[0].shape[0])


def unpack_group(rows, shapes):
    results, first = [], 0
    for shape in shapes:
        count = rows_of((shape,))
        results.append(unpacked(rows[first : first + count], *shape, SHARDS))
        first += count
    return results


def scatter_plain(grads, shapes, devices):
    if devices == SHARDS:
        own = lax.psum_scatter(grads.reshape(-1, D), AXES, scatter_dimension=0, tiled=True)
        return unpack_group(own.astype(F32), shapes)
    grads = grads.reshape(SHARDS, -1, D)
    results, first = [], 0
    for rows, columns in shapes:
        count = rows_of(((rows, columns),))
        part = grads[:, first : first + count].reshape(SHARDS, columns // D, rows // SHARDS, D)
        flat = jnp.swapaxes(part, 1, 2).reshape(devices, -1)
        results.append(lax.psum_scatter(flat, AXES, scatter_dimension=0, tiled=True).reshape(-1).astype(F32))
        first += count
    return results


class Exchange:
    def __init__(self, steps=None):
        self.results = []
        self.steps = None if steps is None else steps(self.results)

    def part(self, number):
        return self.results[number]

    def go(self, count=1):
        if self.steps is not None:
            for _ in range(count):
                next(self.steps)


def count_kernel(kind_ref, lengths_ref, ids_ref, out_ref, *, slots):
    totals = [jnp.zeros((1, 128), F32) for _ in range(8)]
    place = lax.broadcasted_iota(jnp.int32, (SLOT, 128), 0)
    lane = lax.broadcasted_iota(jnp.int32, (SLOT, 128), 1).astype(F32)
    for slot in range(slots):
        kind = kind_ref[slot]
        sequence = lax.shift_right_logical(place, kind + 7)
        within = place & (lax.shift_left(jnp.int32(128), kind) - 1)
        limit = jnp.zeros_like(place)
        for entry in range(4):
            limit = jnp.where(sequence == entry, lengths_ref[slot, entry], limit)
        ids = jnp.broadcast_to(ids_ref[slot : slot + 1].astype(F32), (128, SLOT)).T
        ids = jnp.where(within < limit, ids, -1.0)
        for chunk in range((VOCAB + 127) // 128):
            hits = jnp.where(ids == lane + 128.0 * chunk, 1.0, 0.0)
            totals[chunk] = totals[chunk] + jnp.sum(hits, 0, keepdims=True)
    out_ref[...] = jnp.concatenate([jnp.concatenate(totals[:4], 1), jnp.concatenate(totals[4:], 1)], 0)


def count_live(order, kinds, lengths, ids):
    slots = ids.shape[0]
    return order.call(
        functools.partial(count_kernel, slots=slots),
        "count",
        1,
        [scalars(), scalars(), in_vmem()],
        [(in_vmem(), (2, D), F32)],
        [],
        (kinds, lengths, ids),
        8,
        1,
    )[0]


def local(
    sizes,
    enc_in,
    dec_in,
    bucket,
    enc_lengths,
    dec_lengths,
    pred_ids,
    running_counts,
    enc_attn_in,
    enc_attn_out,
    enc_ff_in,
    enc_ff_out,
    enc_norms,
    dec_self_in,
    dec_self_out,
    dec_cross_q,
    dec_cross_kv,
    dec_cross_out,
    dec_ff_in,
    dec_ff_out,
    dec_norms,
    enc_cotangent,
    dec_cotangent,
):
    devices = math.prod(sizes)
    cube = sizes == CUBE
    index = lax.axis_index("dp") * lax.axis_size("fsdp") + lax.axis_index("fsdp")
    if cube:
        me = jnp.stack([index >> 4 & 1, index >> 3 & 1, index >> 2 & 1, index >> 1 & 1, index & 1]).astype(jnp.int32)
    else:
        me = jnp.zeros((5,), jnp.int32)

    order = Order()

    def gather(name, groups, spans, extra=None):
        if cube:
            return Exchange(lambda results: gather_cube(order, me, name, groups, spans, extra, results))
        exchange = Exchange()
        gather_plain(groups, spans, extra, devices, exchange.results)
        return exchange

    def scatter(name, *groups, small=None):
        if cube:
            return Exchange(lambda results: scatter_cube(order, me, name, groups, small, results))
        exchange = Exchange()
        for (grads,), shapes in groups:
            exchange.results.extend(scatter_plain(grads, shapes, devices))
        if small is not None:
            exchange.results.append(sum_everywhere(small, sizes))
        return exchange

    enc_count, dec_count = enc_norms.shape[0], dec_norms.shape[0]
    both = jnp.concatenate([enc_norms, dec_norms])
    norm_part = jnp.pad(both[None, :], ((0, 0), (0, D - both.shape[0])))
    enc_self_group = list(zip((enc_attn_in, enc_attn_out), SELF_SHAPES))
    dec_self_group = list(zip((dec_self_in, dec_self_out), SELF_SHAPES))
    enc_ff_group = list(zip((enc_ff_in, enc_ff_out), FFN_SHAPES))
    cross_group = list(zip((dec_cross_q, dec_cross_kv, dec_cross_out), CROSS_SHAPES))
    dec_ff_group = list(zip((dec_ff_in, dec_ff_out), FFN_SHAPES))
    first = gather("self", [dec_self_group, enc_self_group], [2], norm_part)
    ffn = gather("ffn", [enc_ff_group], [1])
    late = gather("late", [cross_group, dec_ff_group], [2])
    first.go(2)
    ffn.go()
    late.go()
    counted = count_live(order, bucket, dec_lengths, pred_ids)
    first.go(2)
    self_chain = first.part(0)
    self_chain.go()
    ffn.go(2)
    self_chain.go()
    late.go()
    ffn.go()
    ffn_chain = ffn.part(0)
    self_chain.go()
    ffn_chain.go()
    dec_self_w, enc_self_w, norm_lines = self_chain.results
    enc_norm = norm_lines[:, :enc_count].reshape(4, D).astype(F32)
    dec_norm = norm_lines[:, enc_count : enc_count + dec_count].reshape(6, D).astype(F32)

    enc_qkv, dec_qkv = project(order, me, (enc_in, dec_in), (enc_self_w, dec_self_w), (enc_norm, dec_norm))
    late.go()
    ffn_chain.go()
    attended, *enc_kept = self_attend(order, bucket, enc_lengths, me, enc_in, enc_qkv, enc_self_w, False, "enc_attend")
    late.go()
    late_chain = late.part(0)
    late_chain.go()
    ffn_chain.go()
    first_out, *dec_kept = self_attend(order, bucket, dec_lengths, me, dec_in, dec_qkv, dec_self_w, True, "dec_attend")
    late_chain.go()
    (enc_ff_w,) = ffn_chain.results
    memory, active, slope = ffn_forward(order, me, attended, enc_ff_w, enc_norm)
    late_chain.go()
    cross_w, dec_ff_w = late_chain.results
    decoded, grad_first, grad_memory, dec_ff_grads, cross_grads, upper_norm_g = upper(
        order,
        bucket,
        enc_lengths,
        me,
        first_out,
        memory,
        enc_cotangent,
        dec_cotangent,
        cross_w,
        dec_ff_w,
        dec_norm,
        cube,
    )
    fifth = scatter("dec", (dec_ff_grads, FFN_SHAPES), (cross_grads, CROSS_SHAPES))
    fifth.go()
    grad_attended, enc_ff_grads, enc_ffn_norm_g = ffn_backward(
        order, me, grad_memory, attended, active, slope, enc_ff_w, enc_norm, cube
    )
    fifth.go()
    enc_proj = attend_backward(
        order,
        bucket,
        enc_lengths,
        me,
        grad_attended,
        enc_qkv,
        enc_qkv,
        enc_kept,
        enc_self_w,
        False,
        SELF_OUT,
        D,
        "enc_attend_back",
    )
    fifth.go()
    enc_self_grads = self_weights(
        order, me, grad_attended, enc_in, enc_kept[0], enc_proj, enc_norm, cube, "enc_self_weights"
    )
    sixth = scatter("enc", (enc_ff_grads, FFN_SHAPES), (enc_self_grads, SELF_SHAPES))
    sixth.go()
    dec_proj = attend_backward(
        order,
        bucket,
        dec_lengths,
        me,
        grad_first,
        dec_qkv,
        dec_qkv,
        dec_kept,
        dec_self_w,
        True,
        SELF_OUT,
        D,
        "dec_attend_back",
    )
    fifth.go()
    sixth.go()
    grad_enc_in, enc_self_norm_g = self_rows(
        order, me, grad_attended, enc_in, enc_proj, enc_self_w, enc_norm, "enc_self_rows"
    )
    fifth.go()
    grad_dec_in, dec_self_norm_g = self_rows(order, me, grad_first, dec_in, dec_proj, dec_self_w, dec_norm, "dec_self_rows")
    sixth.go()
    small = jnp.concatenate(
        [enc_self_norm_g[:2], enc_ffn_norm_g[:2], dec_self_norm_g[:2], upper_norm_g[:4], counted, jnp.zeros((4, D), F32)],
        0,
    )
    dec_self_grads = self_weights(
        order, me, grad_first, dec_in, dec_kept[0], dec_proj, dec_norm, cube, "dec_self_weights"
    )
    seventh = scatter("self", (dec_self_grads, SELF_SHAPES), small=small)
    seventh.go()
    fifth.go()
    sixth.go()
    seventh.go()
    sixth.go()
    seventh.go()
    seventh.go()
    sixth.go()
    seventh.go()
    seventh.go()
    dec_ff_in_g, dec_ff_out_g, cross_q_g, cross_kv_g, cross_out_g = fifth.results
    enc_ff_in_g, enc_ff_out_g, enc_attn_in_g, enc_attn_out_g = sixth.results
    dec_self_in_g, dec_self_out_g, small = seventh.results

    enc_norm_own = lax.dynamic_slice(small[:4].reshape(-1), (index * enc_count,), (enc_count,))
    dec_norm_own = lax.dynamic_slice(small[4:10].reshape(-1), (index * dec_count,), (dec_count,))
    counts = running_counts + small[10:12].reshape(-1)[:VOCAB].astype(jnp.int32)
    return (
        memory,
        decoded,
        grad_enc_in,
        grad_dec_in,
        enc_attn_in_g,
        enc_attn_out_g,
        enc_ff_in_g,
        enc_ff_out_g,
        enc_norm_own,
        dec_self_in_g,
        dec_self_out_g,
        cross_q_g,
        cross_kv_g,
        cross_out_g,
        dec_ff_in_g,
        dec_ff_out_g,
        dec_norm_own,
        counts,
    )


def solution(mesh):
    rows = P(AXES, None, None)
    pair = P(AXES, None)
    flat = P(AXES)
    return jax.shard_map(
        functools.partial(local, axis_sizes(mesh)),
        mesh=mesh,
        in_specs=(rows, rows, flat, pair, pair, pair, P()) + (flat,) * 13 + (rows, rows),
        out_specs=(rows,) * 4 + (flat,) * 13 + (P(),),
        check_vma=False,
    )
```
